32 devices in a mesh: lon: 4 (over z), lat: 8 (over y, x, core).
Axes of the slice: x: 2, y: 2, z: 4, core: 2. Of those that a mesh axis runs over, the one named last changes fastest.
Arguments:
- free_elevation: float32 [128, 1024], P('lat', 'lon'), may hold values from -3 to 3
- zonal_volume_carriage: float32 [128, 1024], P('lat', 'lon'), may hold values from -2 to 2
- meridional_volume_carriage: float32 [128, 1024], P('lat', 'lon'), may hold values from -2 to 2
- thermal_field: float32 [60, 128, 1024], P(None, 'lat', 'lon'), may hold values from -6 to 6
- flooded_strata_number: int32 [128, 1024], P('lat', 'lon'), may hold values from 0 to 60, as said below
- aerial_exchanges: float32 [5, 64, 512], P(None, 'lat', 'lon'), may hold values from -6 to 6
- aerial_terrain_flags: int32 [64, 512], P('lat', 'lon'), may hold values 0 or 1
- donor_tile_number: int32 [4, 128, 8], P(None, 'lat', 'lon'), may hold values from 0 to 23
- donor_point_number: int32 [4, 128, 1024], P(None, 'lat', 'lon'), may hold values from 0 to 127
- pairing_coefficients: float32 [4, 128, 1024], P(None, 'lat', 'lon'), may hold values from 0 to 0.5
Outputs:
- advanced_elevation: float32 [128, 1024], P('lat', 'lon')
- transport_x_next: float32 [128, 1024], P('lat', 'lon')
- transport_y_next: float32 [128, 1024], P('lat', 'lon')
- advanced_thermal_field: float32 [60, 128, 1024], P(None, 'lat', 'lon')
- marine_skin_condition: float32 [4, 64, 512], P(None, 'lat', 'lon')
The draws below stay inside these ranges and needn't reach their ends.
Inputs may be any that keep to these rules, and one draw needn't show every extreme that they name: flooded_strata_number is 0 on land; wet columns hold 1 to 60 levels. donor_tile_number // 8 - 1 is the source tile's offset in latitude and donor_tile_number mod 8 the source block (row) within it; the longitude tile is the target's.
All inputs are finite; a program needn't handle non-finite values. No bound on the sum of `aerial_terrain_flags` on one device may be relied on, other than what follows from the above.
Results may differ from the reference program's by a relative error of at most 0.0003.
Values sent between devices are 32-bit elements; how exact they have to be, the bound alone decides.
No kernel may reach another device: no remote copies, remote signals or barrier semaphores. Data moves between devices by JAX's collectives and lax.ppermute only.
A program may use at most 64 MiB of HBM per device.

```python
import math
import jax
import jax.numpy as jnp
from jax import lax

ALAT = 8
ALON = 128
MARINE_STRATA = 60
SUBS = 3
INTERSECTIONS = 4
NFLUX = 5
NSURF = 4
OLAT = 16
OLON = 256
ALAT_ALL = 64
ALON_ALL = 512
MARINE_LATITUDES = 128
MARINE_LONGITUDES = 1024
N_LON = 4


def draw_flooded_strata_number(key, part):
    depth_key = jax.random.fold_in(key, 11)
    land_key = jax.random.fold_in(key, 23)
    grid_shape = (MARINE_LATITUDES, MARINE_LONGITUDES)
    levels_drawn = jax.random.randint(depth_key, grid_shape, 1, MARINE_STRATA + 1)
    row_ids = lax.broadcasted_iota(jnp.int32, grid_shape, 0)
    column_ids = lax.broadcasted_iota(jnp.int32, grid_shape, 1)
    land_share = (row_ids // 4 * 3 + column_ids // 16 * 5) % 8
    rolled = jax.random.randint(land_key, grid_shape, 0, 10)
    return jnp.where(rolled < land_share, 0, levels_drawn).astype(jnp.int32)


def place_ends(entries, rng, smallest, high):
    index_at = [jax.random.randint(jax.random.fold_in(rng, axis), (), 0, length) for axis, length in enumerate(entries.shape)]
    widest = entries.shape.index(max(entries.shape))
    beside = index_at[:widest] + [(index_at[widest] + 1) % entries.shape[widest]] + index_at[widest + 1:]
    return entries.at[tuple(index_at)].set(smallest).at[tuple(beside)].set(high)


def block_levels(own_key, shape, split, least, top_value):
    gain = 1.0
    for dim, parts in split:
        draws = jax.random.uniform(jax.random.fold_in(jax.random.fold_in(own_key, 6), dim), (parts,), jnp.float32, least / len(split), top_value / len(split))
        gain = gain * jnp.repeat(jnp.exp(draws), shape[dim] // parts).reshape((-1,) + (1,) * (len(shape) - 1 - dim))
    return gain


def gaussian(key, shape, scale, bound, cuts=(), kind=jnp.bfloat16):
    result = scale * jax.random.normal(key, shape, jnp.float32)
    if cuts:
        result = result * block_levels(key, shape, cuts, -0.22, 0.18)
    return jnp.clip(result, -bound, bound).astype(kind)


def setup_inputs(seed: int = 0) -> dict:
    keys = jax.random.split(jax.random.key(seed), 11)
    return {
        "free_elevation": gaussian(keys[0], (MARINE_LATITUDES, MARINE_LONGITUDES), 0.5, 3.0, ((0, 8), (1, 4)), jnp.float32),
        "zonal_volume_carriage": gaussian(keys[1], (MARINE_LATITUDES, MARINE_LONGITUDES), 0.3, 2.0, ((0, 8), (1, 4)), jnp.float32),
        "meridional_volume_carriage": gaussian(keys[2], (MARINE_LATITUDES, MARINE_LONGITUDES), 0.3, 2.0, ((0, 8), (1, 4)), jnp.float32),
        "thermal_field": gaussian(keys[3], (MARINE_STRATA, MARINE_LATITUDES, MARINE_LONGITUDES), 1.0, 6.0, ((1, 8), (2, 4)), jnp.float32),
        "flooded_strata_number": draw_flooded_strata_number(jax.random.fold_in(keys[10], 71), 0),
        "aerial_exchanges": gaussian(keys[5], (NFLUX, ALAT_ALL, ALON_ALL), 1.0, 6.0, ((1, 8), (2, 4)), jnp.float32),
        "aerial_terrain_flags": place_ends((jax.random.randint(keys[6], (ALAT_ALL, ALON_ALL), 0, 10) < 3).astype(jnp.int32), jax.random.fold_in(keys[6], 1), 0, 1),
        "donor_tile_number": place_ends(jax.random.randint(keys[7], (INTERSECTIONS, MARINE_LATITUDES, 2 * N_LON), 0, 3 * ALAT), jax.random.fold_in(keys[7], 1), 0, (3 * ALAT) - 1).astype(jnp.int32),
        "donor_point_number": place_ends(jax.random.randint(keys[8], (INTERSECTIONS, MARINE_LATITUDES, MARINE_LONGITUDES), 0, ALON), jax.random.fold_in(keys[8], 1), 0, ALON - 1).astype(jnp.int32),
        "pairing_coefficients": jnp.clip(0.5 * jax.random.uniform(keys[9], (INTERSECTIONS, MARINE_LATITUDES, MARINE_LONGITUDES), jnp.float32) ** block_levels(keys[9], (INTERSECTIONS, MARINE_LATITUDES, MARINE_LONGITUDES), ((1, 8), (2, 4)), -0.2, 0.2), 0.0, 0.5),
    }


grav_step = 0.6
height_step = 0.6
wind_step = 0.5
fresh_step = 0.5
mixing_fourth = 0.02
advect_coef = 0.1
diapycnal_diffusion = 0.2
heat_gain = 0.3
light_gain = 0.3
light_decay = 8.0
depth_floor = 0.25
area_floor = 1.0


def column_depth(stratum_tally_sheet, stratum_entries):
    def add_level(level_index, running):
        level_value = jnp.asarray(level_index).astype(jnp.float32)
        thickness = (1.0 + 2.0 * level_value / stratum_entries) / (2.0 * stratum_entries)
        return running + jnp.where(level_value < stratum_tally_sheet, thickness, 0.0)
    return lax.fori_loop(0, stratum_entries, add_level, jnp.zeros_like(stratum_tally_sheet))


def barotropic_step(planes, stratum_entries):
    height = planes[0]
    zonal_velocity = planes[1]
    meridional_velocity = planes[2]
    stratum_tally_sheet = planes[3]
    wind_east = planes[4]
    wind_north = planes[5]
    fresh_water = planes[6]
    stratum_thicknesses = column_depth(stratum_tally_sheet, stratum_entries)
    lone_flooded_point = (stratum_tally_sheet > 0.5).astype(jnp.float32)
    east_face = lone_flooded_point[1:-1, :-1] * lone_flooded_point[1:-1, 1:]
    east_depth = jnp.minimum(stratum_thicknesses[1:-1, :-1], stratum_thicknesses[1:-1, 1:])
    east_flow = east_face * (zonal_velocity[1:-1, :-1] - grav_step * east_depth * (height[1:-1, 1:] - height[1:-1, :-1]) + wind_step * wind_east[1:-1, :-1])
    north_face = lone_flooded_point[:-1, 1:-1] * lone_flooded_point[1:, 1:-1]
    north_depth = jnp.minimum(stratum_thicknesses[:-1, 1:-1], stratum_thicknesses[1:, 1:-1])
    north_flow = north_face * (meridional_velocity[:-1, 1:-1] - grav_step * north_depth * (height[1:, 1:-1] - height[:-1, 1:-1]) + wind_step * wind_north[:-1, 1:-1])
    spread = east_flow[:, 1:] - east_flow[:, :-1] + north_flow[1:, :] - north_flow[:-1, :]
    inner_wet = lone_flooded_point[1:-1, 1:-1]
    new_height = height[1:-1, 1:-1] + inner_wet * (fresh_step * fresh_water[1:-1, 1:-1] - height_step * spread)
    return jnp.stack([new_height, east_flow[:, 1:], north_flow[1:, :], stratum_tally_sheet[1:-1, 1:-1],
                      wind_east[1:-1, 1:-1], wind_north[1:-1, 1:-1], fresh_water[1:-1, 1:-1]])


def face_masks(count_border, level_order):
    east_open = (level_order < jnp.minimum(count_border[:, :-1], count_border[:, 1:])).astype(jnp.float32)
    north_open = (level_order < jnp.minimum(count_border[:-1, :], count_border[1:, :])).astype(jnp.float32)
    return east_open, north_open


def laplace(field, count_border, level_order):
    east_open, north_open = face_masks(count_border, level_order)
    flux_east = east_open * (field[..., 1:] - field[..., :-1])
    flux_north = north_open * (field[..., 1:, :] - field[..., :-1, :])
    return (flux_east[..., 1:-1, 1:] - flux_east[..., 1:-1, :-1]
            + flux_north[..., 1:, 1:-1] - flux_north[..., :-1, 1:-1])


def face_speeds(count_border, east_border, north_border, stratum_entries):
    stratum_thicknesses = column_depth(count_border, stratum_entries)
    speed_east = east_border[:, :-1] / jnp.maximum(jnp.minimum(stratum_thicknesses[:, :-1], stratum_thicknesses[:, 1:]), depth_floor)
    speed_north = north_border[:-1, :] / jnp.maximum(jnp.minimum(stratum_thicknesses[:-1, :], stratum_thicknesses[1:, :]), depth_floor)
    return speed_east, speed_north


def horizontal_tendency(temp_border, lap_border, count_border, speed_east, speed_north, level_order):
    mixing = laplace(lap_border, count_border, level_order)
    east_open, north_open = face_masks(count_border, level_order)
    carry_east = east_open * speed_east * 0.5 * (temp_border[..., 1:] + temp_border[..., :-1])
    carry_north = north_open * speed_north * 0.5 * (temp_border[..., 1:, :] + temp_border[..., :-1, :])
    advect = (carry_east[..., 1:-1, 1:] - carry_east[..., 1:-1, :-1]
              + carry_north[..., 1:, 1:-1] - carry_north[..., :-1, 1:-1])
    return -advect_coef * advect - mixing_fourth * mixing


def profile_change_rate(thermal_field, lateral_contribution, stratum_tally_sheet, boundary_thermal_exchange, solar_radiation, stratum_entries):
    level_order = jnp.arange(stratum_entries, dtype=jnp.float32)[:, None, None]
    flooded_point_flags = (level_order < stratum_tally_sheet).astype(jnp.float32)
    beneath_stratum_flooded = (level_order + 1.0 < stratum_tally_sheet).astype(jnp.float32)
    sinking_exchange = beneath_stratum_flooded[:-1] * (thermal_field[1:] - thermal_field[:-1])
    blank_sheet = jnp.zeros_like(thermal_field[:1])
    radial_contribution = jnp.concatenate([sinking_exchange, blank_sheet]) - jnp.concatenate([blank_sheet, sinking_exchange])
    absorb = jnp.exp(-level_order / light_decay) * (1.0 - math.exp(-1.0 / light_decay))
    top_level = (level_order < 0.5).astype(jnp.float32)
    donor_entries = light_gain * absorb * solar_radiation + heat_gain * boundary_thermal_exchange * top_level
    return thermal_field + flooded_point_flags * (diapycnal_diffusion * radial_contribution + lateral_contribution + donor_entries)


def gather_forcing(flux_table, flat_index, weight):
    running = jnp.zeros((flux_table.shape[0],) + flat_index.shape[1:], jnp.float32)
    for link_index in range(flat_index.shape[0]):
        running = running + jnp.take(flux_table, flat_index[link_index], axis=1) * weight[link_index][None]
    return running


def spread_back(uppermost_stratum, lone_flooded_point, flat_index, weight, segments):
    link_share = weight * lone_flooded_point[None]
    flat_cells = flat_index.reshape(-1)

    def scatter_plane(plane):
        return jax.ops.segment_sum((plane[None] * link_share).reshape(-1), flat_cells, num_segments=segments)

    link_sums = jnp.stack([scatter_plane(uppermost_stratum[plane_index]) for plane_index in range(uppermost_stratum.shape[0])])
    link_area = jax.ops.segment_sum(link_share.reshape(-1), flat_cells, num_segments=segments)
    return link_sums, link_area


def haloed_sphere(field, width):
    wrapped = jnp.concatenate([field[..., -width:], field, field[..., :width]], axis=-1)
    widths = [(0, 0)] * (field.ndim - 2) + [(width, width), (0, 0)]
    return jnp.pad(wrapped, widths)


def reference(free_elevation, zonal_volume_carriage, meridional_volume_carriage, thermal_field, flooded_strata_number, aerial_exchanges, aerial_terrain_flags,
              donor_tile_number, donor_point_number, pairing_coefficients):
    open_sea = (1 - aerial_terrain_flags).astype(jnp.float32)
    masked = aerial_exchanges * open_sea[None]
    padded = jnp.pad(masked, ((0, 0), (ALAT, ALAT), (0, 0)))
    flux_table = padded.reshape(NFLUX, -1)
    row_ids = lax.broadcasted_iota(jnp.int32, (MARINE_LATITUDES, MARINE_LONGITUDES), 0)
    column_ids = lax.broadcasted_iota(jnp.int32, (MARINE_LATITUDES, MARINE_LONGITUDES), 1)
    block_row = jnp.repeat(donor_tile_number, ALON, axis=2)
    global_row = (row_ids // OLAT) * ALAT + block_row
    global_column = (column_ids // OLON) * ALON + donor_point_number
    flat_index = (global_row * ALON_ALL + global_column).astype(jnp.int32)
    boundary_driving = gather_forcing(flux_table, flat_index, pairing_coefficients)

    stratum_tally_sheet = flooded_strata_number.astype(jnp.float32)
    present_scalar_field = jnp.stack([free_elevation, zonal_volume_carriage, meridional_volume_carriage, stratum_tally_sheet, boundary_driving[0], boundary_driving[1], boundary_driving[4]])
    for cycle_index in range(SUBS):
        present_scalar_field = barotropic_step(haloed_sphere(present_scalar_field, 1), MARINE_STRATA)
    advanced_elevation = present_scalar_field[0]
    zonal_velocity = present_scalar_field[1]
    meridional_velocity = present_scalar_field[2]

    thermal_field_haloed = haloed_sphere(thermal_field, 2)
    count_wide = haloed_sphere(stratum_tally_sheet, 2)
    count_border = count_wide[1:-1, 1:-1]
    flows = haloed_sphere(present_scalar_field[1:3], 1)
    speed_east, speed_north = face_speeds(count_border, flows[0], flows[1], MARINE_STRATA)

    def by_stratum(level_args):
        temp_level, level_order = level_args
        lap_border = laplace(temp_level, count_wide, level_order)
        return horizontal_tendency(temp_level[1:-1, 1:-1], lap_border, count_border, speed_east, speed_north, level_order)

    lateral_contribution = lax.map(by_stratum, (thermal_field_haloed, jnp.arange(MARINE_STRATA, dtype=jnp.float32)))
    advanced_thermal_field = profile_change_rate(thermal_field, lateral_contribution, stratum_tally_sheet, boundary_driving[2], boundary_driving[3], MARINE_STRATA)

    lone_flooded_point = (stratum_tally_sheet > 0.5).astype(jnp.float32)
    stratum_thicknesses = jnp.maximum(column_depth(stratum_tally_sheet, MARINE_STRATA), depth_floor)
    uppermost_stratum = jnp.stack([advanced_thermal_field[0], advanced_elevation, zonal_velocity / stratum_thicknesses, meridional_velocity / stratum_thicknesses]) * lone_flooded_point[None]
    segments = (ALAT_ALL + 2 * ALAT) * ALON_ALL
    link_sums, link_area = spread_back(uppermost_stratum, lone_flooded_point, flat_index, pairing_coefficients, segments)
    link_sums = link_sums.reshape(NSURF, ALAT_ALL + 2 * ALAT, ALON_ALL)[:, ALAT:ALAT + ALAT_ALL]
    link_area = link_area.reshape(ALAT_ALL + 2 * ALAT, ALON_ALL)[ALAT:ALAT + ALAT_ALL]
    marine_skin_condition = open_sea[None] * link_sums / jnp.maximum(link_area, area_floor)[None]
    return advanced_elevation, zonal_velocity, meridional_velocity, advanced_thermal_field, marine_skin_condition
```

```python
import functools
import math

import jax
import jax.numpy as jnp
from jax import lax
from jax.experimental import pallas as pl
from jax.experimental.pallas import tpu as pltpu
from jax.sharding import PartitionSpec as P

SUBS = 3

grav_step = 0.6
height_step = 0.6
wind_step = 0.5
fresh_step = 0.5
mixing_fourth = 0.02
advect_coef = 0.1
diapycnal_diffusion = 0.2
heat_gain = 0.3
light_gain = 0.3
light_decay = 8.0
depth_floor = 0.25
area_floor = 1.0

TILE = 8
LANES = 128
HALF = TILE // 2

f32 = jnp.float32
i32 = jnp.int32


def swap_pairs(count, first, periodic):
    pairs = []
    for low in range(first, count, 2):
        high = low + 1
        if high == count:
            if not periodic:
                continue
            high = 0
        pairs += [(low, high), (high, low)]
    return pairs


def swap(array, axis, first, periodic):
    return lax.ppermute(array, axis, swap_pairs(lax.axis_size(axis), first, periodic))


def lane_ids(rows, width=LANES):
    return lax.broadcasted_iota(i32, (rows, width), 1)


def row_ids(rows, width=LANES):
    return lax.broadcasted_iota(i32, (rows, width), 0)


def roll_rows(array, by):
    by = by % array.shape[0]
    return pltpu.roll(array, by, 0) if by else array


def roll_lanes(array, by):
    by = by % array.shape[1]
    return pltpu.roll(array, by, 1) if by else array


def call(body, outs, ins, name, flops, aliases=None, scratch=(), hbm=()):
    specs = [
        pl.BlockSpec(memory_space=pltpu.HBM if place in hbm else pltpu.VMEM)
        for place in range(len(ins))
    ]
    ins = [
        pltpu.with_memory_space_constraint(leaf, pltpu.HBM) if place in hbm else leaf
        for place, leaf in enumerate(ins)
    ]
    moved = 4 * sum(math.prod(leaf.shape) for leaf in list(ins) + list(outs))
    return pl.pallas_call(
        body,
        out_shape=outs,
        in_specs=specs,
        out_specs=[pl.BlockSpec(memory_space=pltpu.VMEM)] * len(outs),
        scratch_shapes=list(scratch),
        input_output_aliases=aliases or {},
        compiler_params=pltpu.CompilerParams(vmem_limit_bytes=24 * 1024 * 1024),
        cost_estimate=pl.CostEstimate(flops=flops, bytes_accessed=moved, transcendentals=0),
        name=name,
    )(*ins)


def shape(*dims, dtype=f32):
    return jax.ShapeDtypeStruct(dims, dtype)


def write_edge(top, fields, tiles, masked, out_ref):
    sub = row_ids(TILE, out_ref.shape[2])
    mine = (sub >= HALF) == top
    for place in range(len(fields) // 2):
        first = jnp.where(top, fields[2 * place][TILE:], fields[2 * place][:TILE])
        second = jnp.where(top, fields[2 * place + 1][TILE:], fields[2 * place + 1][:TILE])
        out_ref[place] = jnp.where(mine, first, roll_rows(second, HALF))
    at = len(fields) // 2
    numbers = jnp.where(top, tiles[TILE:], tiles[:TILE])
    planes = [numbers] + masked
    for place in range(len(planes) // 2):
        out_ref[at + place] = jnp.concatenate(planes[2 * place : 2 * place + 2], axis=1)


def write_temp_edge(top, temp_ref, out_ref, at):
    levels, _, width = temp_ref.shape
    sub = row_ids(TILE, width)
    for group in range(pl.cdiv(levels, 4)):
        packed = jnp.zeros((TILE, width), f32)
        for spot in range(min(4, levels - 4 * group)):
            level = 4 * group + spot
            low = roll_rows(temp_ref[level, :TILE, :], 2 * spot)
            high = roll_rows(temp_ref[level, TILE:, :], 2 * spot + 2)
            packed = jnp.where(sub // 2 == spot, jnp.where(top, high, low), packed)
        out_ref[at + group] = packed


def goes_north(first):
    return (lax.rem(lax.axis_index("lat"), 2) == 0) == (first == 0)


def edge_fields(state, points, weights):
    links = points.shape[0]
    fields = [state[place] for place in range(4)]
    fields += [points[k].astype(f32) for k in range(links)]
    fields += [weights[k] for k in range(links)]
    return fields


def load_body(
    height,
    zonal,
    merid,
    counts,
    points,
    tile,
    weights,
    flux,
    flags,
    temp,
    edge,
    own,
    state_out,
    points_out,
    weights_out,
    flags_out,
    temp_out,
    counts_in,
    tile_in,
    flux_in,
    sems,
):
    pairs = [
        (flux, flux_in),
        (flags, flags_out),
        (tile, tile_in),
        (counts, counts_in),
        (height, state_out.at[0]),
        (zonal, state_out.at[1]),
        (merid, state_out.at[2]),
        (points, points_out),
        (weights, weights_out),
        (temp, temp_out),
    ]
    copies = [
        pltpu.make_async_copy(source, target, sems.at[place])
        for place, (source, target) in enumerate(pairs)
    ]
    for copy in copies:
        copy.start()
    for copy in copies[:-1]:
        copy.wait()
    state_out[3] = counts_in[...].astype(f32)
    links, blocks, rows = tile.shape
    open_sea = (1 - flags_out[...]).astype(f32)
    masked = [flux_in[plane] * open_sea for plane in range(flux.shape[0])]
    lane = lane_ids(rows)
    diagonal = row_ids(rows, rows) == lane_ids(rows, rows)
    tiles = jnp.zeros((rows, LANES), f32)
    for k in range(links):
        for b in range(blocks):
            line = jnp.broadcast_to(tile_in[k, b : b + 1, :].astype(f32), (rows, rows))
            upright = jnp.sum(jnp.where(diagonal, line, 0.0), axis=1, keepdims=True)
            tiles = jnp.where(lane == k * blocks + b, upright, tiles)
    for plane, values in enumerate(masked):
        own[plane] = values
    own[len(masked)] = tiles[:TILE]
    own[len(masked) + 1] = tiles[TILE:]
    top = goes_north(0)
    fields = edge_fields(state_out, points_out, weights_out)
    write_edge(top, fields, tiles, masked, edge)
    copies[-1].wait()
    write_temp_edge(top, temp_out, edge, len(fields) // 2 + (len(masked) + 1) // 2)


def pack_second_body(own, state, points, weights, temp, draft, temp_edge, edges):
    top = goes_north(1)
    nflux = own.shape[0] - 2
    tiles = jnp.concatenate([own[nflux], own[nflux + 1]], axis=0)
    masked = [own[plane] for plane in range(nflux)]
    write_edge(top, edge_fields(state, points, weights), tiles, masked, draft)
    write_temp_edge(top, temp, temp_edge, 0)
    rows = temp.shape[1]
    for place, columns in enumerate(
        edge_columns([temp[level] for level in range(temp.shape[0])], rows)
    ):
        edges[place] = columns


def edge_columns(fields, rows):
    lane = lane_ids(rows)
    high = jnp.zeros((rows, LANES), f32)
    low = jnp.zeros((rows, LANES), f32)
    for level, field in enumerate(fields):
        ends = jnp.where(lane < HALF, field[:, :LANES], field[:, -LANES:])
        turned = roll_lanes(ends, 2 * level + 2)
        high = jnp.where(lane // 2 == level, turned, high)
        low = jnp.where(lane // 2 == (level + 1) % (LANES // 2), turned, low)
    return roll_lanes(low, -2), high


HALO_FLUXES = (0, 1, 4)


def pack_flux_body(flux_at, draft, received, out):
    last = out.shape[0] - 2
    planes = []
    for plane in HALO_FLUXES:
        spot = flux_at * 2 + 1 + plane
        planes.append(received[spot // 2, :, (spot % 2) * LANES : (spot % 2 + 1) * LANES])
    out[last] = jnp.concatenate(planes[:2], axis=1)
    out[last + 1] = jnp.concatenate([planes[2], planes[2]], axis=1)


def pack_third_body(flux_at, received, out):
    for place, plane in enumerate(HALO_FLUXES):
        spot = flux_at * 2 + 1 + plane
        out[place] = received[spot // 2, :, (spot % 2) * LANES : (spot % 2 + 1) * LANES]


def unpack_temp_body(temp_at, got_a, got_b, halo, edges):
    even = lax.rem(lax.axis_index("lat"), 2) == 0
    levels, _, width = halo.shape
    sub = row_ids(TILE, width)
    fields = []
    for group in range(pl.cdiv(levels, 4)):
        one, two = got_a[temp_at + group], got_b[group]
        north = jnp.where(even, one, two)
        south = jnp.where(even, two, one)
        for spot in range(min(4, levels - 4 * group)):
            level = 4 * group + spot
            rows = jnp.where(
                sub < HALF, roll_rows(north, -2 * spot), roll_rows(south, 6 - 2 * spot)
            )
            halo[level] = rows
            fields.append(rows)
    for place, columns in enumerate(edge_columns(fields, TILE)):
        edges[place] = columns


def pick(array, rows):
    return jnp.take_along_axis(array, rows, axis=0, mode="promise_in_bounds")


def pick_lane(array, lanes):
    return jnp.take_along_axis(array, lanes, axis=1, mode="promise_in_bounds")


def spot_of(array, flux_at, place):
    return array[flux_at + place // 2, :, (place % 2) * LANES : (place % 2 + 1) * LANES]


def by_side(even, one, two):
    return jnp.where(even, one, two), jnp.where(even, two, one)


def row_numbers(numbers, column):
    number = jnp.broadcast_to(numbers[:, column : column + 1].astype(i32), (TILE, LANES))
    return number & (TILE - 1), lax.shift_right_logical(number, 3)


FORCING_AT = {0: 4, 1: 5, 4: 6}


def forcing_body(flux_at, got_a, got_b, own, state, points, weights, ext, light):
    even = lax.rem(lax.axis_index("lat"), 2) == 0
    links, rows, width = points.shape
    blocks = width // LANES
    nflux = own.shape[0] - 2
    ext[:4, :rows, :] = state[...]
    north, south = [], []
    for plane in range(nflux):
        one, two = spot_of(got_a, flux_at, 1 + plane), spot_of(got_b, flux_at, 1 + plane)
        high, low = by_side(even, one, two)
        north.append(high)
        south.append(low)
    mid = [own[plane] for plane in range(nflux)]
    for row_tile in range(rows // TILE):
        here = slice(row_tile * TILE, (row_tile + 1) * TILE)
        for b in range(blocks):
            cols = slice(b * LANES, (b + 1) * LANES)
            totals = [jnp.zeros((TILE, LANES), f32) for _ in range(nflux)]
            for k in range(links):
                within, band = row_numbers(own[nflux + row_tile], k * blocks + b)
                lanes = points[k, here, cols]
                weight = weights[k, here, cols]
                for plane in range(nflux):
                    value = jnp.where(
                        band == 0,
                        pick(south[plane], within),
                        jnp.where(band == 1, pick(mid[plane], within), pick(north[plane], within)),
                    )
                    totals[plane] = totals[plane] + weight * pick_lane(value, lanes)
            for plane in range(nflux):
                if plane in FORCING_AT:
                    ext[FORCING_AT[plane], here, cols] = totals[plane]
                else:
                    light[plane - 2, here, cols] = totals[plane]


def forcing_halo_body(
    flux_at, draft, got_a, got_b, got_c, own, edges, edges_halo, ext, send_a, send_b
):
    even = lax.rem(lax.axis_index("lat"), 2) == 0
    rows, width = 2 * TILE, ext.shape[2]
    blocks = width // LANES
    links = flux_at - 2
    sub = row_ids(TILE, width)
    halos = []
    for place in range(flux_at):
        north, south = by_side(even, got_a[place], got_b[place])
        halos.append(jnp.where(sub < HALF, north, south))
        halos.append(roll_rows(jnp.where(sub < HALF, south, north), HALF))
    for place in range(4):
        ext[place, rows:, :] = halos[place]
    last = got_b.shape[0] - 2
    far_b = [got_b[last, :, :LANES], got_b[last, :, LANES:], got_b[last + 1, :, :LANES]]
    tables = {}
    for place, plane in enumerate(HALO_FLUXES):
        one, two = spot_of(got_a, flux_at, 1 + plane), spot_of(got_b, flux_at, 1 + plane)
        north, south = by_side(even, one, two)
        far_north, far_south = by_side(even, got_c[place], far_b[place])
        tables[plane] = [far_south, south, own[plane], north, far_north]
    sub_one = row_ids(TILE)
    north, south = by_side(even, spot_of(got_a, flux_at, 0), spot_of(got_b, flux_at, 0))
    numbers = jnp.where(sub_one < HALF, north, south)
    for b in range(blocks):
        cols = slice(b * LANES, (b + 1) * LANES)
        totals = {plane: jnp.zeros((TILE, LANES), f32) for plane in HALO_FLUXES}
        for k in range(links):
            within, band = row_numbers(numbers, k * blocks + b)
            band = band + jnp.where(sub_one < HALF, 2, 0)
            lanes = halos[4 + k][:, cols].astype(i32)
            weight = halos[4 + links + k][:, cols]
            for plane in HALO_FLUXES:
                value = pick(tables[plane][0], within)
                for at in range(1, 5):
                    value = jnp.where(band == at, pick(tables[plane][at], within), value)
                totals[plane] = totals[plane] + weight * pick_lane(value, lanes)
        for plane in HALO_FLUXES:
            ext[FORCING_AT[plane], rows:, cols] = totals[plane]

    lane = lane_ids(3 * TILE)
    to_west = jnp.zeros((3 * TILE, LANES), f32)
    to_east = jnp.zeros((3 * TILE, LANES), f32)
    for place in range(ext.shape[0]):
        low = roll_lanes(ext[place, :, :LANES], 3 * place)
        high = roll_lanes(ext[place, :, width - LANES :], -3 * place)
        to_west = jnp.where((lane >= 3 * place) & (lane < 3 * place + 3), low, to_west)
        edge = LANES - 3 * place
        to_east = jnp.where((lane >= edge - 3) & (lane < edge), high, to_east)
    lon_even = lax.rem(lax.axis_index("lon"), 2) == 0
    send_a[0] = jnp.where(lon_even, to_east, to_west)
    send_b[0] = jnp.where(lon_even, to_west, to_east)
    for part, columns in ((slice(0, rows), edges), (slice(rows, rows + TILE), edges_halo)):
        send_a[1, part, :] = jnp.where(lon_even, columns[1], columns[0])
        send_b[1, part, :] = jnp.where(lon_even, columns[0], columns[1])


def column_depth(counts, levels):
    scale = 1.0 / (2.0 * levels)
    return counts * scale + counts * (counts - 1.0) * (scale / levels)


def level_tendency(level, temp_level, halo_level, ends_temp, ends_lap, limits, speeds):
    width = temp_level.shape[1]
    rows = temp_level.shape[0]
    whole = jnp.concatenate([temp_level, halo_level], axis=0)
    lane = lane_ids(3 * TILE, width)
    turn = lax.rem(2 * LANES - 2 * level, LANES)
    level_f = level.astype(f32)

    def beside(array, ends):
        turned = pltpu.roll(ends, turn, 1)
        turned = jnp.concatenate([turned] * (width // LANES), axis=1)
        spots = lane[: array.shape[0]]
        east = roll_lanes(jnp.where(spots == 0, turned, array), -1)
        west = roll_lanes(jnp.where(spots == width - 1, turned, array), 1)
        return east, west

    east, west = beside(whole, ends_temp)
    north, south = roll_rows(whole, -1), roll_rows(whole, 1)
    opens = [level_f < limit for limit in limits]
    lap = -4.0 * whole
    for around, is_open in zip((east, west, north, south), opens):
        lap = lap + jnp.where(is_open, around, whole)
    own = whole[:rows]
    own_lap = lap[:rows]
    lap_east, lap_west = beside(own_lap, ends_lap)
    lap_north, lap_south = roll_rows(lap, -1)[:rows], roll_rows(lap, 1)[:rows]
    opens = [is_open[:rows] for is_open in opens]
    mixing = -4.0 * own_lap
    for around, is_open in zip((lap_east, lap_west, lap_north, lap_south), opens):
        mixing = mixing + jnp.where(is_open, around, own_lap)
    carried = [
        jnp.where(is_open, speed * (around[:rows] + own), 0.0)
        for around, is_open, speed in zip((east, west, north, south), opens, speeds)
    ]
    advect = carried[0] - carried[1] + carried[2] - carried[3]
    return -advect_coef * advect - mixing_fourth * mixing


def level_update(level, own, lateral, down, down_before, counts, solar, heat):
    level_f = level.astype(f32)
    absorb = jnp.exp(jnp.full(own.shape, -1.0 / light_decay, f32) * level_f)
    absorb = absorb * (light_gain * (1.0 - math.exp(-1.0 / light_decay)))
    source = absorb * solar + jnp.where(level == 0, heat_gain, 0.0) * heat
    change = diapycnal_diffusion * (down - down_before) + lateral + source
    return own + jnp.where(level_f < counts, change, 0.0)


def subcycle_body(
    levels,
    ext,
    light,
    edges_own,
    edges_halo,
    got_a,
    got_b,
    temp,
    halo,
    points,
    weights,
    tile_hbm,
    out_height,
    out_zonal,
    out_merid,
    limits_out,
    speeds_out,
    ends_out,
    sums_a,
    sums_b,
    sums_mid,
    values,
    table,
    tile,
    tile_sem,
):
    tile_copy = pltpu.make_async_copy(tile_hbm, tile, tile_sem)
    tile_copy.start()
    edges = [
        jnp.concatenate([edges_own[place], edges_halo[place]], axis=0) for place in range(2)
    ]
    width = ext.shape[2]
    rows = temp.shape[1]
    lon_even = lax.rem(lax.axis_index("lon"), 2) == 0
    even = lax.rem(lax.axis_index("lat"), 2) == 0
    lane = lane_ids(3 * TILE)
    from_east = [jnp.where(lon_even, got_a[place], got_b[place]) for place in range(2)]
    from_west = [jnp.where(lon_even, got_b[place], got_a[place]) for place in range(2)]
    planes = []
    for place in range(ext.shape[0]):
        third = jnp.where(
            lane < 3,
            roll_lanes(from_east[0], -3 * place),
            jnp.where(lane >= LANES - 3, roll_lanes(from_west[0], 3 * place), 0.0),
        )
        planes.append(jnp.concatenate([ext[place], third], axis=1))
    height, zonal, merid, counts, wind_east, wind_north, fresh = planes

    def east_of(array):
        return roll_lanes(array, -1)

    def west_of(array):
        return roll_lanes(array, 1)

    def north_of(array):
        return roll_rows(array, -1)

    def south_of(array):
        return roll_rows(array, 1)

    depth = column_depth(counts, levels)
    wet = (counts > 0.5).astype(f32)
    east_wet = wet * east_of(wet)
    north_wet = wet * north_of(wet)
    east_depth = jnp.minimum(depth, east_of(depth))
    north_depth = jnp.minimum(depth, north_of(depth))
    east_pull = grav_step * east_depth
    north_pull = grav_step * north_depth
    wind_east = wind_step * wind_east
    wind_north = wind_step * wind_north
    fresh = fresh_step * fresh
    for _ in range(SUBS):
        zonal = east_wet * (zonal - east_pull * (east_of(height) - height) + wind_east)
        merid = north_wet * (merid - north_pull * (north_of(height) - height) + wind_north)
        spread = zonal - west_of(zonal) + merid - south_of(merid)
        height = height + wet * (fresh - height_step * spread)
    out_height[...] = height[:rows, :width]
    out_zonal[...] = zonal[:rows, :width]
    out_merid[...] = merid[:rows, :width]

    limit_east = jnp.minimum(counts, east_of(counts))
    limit_north = jnp.minimum(counts, north_of(counts))
    limit_west, limit_south = west_of(limit_east), south_of(limit_north)
    limits = [
        limit[:, :width] for limit in (limit_east, limit_west, limit_north, limit_south)
    ]
    speed_east = 0.5 * zonal / jnp.maximum(east_depth, depth_floor)
    speed_north = 0.5 * merid / jnp.maximum(north_depth, depth_floor)
    speeds = [
        speed[:rows, :width]
        for speed in (speed_east, west_of(speed_east), speed_north, south_of(speed_north))
    ]
    for place in range(4):
        limits_out[place] = limits[place]
        speeds_out[place] = speeds[place]

    lane_level = (lane // 2).astype(f32)
    odd_lane = (lane & 1) == 1
    far_east, far_west = from_east[1], from_west[1]

    def column(limit, at):
        return jnp.broadcast_to(limit[:, at : at + 1], (3 * TILE, LANES))

    def edge_lap(center, toward_east, toward_west, at, at_west):
        total = -4.0 * center
        for around, limit in (
            (toward_east, column(limit_east, at)),
            (toward_west, column(limit_east, at_west)),
            (north_of(center), column(limit_north, at)),
            (south_of(center), column(limit_south, at)),
        ):
            total = total + jnp.where(lane_level < limit, around, center)
        return total

    total_lanes = width + LANES
    lap_west = edge_lap(
        far_west,
        roll_lanes(edges[0], 1),
        roll_lanes(far_west, 1),
        total_lanes - 1,
        total_lanes - 2,
    )
    lap_east = edge_lap(
        far_east, roll_lanes(far_east, -1), roll_lanes(edges[1], -1), width, width - 1
    )
    ends_temp = jnp.where(odd_lane, roll_lanes(far_west, -2), far_east)
    ends_lap = jnp.where(odd_lane, roll_lanes(lap_west, -2), lap_east)
    ends_out[0] = ends_temp
    ends_out[1] = ends_lap

    own_counts = counts[:rows, :width]
    zero = jnp.zeros((), i32)
    lateral = level_tendency(
        zero, temp[0], halo[0], ends_temp, ends_lap[:rows], limits, speeds
    )
    if levels > 1:
        down = jnp.where(own_counts > 1.0, temp[1] - temp[0], 0.0)
    else:
        down = jnp.zeros((rows, width), f32)
    top = level_update(
        zero, temp[0], lateral, down, jnp.zeros_like(down), own_counts, light[1], light[0]
    )
    own_wet = wet[:rows, :width]
    thick = jnp.maximum(depth[:rows, :width], depth_floor)
    surface = [
        top * own_wet,
        height[:rows, :width] * own_wet,
        zonal[:rows, :width] / thick * own_wet,
        merid[:rows, :width] / thick * own_wet,
        own_wet,
    ]
    nsums = len(surface)
    values[...] = jnp.zeros(values.shape, f32)
    for place in range(nsums):
        values[:, place, :] = surface[place]
    table[...] = jnp.zeros(table.shape, f32)
    links = points.shape[0]
    blocks = width // LANES
    cells = lax.broadcasted_iota(i32, (LANES, LANES), 0)
    tile_copy.wait()

    for row in range(rows):
        held = values[row]
        for k in range(links):
            shares = held * weights[k, row : row + 1, :]
            upper = shares.astype(jnp.bfloat16)
            lower = (shares - upper.astype(f32)).astype(jnp.bfloat16)
            both = jnp.concatenate([upper, lower], axis=0)
            for b in range(blocks):
                cols = slice(b * LANES, (b + 1) * LANES)
                hot = (cells == points[k, row : row + 1, cols]).astype(f32).astype(jnp.bfloat16)
                found = lax.dot_general(
                    both[:, cols], hot, (((1,), (1,)), ((), ())), preferred_element_type=f32
                )
                target = tile[k, b, row]
                table[target] = table[target] + found
    for place in range(nsums):
        total = table[:, place, :] + table[:, TILE + place, :]
        south, middle, north = total[:TILE], total[TILE : 2 * TILE], total[2 * TILE :]
        sums_mid[place] = middle
        sums_a[place] = jnp.where(even, north, south)
        sums_b[place] = jnp.where(even, south, north)


LEVELS_AT_ONCE = 4


def tracer_body(temp, halo, limits, speeds, ends, light, state, out):
    levels, rows, width = temp.shape
    own_counts = state[3]

    def one_level(level, down_before):
        own = temp[level]
        lateral = level_tendency(
            level,
            own,
            halo[level],
            ends[0],
            ends[1, :rows],
            [limits[place] for place in range(4)],
            [speeds[place] for place in range(4)],
        )
        beneath = temp[jnp.minimum(level + 1, levels - 1)]
        down = jnp.where((level + 1).astype(f32) < own_counts, beneath - own, 0.0)
        out[level] = level_update(
            level, own, lateral, down, down_before, own_counts, light[1], light[0]
        )
        return down

    lax.fori_loop(
        0, levels, one_level, jnp.zeros((rows, width), f32), unroll=math.gcd(levels, LEVELS_AT_ONCE)
    )


def merge_body(mid, got_a, got_b, flags, out):
    open_sea = (1 - flags[...]).astype(f32)
    nsurf = out.shape[0]
    area = mid[nsurf] + got_a[nsurf] + got_b[nsurf]
    scale = open_sea / jnp.maximum(area, area_floor)
    for place in range(nsurf):
        out[place] = (mid[place] + got_a[place] + got_b[place]) * scale


def shards(
    free_elevation,
    zonal_volume_carriage,
    meridional_volume_carriage,
    thermal_field,
    flooded_strata_number,
    aerial_exchanges,
    aerial_terrain_flags,
    donor_tile_number,
    donor_point_number,
    pairing_coefficients,
):
    levels, rows, width = thermal_field.shape
    nflux, band_rows, lanes = aerial_exchanges.shape
    links, _, blocks = donor_tile_number.shape
    assert rows == 2 * TILE and band_rows == TILE and lanes == LANES
    assert 2 * levels <= LANES and lax.axis_size("lon") % 2 == 0
    nsums = 5
    fields = 4 + 2 * links
    flux_at = fields // 2
    temp_at = flux_at + (nflux + 1) // 2
    groups = pl.cdiv(levels, 4)
    tile_lines = jnp.swapaxes(donor_tile_number, 1, 2)
    edge_a, own, state, points, weights, flags, temp = call(
        load_body,
        [
            shape(temp_at + groups, TILE, width),
            shape(nflux + 2, TILE, LANES),
            shape(4, rows, width),
            shape(links, rows, width, dtype=i32),
            shape(links, rows, width),
            shape(band_rows, lanes, dtype=i32),
            shape(levels, rows, width),
        ],
        (
            free_elevation,
            zonal_volume_carriage,
            meridional_volume_carriage,
            flooded_strata_number,
            donor_point_number,
            tile_lines,
            pairing_coefficients,
            aerial_exchanges,
            aerial_terrain_flags,
            thermal_field,
        ),
        "load",
        1000000,
        scratch=[
            pltpu.VMEM((rows, width), i32),
            pltpu.VMEM((links, blocks, rows), i32),
            pltpu.VMEM((nflux, band_rows, lanes), f32),
            pltpu.SemaphoreType.DMA((10,)),
        ],
        hbm=range(10),
    )
    got_a = swap(edge_a, "lat", 0, False)
    draft_b, temp_b, edges = call(
        pack_second_body,
        [
            shape(temp_at + 2, TILE, width),
            shape(groups, TILE, width),
            shape(2, rows, LANES),
        ],
        (own, state, points, weights, temp),
        "pack_b",
        1000000,
    )
    (edge_b,) = call(
        functools.partial(pack_flux_body, flux_at),
        [shape(temp_at + 2, TILE, width)],
        (draft_b, got_a),
        "pack_b_flux",
        1000,
        aliases={0: 0},
    )
    got_b = swap(edge_b, "lat", 1, False)
    got_temp_b = swap(temp_b, "lat", 1, False)
    (edge_c,) = call(
        functools.partial(pack_third_body, flux_at),
        [shape(len(HALO_FLUXES), TILE, LANES)],
        (got_b,),
        "pack_c",
        1000,
    )
    got_c = swap(edge_c, "lat", 0, False)
    draft_ext, light = call(
        functools.partial(forcing_body, flux_at),
        [shape(7, 3 * TILE, width), shape(2, rows, width)],
        (got_a, got_b, own, state, points, weights),
        "forcing",
        1000000,
    )
    halo, edges_halo = call(
        functools.partial(unpack_temp_body, temp_at),
        [shape(levels, TILE, width), shape(2, TILE, LANES)],
        (got_a, got_temp_b),
        "unpack_temp",
        1000000,
    )
    ext, send_a, send_b = call(
        functools.partial(forcing_halo_body, flux_at),
        [
            shape(7, 3 * TILE, width),
            shape(2, 3 * TILE, LANES),
            shape(2, 3 * TILE, LANES),
        ],
        (draft_ext, got_a, got_b, got_c, own, edges, edges_halo),
        "forcing_halo",
        1000000,
        aliases={0: 0},
    )
    lon_a = swap(send_a, "lon", 0, True)
    lon_b = swap(send_b, "lon", 1, True)
    (
        advanced_elevation,
        transport_x_next,
        transport_y_next,
        limits,
        speeds,
        ends,
        sums_a,
        sums_b,
        sums_mid,
    ) = call(
        functools.partial(subcycle_body, levels),
        [shape(rows, width)] * 3
        + [shape(4, 3 * TILE, width), shape(4, rows, width), shape(2, 3 * TILE, LANES)]
        + [shape(nsums, TILE, LANES)] * 3,
        (
            ext,
            light,
            edges,
            edges_halo,
            lon_a,
            lon_b,
            temp,
            halo,
            points,
            weights,
            tile_lines,
        ),
        "subcycles",
        100000000,
        scratch=[
            pltpu.VMEM((rows, TILE, width), f32),
            pltpu.VMEM((3 * TILE, 2 * TILE, LANES), f32),
            pltpu.SMEM((links, blocks, rows), i32),
            pltpu.SemaphoreType.DMA(()),
        ],
        hbm=(10,),
    )
    back_a = swap(sums_a, "lat", 0, False)
    back_b = swap(sums_b, "lat", 1, False)
    (advanced_thermal_field,) = call(
        tracer_body,
        [shape(levels, rows, width)],
        (temp, halo, limits, speeds, ends, light, state),
        "tracer",
        20000000,
    )
    (marine_skin_condition,) = call(
        merge_body,
        [shape(nsums - 1, TILE, LANES)],
        (sums_mid, back_a, back_b, flags),
        "merge",
        1000,
    )
    return (
        advanced_elevation,
        transport_x_next,
        transport_y_next,
        advanced_thermal_field,
        marine_skin_condition,
    )


def solution(mesh):
    flat = P("lat", "lon")
    deep = P(None, "lat", "lon")
    return jax.shard_map(
        shards,
        mesh=mesh,
        in_specs=(flat, flat, flat, deep, flat, deep, flat, deep, deep, deep),
        out_specs=(flat, flat, flat, deep, deep),
        check_vma=False,
    )
```

```python
import functools
import math

import jax
import jax.numpy as jnp
from jax import lax
from jax.experimental import pallas as pl
from jax.experimental.pallas import tpu as pltpu
from jax.sharding import PartitionSpec as P

SUBS = 3

grav_step = 0.6
height_step = 0.6
wind_step = 0.5
fresh_step = 0.5
mixing_fourth = 0.02
advect_coef = 0.1
diapycnal_diffusion = 0.2
heat_gain = 0.3
light_gain = 0.3
light_decay = 8.0
depth_floor = 0.25
area_floor = 1.0

TILE = 8
LANES = 128
HALF = TILE // 2

f32 = jnp.float32
i32 = jnp.int32

LATE = 4.0
FLOPS_PER_US = 1150000000


def swap_pairs(count, first, periodic):
    pairs = []
    for low in range(first, count, 2):
        high = low + 1
        if high == count:
            if not periodic:
                continue
            high = 0
        pairs += [(low, high), (high, low)]
    return pairs


def swap(array, axis, first, periodic):
    return lax.ppermute(array, axis, swap_pairs(lax.axis_size(axis), first, periodic))


def lane_ids(rows, width=LANES):
    return lax.broadcasted_iota(i32, (rows, width), 1)


def row_ids(rows, width=LANES):
    return lax.broadcasted_iota(i32, (rows, width), 0)


def roll_rows(array, by):
    by = by % array.shape[0]
    return pltpu.roll(array, by, 0) if by else array


def roll_lanes(array, by):
    by = by % array.shape[1]
    return pltpu.roll(array, by, 1) if by else array


def call(body, outs, ins, name, took, aliases=None, scratch=(), hbm=()):
    specs = [
        pl.BlockSpec(memory_space=pltpu.HBM if place in hbm else pltpu.VMEM)
        for place in range(len(ins))
    ]
    ins = [
        pltpu.with_memory_space_constraint(leaf, pltpu.HBM) if place in hbm else leaf
        for place, leaf in enumerate(ins)
    ]
    moved = 4 * sum(math.prod(leaf.shape) for leaf in outs)
    return pl.pallas_call(
        body,
        out_shape=outs,
        in_specs=specs,
        out_specs=[pl.BlockSpec(memory_space=leaf.memory_space) for leaf in outs],
        scratch_shapes=list(scratch),
        input_output_aliases=aliases or {},
        compiler_params=pltpu.CompilerParams(vmem_limit_bytes=24 * 1024 * 1024),
        cost_estimate=pl.CostEstimate(
            flops=int(took * FLOPS_PER_US), bytes_accessed=moved, transcendentals=0
        ),
        name=name,
    )(*ins)


def shape(*dims, dtype=f32):
    return pltpu.VMEM(dims, dtype)


def write_edge(top, fields, tiles, masked, out_ref):
    sub = row_ids(TILE, out_ref.shape[2])
    mine = (sub >= HALF) == top
    for place in range(len(fields) // 2):
        first = jnp.where(top, fields[2 * place][TILE:], fields[2 * place][:TILE])
        second = jnp.where(top, fields[2 * place + 1][TILE:], fields[2 * place + 1][:TILE])
        out_ref[place] = jnp.where(mine, first, roll_rows(second, HALF))
    at = len(fields) // 2
    numbers = jnp.where(top, tiles[TILE:], tiles[:TILE])
    planes = [numbers] + masked
    for place in range(len(planes) // 2):
        out_ref[at + place] = jnp.concatenate(planes[2 * place : 2 * place + 2], axis=1)


def write_temp_edge(top, temp_ref, out_ref, at):
    levels, _, width = temp_ref.shape
    sub = row_ids(TILE, width)
    for group in range(pl.cdiv(levels, 4)):
        packed = jnp.zeros((TILE, width), f32)
        for spot in range(min(4, levels - 4 * group)):
            level = 4 * group + spot
            low = roll_rows(temp_ref[level, :TILE, :], 2 * spot)
            high = roll_rows(temp_ref[level, TILE:, :], 2 * spot + 2)
            packed = jnp.where(sub // 2 == spot, jnp.where(top, high, low), packed)
        out_ref[at + group] = packed


def goes_north(first):
    return (lax.rem(lax.axis_index("lat"), 2) == 0) == (first == 0)


def edge_fields(state, points, weights):
    links = points.shape[0]
    fields = [state[place] for place in range(4)]
    fields += [points[k].astype(f32) for k in range(links)]
    fields += [weights[k] for k in range(links)]
    return fields


def load_body(
    height,
    zonal,
    merid,
    counts,
    points,
    tile,
    weights,
    flux,
    flags,
    temp,
    edge,
    own,
    state_out,
    points_out,
    weights_out,
    flags_out,
    temp_out,
    counts_in,
    tile_in,
    flux_in,
    sems,
):
    pairs = [
        (flux, flux_in),
        (flags, flags_out),
        (tile, tile_in),
        (counts, counts_in),
        (height, state_out.at[0]),
        (zonal, state_out.at[1]),
        (merid, state_out.at[2]),
        (points, points_out),
        (weights, weights_out),
        (temp, temp_out),
    ]
    copies = [
        pltpu.make_async_copy(source, target, sems.at[place])
        for place, (source, target) in enumerate(pairs)
    ]
    for copy in copies:
        copy.start()
    for copy in copies[:-1]:
        copy.wait()
    state_out[3] = counts_in[...].astype(f32)
    links, blocks, rows = tile.shape
    open_sea = (1 - flags_out[...]).astype(f32)
    masked = [flux_in[plane] * open_sea for plane in range(flux.shape[0])]
    lane = lane_ids(rows)
    diagonal = row_ids(rows, rows) == lane_ids(rows, rows)
    tiles = jnp.zeros((rows, LANES), f32)
    for k in range(links):
        for b in range(blocks):
            line = jnp.broadcast_to(tile_in[k, b : b + 1, :].astype(f32), (rows, rows))
            upright = jnp.sum(jnp.where(diagonal, line, 0.0), axis=1, keepdims=True)
            tiles = jnp.where(lane == k * blocks + b, upright, tiles)
    for plane, values in enumerate(masked):
        own[plane] = values
    own[len(masked)] = tiles[:TILE]
    own[len(masked) + 1] = tiles[TILE:]
    top = goes_north(0)
    fields = edge_fields(state_out, points_out, weights_out)
    write_edge(top, fields, tiles, masked, edge)
    copies[-1].wait()
    write_temp_edge(top, temp_out, edge, len(fields) // 2 + (len(masked) + 1) // 2)


def pack_second_body(own, state, points, weights, temp, draft, temp_edge, edges):
    top = goes_north(1)
    nflux = own.shape[0] - 2
    tiles = jnp.concatenate([own[nflux], own[nflux + 1]], axis=0)
    masked = [own[plane] for plane in range(nflux)]
    fields = edge_fields(state, points, weights)
    write_edge(top, fields, tiles, masked, draft)
    write_temp_edge(top, temp, temp_edge, 0)
    rows = temp.shape[1]
    columns = edge_columns([temp[level] for level in range(temp.shape[0])], rows)
    for place in range(2):
        edges[place] = columns[place]
    at = draft.shape[0] - 4
    both = jnp.concatenate(columns, axis=1)
    draft[at] = jnp.where(top, both[TILE:], both[:TILE])
    draft[at + 1] = jnp.where(top, temp[0, TILE:, :], temp[0, :TILE, :])


def edge_columns(fields, rows):
    lane = lane_ids(rows)
    high = jnp.zeros((rows, LANES), f32)
    low = jnp.zeros((rows, LANES), f32)
    for level, field in enumerate(fields):
        ends = jnp.where(lane < HALF, field[:, :LANES], field[:, -LANES:])
        turned = roll_lanes(ends, 2 * level + 2)
        high = jnp.where(lane // 2 == level, turned, high)
        low = jnp.where(lane // 2 == (level + 1) % (LANES // 2), turned, low)
    return roll_lanes(low, -2), high


HALO_FLUXES = (0, 1, 4)


def pack_flux_body(flux_at, draft, received, out):
    last = out.shape[0] - 2
    planes = []
    for plane in HALO_FLUXES:
        spot = flux_at * 2 + 1 + plane
        planes.append(received[spot // 2, :, (spot % 2) * LANES : (spot % 2 + 1) * LANES])
    out[last] = jnp.concatenate(planes[:2], axis=1)
    out[last + 1] = jnp.concatenate([planes[2], planes[2]], axis=1)


def pass_body(first, second, out):
    out[0] = first[0]


def pack_third_body(flux_at, received, out):
    for place, plane in enumerate(HALO_FLUXES):
        spot = flux_at * 2 + 1 + plane
        out[place] = received[spot // 2, :, (spot % 2) * LANES : (spot % 2 + 1) * LANES]


def unpack_rows(top, packed, level):
    spot = level % 4
    return jnp.where(top, roll_rows(packed, -2 * spot), roll_rows(packed, 6 - 2 * spot))


def near_lanes(width):
    north = lax.rem(lax.axis_index("lat"), 2) == 0
    return (row_ids(TILE, width) < HALF) == north


def unpack_first_body(temp_at, got_a, halo, edges):
    levels, _, width = halo.shape
    even = lax.rem(lax.axis_index("lat"), 2) == 0
    fields = []
    for level in range(levels):
        rows = unpack_rows(even, got_a[temp_at + level // 4], level)
        halo[level] = rows
        fields.append(rows)
    for place, columns in enumerate(edge_columns(fields, TILE)):
        edges[place] = columns


def pick(array, rows):
    return jnp.take_along_axis(array, rows, axis=0, mode="promise_in_bounds")


def pick_lane(array, lanes):
    return jnp.take_along_axis(array, lanes, axis=1, mode="promise_in_bounds")


def spot_of(array, flux_at, place):
    return array[flux_at + place // 2, :, (place % 2) * LANES : (place % 2 + 1) * LANES]


def by_side(even, one, two):
    return jnp.where(even, one, two), jnp.where(even, two, one)


def row_numbers(numbers, column):
    number = jnp.broadcast_to(numbers[:, column : column + 1].astype(i32), (TILE, LANES))
    return number & (TILE - 1), lax.shift_right_logical(number, 3)


FORCING_AT = {0: 4, 1: 5, 4: 6}


def forcing_body(flux_at, got_a, got_b, own, state, points, weights, ext, light):
    even = lax.rem(lax.axis_index("lat"), 2) == 0
    links, rows, width = points.shape
    blocks = width // LANES
    nflux = own.shape[0] - 2
    ext[:4, :rows, :] = state[...]
    north, south = [], []
    for plane in range(nflux):
        one, two = spot_of(got_a, flux_at, 1 + plane), spot_of(got_b, flux_at, 1 + plane)
        high, low = by_side(even, one, two)
        north.append(high)
        south.append(low)
    mid = [own[plane] for plane in range(nflux)]
    for row_tile in range(rows // TILE):
        here = slice(row_tile * TILE, (row_tile + 1) * TILE)
        for b in range(blocks):
            cols = slice(b * LANES, (b + 1) * LANES)
            totals = [jnp.zeros((TILE, LANES), f32) for _ in range(nflux)]
            for k in range(links):
                within, band = row_numbers(own[nflux + row_tile], k * blocks + b)
                lanes = points[k, here, cols]
                weight = weights[k, here, cols]
                for plane in range(nflux):
                    value = jnp.where(
                        band == 0,
                        pick(south[plane], within),
                        jnp.where(band == 1, pick(mid[plane], within), pick(north[plane], within)),
                    )
                    totals[plane] = totals[plane] + weight * pick_lane(value, lanes)
            for plane in range(nflux):
                if plane in FORCING_AT:
                    ext[FORCING_AT[plane], here, cols] = totals[plane]
                else:
                    light[plane - 2, here, cols] = totals[plane]


def forcing_halo_body(
    flux_at, draft, got_a, got_b, got_c, own, edges, edges_near, ext, send_a, send_b, edges_halo
):
    even = lax.rem(lax.axis_index("lat"), 2) == 0
    rows, width = 2 * TILE, ext.shape[2]
    blocks = width // LANES
    links = flux_at - 2
    sub = row_ids(TILE, width)
    halos = []
    for place in range(flux_at):
        north, south = by_side(even, got_a[place], got_b[place])
        halos.append(jnp.where(sub < HALF, north, south))
        halos.append(roll_rows(jnp.where(sub < HALF, south, north), HALF))
    for place in range(4):
        ext[place, rows:, :] = halos[place]
    last = got_b.shape[0] - 2
    far_b = [got_b[last, :, :LANES], got_b[last, :, LANES:], got_b[last + 1, :, :LANES]]
    tables = {}
    for place, plane in enumerate(HALO_FLUXES):
        one, two = spot_of(got_a, flux_at, 1 + plane), spot_of(got_b, flux_at, 1 + plane)
        north, south = by_side(even, one, two)
        far_north, far_south = by_side(even, got_c[place], far_b[place])
        tables[plane] = [far_south, south, own[plane], north, far_north]
    sub_one = row_ids(TILE)
    north, south = by_side(even, spot_of(got_a, flux_at, 0), spot_of(got_b, flux_at, 0))
    numbers = jnp.where(sub_one < HALF, north, south)
    for b in range(blocks):
        cols = slice(b * LANES, (b + 1) * LANES)
        totals = {plane: jnp.zeros((TILE, LANES), f32) for plane in HALO_FLUXES}
        for k in range(links):
            within, band = row_numbers(numbers, k * blocks + b)
            band = band + jnp.where(sub_one < HALF, 2, 0)
            lanes = halos[4 + k][:, cols].astype(i32)
            weight = halos[4 + links + k][:, cols]
            for plane in HALO_FLUXES:
                value = pick(tables[plane][0], within)
                for at in range(1, 5):
                    value = jnp.where(band == at, pick(tables[plane][at], within), value)
                totals[plane] = totals[plane] + weight * pick_lane(value, lanes)
        for plane in HALO_FLUXES:
            ext[FORCING_AT[plane], rows:, cols] = totals[plane]

    lane = lane_ids(3 * TILE)
    to_west = jnp.zeros((3 * TILE, LANES), f32)
    to_east = jnp.zeros((3 * TILE, LANES), f32)
    for place in range(ext.shape[0]):
        low = roll_lanes(ext[place, :, :LANES], 3 * place)
        high = roll_lanes(ext[place, :, width - LANES :], -3 * place)
        to_west = jnp.where((lane >= 3 * place) & (lane < 3 * place + 3), low, to_west)
        edge = LANES - 3 * place
        to_east = jnp.where((lane >= edge - 3) & (lane < edge), high, to_east)
    near = near_lanes(LANES)
    at = got_b.shape[0] - 4
    for place in range(2):
        far = got_b[at, :, place * LANES : (place + 1) * LANES]
        edges_halo[place] = jnp.where(near, edges_near[place], far)
    lon_even = lax.rem(lax.axis_index("lon"), 2) == 0
    send_a[0] = jnp.where(lon_even, to_east, to_west)
    send_b[0] = jnp.where(lon_even, to_west, to_east)
    for part, columns in ((slice(0, rows), edges), (slice(rows, rows + TILE), edges_halo)):
        send_a[1, part, :] = jnp.where(lon_even, columns[1], columns[0])
        send_b[1, part, :] = jnp.where(lon_even, columns[0], columns[1])


def column_depth(counts, levels):
    scale = 1.0 / (2.0 * levels)
    return counts * scale + counts * (counts - 1.0) * (scale / levels)


def level_tendency(level, temp_level, halo_level, ends_temp, ends_lap, limits, speeds):
    rows, width = temp_level.shape
    whole = jnp.concatenate([temp_level, halo_level], axis=0)
    lane = lane_ids(3 * TILE)
    turn = lax.rem(2 * LANES - 2 * level, LANES)
    level_f = level.astype(f32)

    def beside(array, ends):
        ends = pltpu.roll(ends, turn, 1)
        lanes = lane[: array.shape[0]]
        parts = [array[:, at : at + LANES] for at in range(0, width, LANES)]
        right = [roll_lanes(part, -1) for part in parts] + [ends]
        left = [ends] + [roll_lanes(part, 1) for part in parts]
        east = [jnp.where(lanes == LANES - 1, b, a) for a, b in zip(right, right[1:])]
        west = [jnp.where(lanes == 0, a, b) for a, b in zip(left, left[1:])]
        return jnp.concatenate(east, axis=1), jnp.concatenate(west, axis=1)

    east, west = beside(whole, ends_temp)
    north, south = roll_rows(whole, -1), roll_rows(whole, 1)
    opens = [level_f < limit for limit in limits]
    lap = -4.0 * whole
    for around, is_open in zip((east, west, north, south), opens):
        lap = lap + jnp.where(is_open, around, whole)
    own = whole[:rows]
    own_lap = lap[:rows]
    lap_east, lap_west = beside(own_lap, ends_lap)
    lap_north, lap_south = roll_rows(lap, -1)[:rows], roll_rows(lap, 1)[:rows]
    opens = [is_open[:rows] for is_open in opens]
    mixing = -4.0 * own_lap
    for around, is_open in zip((lap_east, lap_west, lap_north, lap_south), opens):
        mixing = mixing + jnp.where(is_open, around, own_lap)
    carried = [
        jnp.where(is_open, speed * (around[:rows] + own), 0.0)
        for around, is_open, speed in zip((east, west, north, south), opens, speeds)
    ]
    advect = carried[0] - carried[1] + carried[2] - carried[3]
    return -advect_coef * advect - mixing_fourth * mixing


def level_update(level, own, lateral, down, down_before, counts, solar, heat):
    level_f = level.astype(f32)
    absorb = jnp.exp(jnp.full(own.shape, -1.0 / light_decay, f32) * level_f)
    absorb = absorb * (light_gain * (1.0 - math.exp(-1.0 / light_decay)))
    source = absorb * solar + jnp.where(level == 0, heat_gain, 0.0) * heat
    change = diapycnal_diffusion * (down - down_before) + lateral + source
    return own + jnp.where(level_f < counts, change, 0.0)


def hot_body(points, hot):
    links, rows, width = points.shape
    blocks = width // LANES
    lane = lane_ids(LANES)
    lines = [
        points[k, :, b * LANES : (b + 1) * LANES] for k in range(links) for b in range(blocks)
    ]
    held = []
    for at in range(0, len(lines) * rows, LANES):
        group = lines[at // rows : (at + LANES) // rows]
        held.append(jnp.transpose(jnp.concatenate(group, axis=0).astype(f32)).astype(i32))
    for at in range(links * blocks * rows):
        column = held[at // LANES][:, at % LANES : at % LANES + 1]
        hot[at] = (column == lane).astype(f32).astype(jnp.bfloat16)


def subcycle_body(
    levels,
    ext,
    light,
    edges_own,
    edges_halo,
    got_a,
    got_b,
    temp,
    halo_near,
    lat_b,
    hot,
    weights,
    tile_hbm,
    out_height,
    out_zonal,
    out_merid,
    limits_out,
    speeds_out,
    ends_out,
    sums_a,
    sums_b,
    sums_mid,
    values,
    table,
    tile,
    tile_sem,
):
    tile_copy = pltpu.make_async_copy(tile_hbm, tile, tile_sem)
    tile_copy.start()
    edges = [
        jnp.concatenate([edges_own[place], edges_halo[place]], axis=0) for place in range(2)
    ]
    width = ext.shape[2]
    rows = temp.shape[1]
    lon_even = lax.rem(lax.axis_index("lon"), 2) == 0
    even = lax.rem(lax.axis_index("lat"), 2) == 0
    lane = lane_ids(3 * TILE)
    from_east = [jnp.where(lon_even, got_a[place], got_b[place]) for place in range(2)]
    from_west = [jnp.where(lon_even, got_b[place], got_a[place]) for place in range(2)]
    planes = []
    for place in range(ext.shape[0]):
        third = jnp.where(
            lane < 3,
            roll_lanes(from_east[0], -3 * place),
            jnp.where(lane >= LANES - 3, roll_lanes(from_west[0], 3 * place), 0.0),
        )
        planes.append(jnp.concatenate([ext[place], third], axis=1))
    height, zonal, merid, counts, wind_east, wind_north, fresh = planes

    def east_of(array):
        return roll_lanes(array, -1)

    def west_of(array):
        return roll_lanes(array, 1)

    def north_of(array):
        return roll_rows(array, -1)

    def south_of(array):
        return roll_rows(array, 1)

    depth = column_depth(counts, levels)
    wet = (counts > 0.5).astype(f32)
    east_wet = wet * east_of(wet)
    north_wet = wet * north_of(wet)
    east_depth = jnp.minimum(depth, east_of(depth))
    north_depth = jnp.minimum(depth, north_of(depth))
    east_pull = grav_step * east_depth
    north_pull = grav_step * north_depth
    wind_east = wind_step * wind_east
    wind_north = wind_step * wind_north
    fresh = fresh_step * fresh
    for _ in range(SUBS):
        zonal = east_wet * (zonal - east_pull * (east_of(height) - height) + wind_east)
        merid = north_wet * (merid - north_pull * (north_of(height) - height) + wind_north)
        spread = zonal - west_of(zonal) + merid - south_of(merid)
        height = height + wet * (fresh - height_step * spread)
    out_height[...] = height[:rows, :width]
    out_zonal[...] = zonal[:rows, :width]
    out_merid[...] = merid[:rows, :width]

    limit_east = jnp.minimum(counts, east_of(counts))
    limit_north = jnp.minimum(counts, north_of(counts))
    limit_west, limit_south = west_of(limit_east), south_of(limit_north)
    limits = [
        limit[:, :width] for limit in (limit_east, limit_west, limit_north, limit_south)
    ]
    speed_east = 0.5 * zonal / jnp.maximum(east_depth, depth_floor)
    speed_north = 0.5 * merid / jnp.maximum(north_depth, depth_floor)
    speeds = [
        speed[:rows, :width]
        for speed in (speed_east, west_of(speed_east), speed_north, south_of(speed_north))
    ]
    for place in range(4):
        limits_out[place] = limits[place]
        speeds_out[place] = speeds[place]

    lane_level = (lane // 2).astype(f32)
    odd_lane = (lane & 1) == 1
    far_east, far_west = from_east[1], from_west[1]

    def column(limit, at):
        return jnp.broadcast_to(limit[:, at : at + 1], (3 * TILE, LANES))

    def edge_lap(center, toward_east, toward_west, at, at_west):
        total = -4.0 * center
        for around, limit in (
            (toward_east, column(limit_east, at)),
            (toward_west, column(limit_east, at_west)),
            (north_of(center), column(limit_north, at)),
            (south_of(center), column(limit_south, at)),
        ):
            total = total + jnp.where(lane_level < limit, around, center)
        return total

    total_lanes = width + LANES
    lap_west = edge_lap(
        far_west,
        roll_lanes(edges[0], 1),
        roll_lanes(far_west, 1),
        total_lanes - 1,
        total_lanes - 2,
    )
    lap_east = edge_lap(
        far_east, roll_lanes(far_east, -1), roll_lanes(edges[1], -1), width, width - 1
    )
    ends_temp = roll_lanes(jnp.where(odd_lane, far_west, far_east), -1)
    ends_lap = roll_lanes(jnp.where(odd_lane, lap_west, lap_east), -1)
    ends_out[0] = ends_temp
    ends_out[1] = ends_lap

    own_counts = counts[:rows, :width]
    zero = jnp.zeros((), i32)
    top_halo = jnp.where(near_lanes(width), halo_near[0], lat_b[lat_b.shape[0] - 3])
    lateral = level_tendency(
        zero, temp[0], top_halo, ends_temp, ends_lap[:rows], limits, speeds
    )
    if levels > 1:
        down = jnp.where(own_counts > 1.0, temp[1] - temp[0], 0.0)
    else:
        down = jnp.zeros((rows, width), f32)
    top = level_update(
        zero, temp[0], lateral, down, jnp.zeros_like(down), own_counts, light[1], light[0]
    )
    own_wet = wet[:rows, :width]
    thick = jnp.maximum(depth[:rows, :width], depth_floor)
    surface = [
        top * own_wet,
        height[:rows, :width] * own_wet,
        zonal[:rows, :width] / thick * own_wet,
        merid[:rows, :width] / thick * own_wet,
        own_wet,
    ]
    nsums = len(surface)
    values[...] = jnp.zeros(values.shape, f32)
    for place in range(nsums):
        values[:, place, :] = surface[place]
    table[...] = jnp.zeros(table.shape, f32)
    links = weights.shape[0]
    blocks = width // LANES
    tile_copy.wait()

    for row in range(rows):
        held = values[row]
        for k in range(links):
            shares = held * weights[k, row : row + 1, :]
            upper = shares.astype(jnp.bfloat16)
            lower = (shares - upper.astype(f32)).astype(jnp.bfloat16)
            both = jnp.concatenate([upper, lower], axis=0)
            for b in range(blocks):
                cols = slice(b * LANES, (b + 1) * LANES)
                found = jnp.dot(
                    both[:, cols],
                    hot[(k * blocks + b) * rows + row],
                    preferred_element_type=f32,
                )
                target = tile[k, b, row]
                table[target] = table[target] + found
    for place in range(nsums):
        total = table[:, place, :] + table[:, TILE + place, :]
        south, middle, north = total[:TILE], total[TILE : 2 * TILE], total[2 * TILE :]
        sums_mid[place] = middle
        sums_a[place] = jnp.where(even, north, south)
        sums_b[place] = jnp.where(even, south, north)


LEVELS_AT_ONCE = 6


def run_levels(first, count, temp, halo, limits, speeds, ends, light, state, out, done=None):
    levels, rows, width = temp.shape
    own_counts = state[3]
    step = math.gcd(count, LEVELS_AT_ONCE)

    def falls(level):
        beneath = temp[jnp.minimum(level + 1, levels - 1)]
        return jnp.where((level + 1).astype(f32) < own_counts, beneath - temp[level], 0.0)

    def group(at, down_before):
        for inner in range(step):
            level = first + at * step + inner
            own = temp[level]
            lateral = level_tendency(
                level,
                own,
                halo[level],
                ends[0],
                ends[1, :rows],
                [limits[place] for place in range(4)],
                [speeds[place] for place in range(4)],
            )
            down = falls(level)
            out[at * step + inner] = level_update(
                level, own, lateral, down, down_before, own_counts, light[1], light[0]
            )
            down_before = down
        if done is not None:
            done(at, step)
        return down_before

    start = falls(jnp.int32(first - 1)) if first else jnp.zeros((rows, width), f32)
    lax.fori_loop(0, count // step, group, start)


def upper_body(count, temp, halo_near, limits, speeds, ends, light, state, got_b, out, halo):
    even = lax.rem(lax.axis_index("lat"), 2) == 0
    near = near_lanes(temp.shape[2])
    for level in range(temp.shape[0]):
        rows = unpack_rows(jnp.logical_not(even), got_b[level // 4], level)
        halo[level] = jnp.where(near, halo_near[level], rows)
    run_levels(0, count, temp, halo, limits, speeds, ends, light, state, out)


def lower_body(
    first,
    temp,
    halo,
    limits,
    speeds,
    ends,
    light,
    state,
    upper,
    height,
    zonal,
    merid,
    mid,
    got_a,
    got_b,
    flags,
    out_height,
    out_zonal,
    out_merid,
    out,
    out_surface,
    lower,
    surface,
    sems,
    level_sems,
):
    open_sea = (1 - flags[...]).astype(f32)
    nsurf = surface.shape[0]
    area = mid[nsurf] + got_a[nsurf] + got_b[nsurf]
    scale = open_sea / jnp.maximum(area, area_floor)
    for place in range(nsurf):
        surface[place] = (mid[place] + got_a[place] + got_b[place]) * scale
    pairs = [
        (surface, out_surface),
        (upper, out.at[pl.ds(0, first)]),
        (height, out_height),
        (zonal, out_zonal),
        (merid, out_merid),
    ]
    copies = [
        pltpu.make_async_copy(source, target, sems.at[place])
        for place, (source, target) in enumerate(pairs)
    ]
    for copy in copies:
        copy.start()
    count = temp.shape[0] - first

    def level_copy(at, step):
        return pltpu.make_async_copy(
            lower.at[pl.ds(at * step, step)],
            out.at[pl.ds(first + at * step, step)],
            level_sems.at[at],
        )

    run_levels(
        first,
        count,
        temp,
        halo,
        limits,
        speeds,
        ends,
        light,
        state,
        lower,
        lambda at, step: level_copy(at, step).start(),
    )
    step = math.gcd(count, LEVELS_AT_ONCE)
    for at in range(count // step):
        level_copy(at, step).wait()
    for copy in copies:
        copy.wait()


def shards(
    free_elevation,
    zonal_volume_carriage,
    meridional_volume_carriage,
    thermal_field,
    flooded_strata_number,
    aerial_exchanges,
    aerial_terrain_flags,
    donor_tile_number,
    donor_point_number,
    pairing_coefficients,
):
    levels, rows, width = thermal_field.shape
    nflux, band_rows, lanes = aerial_exchanges.shape
    links, _, blocks = donor_tile_number.shape
    assert rows == 2 * TILE and band_rows == TILE and lanes == LANES
    assert 2 * levels <= LANES and lax.axis_size("lon") % 2 == 0
    nsums = 5
    fields = 4 + 2 * links
    flux_at = fields // 2
    temp_at = flux_at + (nflux + 1) // 2
    groups = pl.cdiv(levels, 4)
    tile_lines = jnp.swapaxes(donor_tile_number, 1, 2)
    edge_a, own, state, points, weights, flags, temp = call(
        load_body,
        [
            shape(temp_at + groups, TILE, width),
            shape(nflux + 2, TILE, LANES),
            shape(4, rows, width),
            shape(links, rows, width, dtype=i32),
            shape(links, rows, width),
            shape(band_rows, lanes, dtype=i32),
            shape(levels, rows, width),
        ],
        (
            free_elevation,
            zonal_volume_carriage,
            meridional_volume_carriage,
            flooded_strata_number,
            donor_point_number,
            tile_lines,
            pairing_coefficients,
            aerial_exchanges,
            aerial_terrain_flags,
            thermal_field,
        ),
        "load",
        1.5,
        scratch=[
            pltpu.VMEM((rows, width), i32),
            pltpu.VMEM((links, blocks, rows), i32),
            pltpu.VMEM((nflux, band_rows, lanes), f32),
            pltpu.SemaphoreType.DMA((10,)),
        ],
        hbm=range(10),
    )
    got_a = swap(edge_a, "lat", 0, False)
    draft_b, temp_b, edges = call(
        pack_second_body,
        [
            shape(temp_at + 4, TILE, width),
            shape(groups, TILE, width),
            shape(2, rows, LANES),
        ],
        (own, state, points, weights, temp),
        "pack_b",
        0.3,
    )
    (edge_b,) = call(
        functools.partial(pack_flux_body, flux_at),
        [shape(temp_at + 4, TILE, width)],
        (draft_b, got_a),
        "pack_b_flux",
        0.02,
        aliases={0: 0},
    )
    got_b = swap(edge_b, "lat", 1, False)
    (temp_b,) = call(
        pass_body, [shape(groups, TILE, width)], (temp_b, edge_b), "pass_temp", LATE, aliases={0: 0}
    )
    got_temp_b = swap(temp_b, "lat", 1, False)
    (edge_c,) = call(
        functools.partial(pack_third_body, flux_at),
        [shape(len(HALO_FLUXES), TILE, LANES)],
        (got_b,),
        "pack_c",
        0.02,
    )
    got_c = swap(edge_c, "lat", 0, False)
    draft_ext, light = call(
        functools.partial(forcing_body, flux_at),
        [shape(7, 3 * TILE, width), shape(2, rows, width)],
        (got_a, got_b, own, state, points, weights),
        "forcing",
        0.4,
    )
    halo_near, edges_near = call(
        functools.partial(unpack_first_body, temp_at),
        [shape(levels, TILE, width), shape(2, TILE, LANES)],
        (got_a,),
        "unpack_a",
        0.2,
    )
    ext, send_a, send_b, edges_halo = call(
        functools.partial(forcing_halo_body, flux_at),
        [
            shape(7, 3 * TILE, width),
            shape(2, 3 * TILE, LANES),
            shape(2, 3 * TILE, LANES),
            shape(2, TILE, LANES),
        ],
        (draft_ext, got_a, got_b, got_c, own, edges, edges_near),
        "forcing_halo",
        0.3,
        aliases={0: 0},
    )
    lon_b = swap(send_b, "lon", 1, True)
    (send_a,) = call(
        pass_body, [shape(2, 3 * TILE, LANES)], (send_a, send_b), "pass_lon", LATE, aliases={0: 0}
    )
    lon_a = swap(send_a, "lon", 0, True)
    (hot,) = call(
        hot_body,
        [shape(links * blocks * rows, LANES, LANES, dtype=jnp.bfloat16)],
        (points,),
        "hot",
        2.5,
    )
    (
        advanced_elevation,
        transport_x_next,
        transport_y_next,
        limits,
        speeds,
        ends,
        sums_a,
        sums_b,
        sums_mid,
    ) = call(
        functools.partial(subcycle_body, levels),
        [shape(rows, width)] * 3
        + [shape(4, 3 * TILE, width), shape(4, rows, width), shape(2, 3 * TILE, LANES)]
        + [shape(nsums, TILE, LANES)] * 3,
        (
            ext,
            light,
            edges,
            edges_halo,
            lon_a,
            lon_b,
            temp,
            halo_near,
            got_b,
            hot,
            weights,
            tile_lines,
        ),
        "subcycles",
        2.6,
        scratch=[
            pltpu.VMEM((rows, TILE, width), f32),
            pltpu.VMEM((3 * TILE, 2 * TILE, LANES), f32),
            pltpu.SMEM((links, blocks, rows), i32),
            pltpu.SemaphoreType.DMA(()),
        ],
        hbm=(11,),
    )
    back_b = swap(sums_b, "lat", 1, False)
    (sums_a,) = call(
        pass_body, [shape(nsums, TILE, LANES)], (sums_a, sums_b), "pass_sums", LATE, aliases={0: 0}
    )
    back_a = swap(sums_a, "lat", 0, False)
    first = levels // 10 * 6
    tracer = (temp, halo_near, limits, speeds, ends, light, state)
    upper, halo = call(
        functools.partial(upper_body, first),
        [shape(first, rows, width), shape(levels, TILE, width)],
        tracer + (got_temp_b,),
        "tracer_upper",
        2.3,
        aliases={1: 1},
    )
    tracer = (temp, halo, limits, speeds, ends, light, state)
    return call(
        functools.partial(lower_body, first),
        [
            pltpu.HBM((rows, width), f32),
            pltpu.HBM((rows, width), f32),
            pltpu.HBM((rows, width), f32),
            pltpu.HBM((levels, rows, width), f32),
            pltpu.HBM((nsums - 1, band_rows, lanes), f32),
        ],
        tracer
        + (
            upper,
            advanced_elevation,
            transport_x_next,
            transport_y_next,
            sums_mid,
            back_a,
            back_b,
            flags,
        ),
        "tracer_lower",
        2.4,
        scratch=[
            pltpu.VMEM((levels - first, rows, width), f32),
            pltpu.VMEM((nsums - 1, band_rows, lanes), f32),
            pltpu.SemaphoreType.DMA((5,)),
            pltpu.SemaphoreType.DMA((levels - first,)),
        ],
    )


def solution(mesh):
    flat = P("lat", "lon")
    deep = P(None, "lat", "lon")
    return jax.shard_map(
        shards,
        mesh=mesh,
        in_specs=(flat, flat, flat, deep, flat, deep, flat, deep, deep, deep),
        out_specs=(flat, flat, flat, deep, deep),
        check_vma=False,
    )
```

```python
import functools
import math

import jax
import jax.numpy as jnp
from jax import lax
from jax.experimental import pallas as pl
from jax.experimental.pallas import tpu as pltpu
from jax.sharding import PartitionSpec as P

SUBS = 3

grav_step = 0.6
height_step = 0.6
wind_step = 0.5
fresh_step = 0.5
mixing_fourth = 0.02
advect_coef = 0.1
diapycnal_diffusion = 0.2
heat_gain = 0.3
light_gain = 0.3
light_decay = 8.0
depth_floor = 0.25
area_floor = 1.0

TILE = 8
LANES = 128
HALF = TILE // 2

f32 = jnp.float32
i32 = jnp.int32

LATE = 4.0
FLOPS_PER_US = 1150000000


def swap_pairs(count, first, periodic):
    pairs = []
    for low in range(first, count, 2):
        high = low + 1
        if high == count:
            if not periodic:
                continue
            high = 0
        pairs += [(low, high), (high, low)]
    return pairs


def swap(array, axis, first, periodic):
    return lax.ppermute(array, axis, swap_pairs(lax.axis_size(axis), first, periodic))


def lane_ids(rows, width=LANES):
    return lax.broadcasted_iota(i32, (rows, width), 1)


def row_ids(rows, width=LANES):
    return lax.broadcasted_iota(i32, (rows, width), 0)


def roll_rows(array, by):
    by = by % array.shape[0]
    return pltpu.roll(array, by, 0) if by else array


def roll_lanes(array, by):
    by = by % array.shape[1]
    return pltpu.roll(array, by, 1) if by else array


def call(body, outs, ins, name, took, aliases=None, scratch=(), hbm=()):
    specs = [
        pl.BlockSpec(memory_space=pltpu.HBM if place in hbm else pltpu.VMEM)
        for place in range(len(ins))
    ]
    ins = [
        pltpu.with_memory_space_constraint(leaf, pltpu.HBM) if place in hbm else leaf
        for place, leaf in enumerate(ins)
    ]
    return pl.pallas_call(
        body,
        out_shape=outs,
        in_specs=specs,
        out_specs=[pl.BlockSpec(memory_space=leaf.memory_space) for leaf in outs],
        scratch_shapes=list(scratch),
        input_output_aliases=aliases or {},
        compiler_params=pltpu.CompilerParams(vmem_limit_bytes=24 * 1024 * 1024),
        cost_estimate=pl.CostEstimate(
            flops=int(took * FLOPS_PER_US), bytes_accessed=1024, transcendentals=0
        ),
        name=name,
    )(*ins)


def shape(*dims, dtype=f32):
    return pltpu.VMEM(dims, dtype)


def write_edge(top, fields, out_ref):
    sub = row_ids(TILE, out_ref.shape[2])
    mine = (sub >= HALF) == top
    for place in range(len(fields) // 2):
        first = jnp.where(top, fields[2 * place][TILE:], fields[2 * place][:TILE])
        second = jnp.where(top, fields[2 * place + 1][TILE:], fields[2 * place + 1][:TILE])
        out_ref[place] = jnp.where(mine, first, roll_rows(second, HALF))


def write_planes(planes, out_ref, at):
    planes = planes + [planes[-1]] * (len(planes) % 2)
    for place in range(len(planes) // 2):
        out_ref[at + place] = jnp.concatenate(planes[2 * place : 2 * place + 2], axis=1)


def flux_planes(top, own):
    nflux = own.shape[0] - 2
    return [jnp.where(top, own[nflux + 1], own[nflux])] + [own[plane] for plane in range(nflux)]


def write_temp_edge(top, temp_ref, out_ref, at):
    levels, _, width = temp_ref.shape
    sub = row_ids(TILE, width)
    for group in range(pl.cdiv(levels, 4)):
        packed = jnp.zeros((TILE, width), f32)
        for spot in range(min(4, levels - 4 * group)):
            level = 4 * group + spot
            low = roll_rows(temp_ref[level, :TILE, :], 2 * spot)
            high = roll_rows(temp_ref[level, TILE:, :], 2 * spot + 2)
            packed = jnp.where(sub // 2 == spot, jnp.where(top, high, low), packed)
        out_ref[at + group] = packed


def goes_north(first):
    return (lax.rem(lax.axis_index("lat"), 2) == 0) == (first == 0)


def edge_fields(state, points, weights):
    links = points.shape[0]
    fields = [state[place] for place in range(4)]
    fields += [points[k].astype(f32) for k in range(links)]
    fields += [weights[k] for k in range(links)]
    return fields


def load_body(
    height,
    zonal,
    merid,
    counts,
    points,
    tile,
    weights,
    flux,
    flags,
    temp,
    edge,
    own,
    state_out,
    points_out,
    weights_out,
    flags_out,
    temp_out,
    counts_in,
    tile_in,
    flux_in,
    sems,
):
    pairs = [
        (flux, flux_in),
        (flags, flags_out),
        (tile, tile_in),
        (counts, counts_in),
        (height, state_out.at[0]),
        (zonal, state_out.at[1]),
        (merid, state_out.at[2]),
        (points, points_out),
        (weights, weights_out),
        (temp, temp_out),
    ]
    copies = [
        pltpu.make_async_copy(source, target, sems.at[place])
        for place, (source, target) in enumerate(pairs)
    ]
    for copy in copies:
        copy.start()
    for copy in copies[:-1]:
        copy.wait()
    state_out[3] = counts_in[...].astype(f32)
    links, blocks, rows = tile.shape
    open_sea = (1 - flags_out[...]).astype(f32)
    masked = [flux_in[plane] * open_sea for plane in range(flux.shape[0])]
    lane = lane_ids(rows)
    diagonal = row_ids(rows, rows) == lane_ids(rows, rows)
    tiles = jnp.zeros((rows, LANES), f32)
    for k in range(links):
        for b in range(blocks):
            line = jnp.broadcast_to(tile_in[k, b : b + 1, :].astype(f32), (rows, rows))
            upright = jnp.sum(jnp.where(diagonal, line, 0.0), axis=1, keepdims=True)
            tiles = jnp.where(lane == k * blocks + b, upright, tiles)
    for plane, values in enumerate(masked):
        own[plane] = values
    own[len(masked)] = tiles[:TILE]
    own[len(masked) + 1] = tiles[TILE:]
    top = goes_north(0)
    fields = edge_fields(state_out, points_out, weights_out)
    write_edge(top, fields, edge)
    planes = flux_planes(top, own)
    at = len(fields) // 2
    write_planes(planes, edge, at)
    copies[-1].wait()
    write_temp_edge(top, temp_out, edge, at + (len(planes) + 1) // 2)


def pack_second_body(own, state, points, weights, temp, draft, temp_edge, edges):
    top = goes_north(1)
    fields = edge_fields(state, points, weights)
    write_edge(top, fields, draft)
    planes = flux_planes(top, own)
    at = len(fields) // 2
    write_planes(planes, draft, at)
    levels, rows, _ = temp.shape
    columns = edge_columns([temp[level] for level in range(levels)], rows)
    for place in range(2):
        edges[place] = columns[place]
    both = jnp.concatenate(columns, axis=1)
    draft[at + (len(planes) + 1) // 2] = jnp.where(top, both[TILE:], both[:TILE])
    write_temp_edge(top, temp, temp_edge, 0)


def pack_flux_body(flux_at, draft, received, out):
    far = [spot_of(received, flux_at, 1 + plane) for plane in HALO_FLUXES]
    write_planes(far, out, out.shape[0] - (len(far) + 1) // 2)


def edge_columns(fields, rows):
    lane = lane_ids(rows)
    high = jnp.zeros((rows, LANES), f32)
    low = jnp.zeros((rows, LANES), f32)
    for level, field in enumerate(fields):
        ends = jnp.where(lane < HALF, field[:, :LANES], field[:, -LANES:])
        turned = roll_lanes(ends, 2 * level + 2)
        high = jnp.where(lane // 2 == level, turned, high)
        low = jnp.where(lane // 2 == (level + 1) % (LANES // 2), turned, low)
    return roll_lanes(low, -2), high


HALO_FLUXES = (0, 1, 4)


def pass_body(first, second, out):
    out[0] = first[0]


def pack_third_body(flux_at, received, out):
    for place, plane in enumerate(HALO_FLUXES):
        out[place] = spot_of(received, flux_at, 1 + plane)


def unpack_rows(top, packed, level):
    spot = level % 4
    return jnp.where(top, roll_rows(packed, -2 * spot), roll_rows(packed, 6 - 2 * spot))


def near_lanes(width):
    return (row_ids(TILE, width) < HALF) == (lax.rem(lax.axis_index("lat"), 2) == 0)


def unpack_near_body(temp_at, got_a, halo, edges):
    levels = halo.shape[0]
    even = lax.rem(lax.axis_index("lat"), 2) == 0
    fields = []
    for level in range(levels):
        rows = unpack_rows(even, got_a[temp_at + level // 4], level)
        halo[level] = rows
        fields.append(rows)
    for place, columns in enumerate(edge_columns(fields, TILE)):
        edges[place] = columns


def pick(array, rows):
    return jnp.take_along_axis(array, rows, axis=0, mode="promise_in_bounds")


def pick_lane(array, lanes):
    return jnp.take_along_axis(array, lanes, axis=1, mode="promise_in_bounds")


def spot_of(array, flux_at, place):
    return array[flux_at + place // 2, :, (place % 2) * LANES : (place % 2 + 1) * LANES]


def by_side(even, one, two):
    return jnp.where(even, one, two), jnp.where(even, two, one)


def row_numbers(numbers, column):
    number = jnp.broadcast_to(numbers[:, column : column + 1].astype(i32), (TILE, LANES))
    return number & (TILE - 1), lax.shift_right_logical(number, 3)


FORCING_AT = {0: 4, 1: 5, 4: 6}


def forcing_body(flux_at, got_a, got_b, own, state, points, weights, ext, light):
    even = lax.rem(lax.axis_index("lat"), 2) == 0
    links, rows, width = points.shape
    blocks = width // LANES
    nflux = own.shape[0] - 2
    ext[:4, :rows, :] = state[...]
    north, south = [], []
    for plane in range(nflux):
        one, two = spot_of(got_a, flux_at, 1 + plane), spot_of(got_b, flux_at, 1 + plane)
        high, low = by_side(even, one, two)
        north.append(high)
        south.append(low)
    mid = [own[plane] for plane in range(nflux)]
    for row_tile in range(rows // TILE):
        here = slice(row_tile * TILE, (row_tile + 1) * TILE)
        for b in range(blocks):
            cols = slice(b * LANES, (b + 1) * LANES)
            totals = [jnp.zeros((TILE, LANES), f32) for _ in range(nflux)]
            for k in range(links):
                within, band = row_numbers(own[nflux + row_tile], k * blocks + b)
                lanes = points[k, here, cols]
                weight = weights[k, here, cols]
                for plane in range(nflux):
                    value = jnp.where(
                        band == 0,
                        pick(south[plane], within),
                        jnp.where(band == 1, pick(mid[plane], within), pick(north[plane], within)),
                    )
                    totals[plane] = totals[plane] + weight * pick_lane(value, lanes)
            for plane in range(nflux):
                if plane in FORCING_AT:
                    ext[FORCING_AT[plane], here, cols] = totals[plane]
                else:
                    light[plane - 2, here, cols] = totals[plane]


def forcing_halo_body(
    flux_at,
    draft,
    got_a,
    got_b,
    got_c,
    own,
    edges,
    edges_near,
    ext,
    send_a,
    send_b,
    edges_halo,
):
    even = lax.rem(lax.axis_index("lat"), 2) == 0
    rows, width = 2 * TILE, ext.shape[2]
    blocks = width // LANES
    links = flux_at - 2
    sub = row_ids(TILE, width)
    halos = []
    for place in range(flux_at):
        north, south = by_side(even, got_a[place], got_b[place])
        halos.append(jnp.where(sub < HALF, north, south))
        halos.append(roll_rows(jnp.where(sub < HALF, south, north), HALF))
    for place in range(4):
        ext[place, rows:, :] = halos[place]
    tables = {}
    far_at = got_b.shape[0] - (len(HALO_FLUXES) + 1) // 2
    for place, plane in enumerate(HALO_FLUXES):
        one, two = spot_of(got_a, flux_at, 1 + plane), spot_of(got_b, flux_at, 1 + plane)
        north, south = by_side(even, one, two)
        far_north, far_south = by_side(even, got_c[place], spot_of(got_b, far_at, place))
        tables[plane] = [far_south, south, own[plane], north, far_north]
    sub_one = row_ids(TILE)
    north, south = by_side(even, spot_of(got_a, flux_at, 0), spot_of(got_b, flux_at, 0))
    numbers = jnp.where(sub_one < HALF, north, south)
    for b in range(blocks):
        cols = slice(b * LANES, (b + 1) * LANES)
        totals = {plane: jnp.zeros((TILE, LANES), f32) for plane in HALO_FLUXES}
        for k in range(links):
            within, band = row_numbers(numbers, k * blocks + b)
            band = band + jnp.where(sub_one < HALF, 2, 0)
            lanes = halos[4 + k][:, cols].astype(i32)
            weight = halos[4 + links + k][:, cols]
            for plane in HALO_FLUXES:
                value = pick(tables[plane][0], within)
                for at in range(1, 5):
                    value = jnp.where(band == at, pick(tables[plane][at], within), value)
                totals[plane] = totals[plane] + weight * pick_lane(value, lanes)
        for plane in HALO_FLUXES:
            ext[FORCING_AT[plane], rows:, cols] = totals[plane]

    lane = lane_ids(3 * TILE)
    to_west = jnp.zeros((3 * TILE, LANES), f32)
    to_east = jnp.zeros((3 * TILE, LANES), f32)
    for place in range(ext.shape[0]):
        low = roll_lanes(ext[place, :, :LANES], 3 * place)
        high = roll_lanes(ext[place, :, width - LANES :], -3 * place)
        to_west = jnp.where((lane >= 3 * place) & (lane < 3 * place + 3), low, to_west)
        edge = LANES - 3 * place
        to_east = jnp.where((lane >= edge - 3) & (lane < edge), high, to_east)
    near = near_lanes(LANES)
    for place in range(2):
        edges_halo[place] = jnp.where(near, edges_near[place], spot_of(got_b, far_at - 1, place))
    lon_even = lax.rem(lax.axis_index("lon"), 2) == 0
    send_a[0] = jnp.where(lon_even, to_east, to_west)
    send_b[0] = jnp.where(lon_even, to_west, to_east)
    for part, columns in ((slice(0, rows), edges), (slice(rows, rows + TILE), edges_halo)):
        send_a[1, part, :] = jnp.where(lon_even, columns[1], columns[0])
        send_b[1, part, :] = jnp.where(lon_even, columns[0], columns[1])


def column_depth(counts, levels):
    scale = 1.0 / (2.0 * levels)
    return counts * scale + counts * (counts - 1.0) * (scale / levels)


def sideways(array, ends):
    rows, width = array.shape
    lane = lane_ids(rows)
    parts = [array[:, at : at + LANES] for at in range(0, width, LANES)]
    right = [roll_lanes(part, -1) for part in parts] + [ends]
    left = [ends] + [roll_lanes(part, 1) for part in parts]
    east = [jnp.where(lane == LANES - 1, b, a) for a, b in zip(right, right[1:])]
    west = [jnp.where(lane == 0, a, b) for a, b in zip(left, left[1:])]
    return jnp.concatenate(east, axis=1), jnp.concatenate(west, axis=1)


def turned(ends, level):
    return pltpu.roll(ends, lax.rem(2 * LANES - 2 * level, LANES), 1)


LEVELS_AT_ONCE = 6


def before_body(ext, light, temp, halo_near, got_b, base, laps, halo):
    levels, rows, width = temp.shape
    counts = ext[3]
    own_counts = counts[:rows]
    lane = lane_ids(3 * TILE, width)
    limit_east = jnp.where(lane == width - 1, 0.0, jnp.minimum(counts, roll_lanes(counts, -1)))
    limit_north = jnp.minimum(counts, roll_rows(counts, -1))
    limits = (limit_east, roll_lanes(limit_east, 1), limit_north, roll_rows(limit_north, 1))
    step = math.gcd(levels, LEVELS_AT_ONCE)
    odd = lax.rem(lax.axis_index("lat"), 2) == 1
    near = near_lanes(width)
    for level in range(levels):
        rows_far = unpack_rows(odd, got_b[level // 4], level)
        halo[level] = jnp.where(near, halo_near[level], rows_far)

    def group(at, down_before):
        for inner in range(step):
            level = at * step + inner
            level_f = level.astype(f32)
            own = temp[level]
            whole = jnp.concatenate([own, halo[level]], axis=0)
            east, west = sideways(whole, whole[:, :LANES])
            lap = -4.0 * whole
            for around, limit in zip(
                (east, west, roll_rows(whole, -1), roll_rows(whole, 1)), limits
            ):
                lap = lap + jnp.where(level_f < limit, around, whole)
            laps[level] = lap
            beneath = temp[jnp.minimum(level + 1, levels - 1)]
            down = jnp.where(level_f + 1.0 < own_counts, beneath - own, 0.0)
            absorb = jnp.exp(jnp.full(own.shape, -1.0 / light_decay, f32) * level_f)
            absorb = absorb * (light_gain * (1.0 - math.exp(-1.0 / light_decay)))
            source = absorb * light[1] + jnp.where(level == 0, heat_gain, 0.0) * light[0]
            change = diapycnal_diffusion * (down - down_before) + source
            base[level] = own + jnp.where(level_f < own_counts, change, 0.0)
            down_before = down
        return down_before

    lax.fori_loop(0, levels // step, group, jnp.zeros((rows, width), f32))


def finish_level(level, own, halo_level, base, lap, ends, limits, speeds):
    rows, width = own.shape
    level_f = level.astype(f32)
    lane = lane_ids(3 * TILE)
    side = turned(ends[2], level)
    parts = [lap[:, at : at + LANES] for at in range(0, width, LANES)]
    parts[0] = parts[0] + jnp.where(lane == 0, side, 0.0)
    parts[-1] = parts[-1] + jnp.where(lane == LANES - 1, side, 0.0)
    lap = jnp.concatenate(parts, axis=1)
    whole = jnp.concatenate([own, halo_level], axis=0)
    own_lap = lap[:rows]
    around_temp = sideways(own, turned(ends[0][:rows], level))
    around_temp += (roll_rows(whole, -1)[:rows], roll_rows(whole, 1)[:rows])
    around_lap = sideways(own_lap, turned(ends[1][:rows], level))
    around_lap += (roll_rows(lap, -1)[:rows], roll_rows(lap, 1)[:rows])
    change = jnp.zeros((rows, width), f32)
    for place, limit in enumerate(limits):
        moved = mixing_fourth * (own_lap - around_lap[place])
        moved = moved - speeds[place] * (around_temp[place] + own)
        change = change + jnp.where(level_f < limit, moved, 0.0)
    return base + change


def hot_body(points, hot):
    links, rows, width = points.shape
    blocks = width // LANES
    cells = row_ids(LANES).astype(f32).astype(jnp.bfloat16)
    one, none = jnp.bfloat16(1.0), jnp.bfloat16(0.0)
    for k in range(links):
        for b in range(blocks):
            for row in range(rows):
                line = points[k, row : row + 1, b * LANES : (b + 1) * LANES]
                line = jnp.broadcast_to(line.astype(f32), (2 * TILE, LANES)).astype(jnp.bfloat16)
                line = jnp.concatenate([line] * (LANES // (2 * TILE)), axis=0)
                hot[(k * blocks + b) * rows + row] = jnp.transpose(jnp.where(line == cells, one, none))


def subcycle_body(
    levels,
    ext,
    edges_own,
    edges_halo,
    got_a,
    got_b,
    temp,
    halo,
    base,
    laps,
    hot,
    weights,
    tile_hbm,
    out_height,
    out_zonal,
    out_merid,
    limits_out,
    speeds_out,
    ends_out,
    sums_a,
    sums_b,
    sums_mid,
    values,
    table,
    tile,
    tile_sem,
):
    tile_copy = pltpu.make_async_copy(tile_hbm, tile, tile_sem)
    tile_copy.start()
    edges = [
        jnp.concatenate([edges_own[place], edges_halo[place]], axis=0) for place in range(2)
    ]
    width = ext.shape[2]
    rows = temp.shape[1]
    lon_even = lax.rem(lax.axis_index("lon"), 2) == 0
    even = lax.rem(lax.axis_index("lat"), 2) == 0
    lane = lane_ids(3 * TILE)
    from_east = [jnp.where(lon_even, got_a[place], got_b[place]) for place in range(2)]
    from_west = [jnp.where(lon_even, got_b[place], got_a[place]) for place in range(2)]
    planes = []
    for place in range(ext.shape[0]):
        third = jnp.where(
            lane < 3,
            roll_lanes(from_east[0], -3 * place),
            jnp.where(lane >= LANES - 3, roll_lanes(from_west[0], 3 * place), 0.0),
        )
        planes.append(jnp.concatenate([ext[place], third], axis=1))
    height, zonal, merid, counts, wind_east, wind_north, fresh = planes

    def east_of(array):
        return roll_lanes(array, -1)

    def west_of(array):
        return roll_lanes(array, 1)

    def north_of(array):
        return roll_rows(array, -1)

    def south_of(array):
        return roll_rows(array, 1)

    depth = column_depth(counts, levels)
    wet = (counts > 0.5).astype(f32)
    east_wet = wet * east_of(wet)
    north_wet = wet * north_of(wet)
    east_depth = jnp.minimum(depth, east_of(depth))
    north_depth = jnp.minimum(depth, north_of(depth))
    east_pull = grav_step * east_depth
    north_pull = grav_step * north_depth
    wind_east = wind_step * wind_east
    wind_north = wind_step * wind_north
    fresh = fresh_step * fresh
    for _ in range(SUBS):
        zonal = east_wet * (zonal - east_pull * (east_of(height) - height) + wind_east)
        merid = north_wet * (merid - north_pull * (north_of(height) - height) + wind_north)
        spread = zonal - west_of(zonal) + merid - south_of(merid)
        height = height + wet * (fresh - height_step * spread)
    out_height[...] = height[:rows, :width]
    out_zonal[...] = zonal[:rows, :width]
    out_merid[...] = merid[:rows, :width]

    limit_east = jnp.minimum(counts, east_of(counts))
    limit_north = jnp.minimum(counts, north_of(counts))
    limit_west, limit_south = west_of(limit_east), south_of(limit_north)
    limits = [
        limit[:rows, :width] for limit in (limit_east, limit_west, limit_north, limit_south)
    ]
    speed_east = 0.5 * advect_coef * zonal / jnp.maximum(east_depth, depth_floor)
    speed_north = 0.5 * advect_coef * merid / jnp.maximum(north_depth, depth_floor)
    speeds = [
        speed[:rows, :width]
        for speed in (speed_east, -west_of(speed_east), speed_north, -south_of(speed_north))
    ]
    for place in range(4):
        limits_out[place] = limits[place]
        speeds_out[place] = speeds[place]

    lane_level = (lane // 2).astype(f32)
    odd_lane = (lane & 1) == 1
    far_east, far_west = from_east[1], from_west[1]

    def column(limit, at):
        return jnp.broadcast_to(limit[:, at : at + 1], (3 * TILE, LANES))

    def edge_lap(center, toward_east, toward_west, at, at_west):
        total = -4.0 * center
        for around, limit in (
            (toward_east, column(limit_east, at)),
            (toward_west, column(limit_east, at_west)),
            (north_of(center), column(limit_north, at)),
            (south_of(center), column(limit_south, at)),
        ):
            total = total + jnp.where(lane_level < limit, around, center)
        return total

    total_lanes = width + LANES
    lap_west = edge_lap(
        far_west,
        roll_lanes(edges[0], 1),
        roll_lanes(far_west, 1),
        total_lanes - 1,
        total_lanes - 2,
    )
    lap_east = edge_lap(
        far_east, roll_lanes(far_east, -1), roll_lanes(edges[1], -1), width, width - 1
    )
    side_west = far_west - roll_lanes(edges[0], 1)
    side_west = jnp.where(lane_level < column(limit_east, total_lanes - 1), side_west, 0.0)
    side_east = far_east - roll_lanes(edges[1], -1)
    side_east = jnp.where(lane_level < column(limit_east, width - 1), side_east, 0.0)
    ends = []
    for west, east in ((far_west, far_east), (lap_west, lap_east), (side_west, side_east)):
        ends.append(roll_lanes(jnp.where(odd_lane, west, east), -1))
    for place in range(3):
        ends_out[place] = ends[place]

    zero = jnp.zeros((), i32)
    top = finish_level(zero, temp[0], halo[0], base[0], laps[0], ends, limits, speeds)
    own_wet = wet[:rows, :width]
    thick = jnp.maximum(depth[:rows, :width], depth_floor)
    surface = [
        top * own_wet,
        height[:rows, :width] * own_wet,
        zonal[:rows, :width] / thick * own_wet,
        merid[:rows, :width] / thick * own_wet,
        own_wet,
    ]
    nsums = len(surface)
    values[...] = jnp.zeros(values.shape, f32)
    for place in range(nsums):
        values[:, place, :] = surface[place]
    table[...] = jnp.zeros(table.shape, f32)
    links = weights.shape[0]
    blocks = width // LANES
    tile_copy.wait()

    for row in range(rows):
        held = values[row]
        for k in range(links):
            shares = held * weights[k, row : row + 1, :]
            upper = shares.astype(jnp.bfloat16)
            lower = (shares - upper.astype(f32)).astype(jnp.bfloat16)
            both = jnp.concatenate([upper, lower], axis=0)
            for b in range(blocks):
                cols = slice(b * LANES, (b + 1) * LANES)
                found = jnp.dot(
                    both[:, cols],
                    hot[(k * blocks + b) * rows + row],
                    preferred_element_type=f32,
                )
                target = tile[k, b, row]
                table[target] = table[target] + found
    for place in range(nsums):
        total = table[:, place, :] + table[:, TILE + place, :]
        south, middle, north = total[:TILE], total[TILE : 2 * TILE], total[2 * TILE :]
        sums_mid[place] = middle
        sums_a[place] = jnp.where(even, north, south)
        sums_b[place] = jnp.where(even, south, north)


def run_levels(first, count, temp, halo, base, laps, limits, speeds, ends, out, done=None):
    step = math.gcd(count, LEVELS_AT_ONCE)

    def group(at, carry):
        for inner in range(step):
            level = first + at * step + inner
            out[at * step + inner] = finish_level(
                level,
                temp[level],
                halo[level],
                base[level],
                laps[level],
                [ends[place] for place in range(3)],
                [limits[place] for place in range(4)],
                [speeds[place] for place in range(4)],
            )
        if done is not None:
            done(at, step)
        return carry

    lax.fori_loop(0, count // step, group, 0)


def upper_body(count, temp, halo, base, laps, limits, speeds, ends, out):
    run_levels(0, count, temp, halo, base, laps, limits, speeds, ends, out)


def lower_body(
    first,
    temp,
    halo,
    base,
    laps,
    limits,
    speeds,
    ends,
    upper,
    height,
    zonal,
    merid,
    mid,
    got_a,
    got_b,
    flags,
    out_height,
    out_zonal,
    out_merid,
    out,
    out_surface,
    lower,
    surface,
    sems,
    level_sems,
):
    open_sea = (1 - flags[...]).astype(f32)
    nsurf = surface.shape[0]
    area = mid[nsurf] + got_a[nsurf] + got_b[nsurf]
    scale = open_sea / jnp.maximum(area, area_floor)
    for place in range(nsurf):
        surface[place] = (mid[place] + got_a[place] + got_b[place]) * scale
    pairs = [
        (surface, out_surface),
        (upper, out.at[pl.ds(0, first)]),
        (height, out_height),
        (zonal, out_zonal),
        (merid, out_merid),
    ]
    copies = [
        pltpu.make_async_copy(source, target, sems.at[place])
        for place, (source, target) in enumerate(pairs)
    ]
    for copy in copies:
        copy.start()
    count = temp.shape[0] - first

    def level_copy(at, step):
        return pltpu.make_async_copy(
            lower.at[pl.ds(at * step, step)],
            out.at[pl.ds(first + at * step, step)],
            level_sems.at[at],
        )

    run_levels(
        first,
        count,
        temp,
        halo,
        base,
        laps,
        limits,
        speeds,
        ends,
        lower,
        lambda at, step: level_copy(at, step).start(),
    )
    step = math.gcd(count, LEVELS_AT_ONCE)
    for at in range(count // step):
        level_copy(at, step).wait()
    for copy in copies:
        copy.wait()


def shards(
    free_elevation,
    zonal_volume_carriage,
    meridional_volume_carriage,
    thermal_field,
    flooded_strata_number,
    aerial_exchanges,
    aerial_terrain_flags,
    donor_tile_number,
    donor_point_number,
    pairing_coefficients,
):
    levels, rows, width = thermal_field.shape
    nflux, band_rows, lanes = aerial_exchanges.shape
    links, _, blocks = donor_tile_number.shape
    assert rows == 2 * TILE and band_rows == TILE and lanes == LANES
    assert 2 * levels <= LANES and lax.axis_size("lon") % 2 == 0
    nsums = 5
    fields = 4 + 2 * links
    flux_at = fields // 2
    flux_tiles = (nflux + 2) // 2
    temp_at = flux_at + flux_tiles
    groups = pl.cdiv(levels, 4)
    tile_lines = jnp.swapaxes(donor_tile_number, 1, 2)
    edge_a, own, state, points, weights, flags, temp = call(
        load_body,
        [
            shape(temp_at + groups, TILE, width),
            shape(nflux + 2, TILE, LANES),
            shape(4, rows, width),
            shape(links, rows, width, dtype=i32),
            shape(links, rows, width),
            shape(band_rows, lanes, dtype=i32),
            shape(levels, rows, width),
        ],
        (
            free_elevation,
            zonal_volume_carriage,
            meridional_volume_carriage,
            flooded_strata_number,
            donor_point_number,
            tile_lines,
            pairing_coefficients,
            aerial_exchanges,
            aerial_terrain_flags,
            thermal_field,
        ),
        "load",
        1.6,
        scratch=[
            pltpu.VMEM((rows, width), i32),
            pltpu.VMEM((links, blocks, rows), i32),
            pltpu.VMEM((nflux, band_rows, lanes), f32),
            pltpu.SemaphoreType.DMA((10,)),
        ],
        hbm=range(10),
    )
    got_a = swap(edge_a, "lat", 0, False)
    edge_tiles = temp_at + 1 + (len(HALO_FLUXES) + 1) // 2
    draft_b, temp_b, edges = call(
        pack_second_body,
        [
            shape(edge_tiles, TILE, width),
            shape(groups, TILE, width),
            shape(2, rows, LANES),
        ],
        (own, state, points, weights, temp),
        "pack_b",
        0.3,
    )
    (edge_b,) = call(
        functools.partial(pack_flux_body, flux_at),
        [shape(edge_tiles, TILE, width)],
        (draft_b, got_a),
        "pack_flux",
        0.0,
        aliases={0: 0},
    )
    got_b = swap(edge_b, "lat", 1, False)
    (temp_b,) = call(
        pass_body, [shape(groups, TILE, width)], (temp_b, edge_b), "pass_temp", LATE, aliases={0: 0}
    )
    got_temp_b = swap(temp_b, "lat", 1, False)
    (edge_c,) = call(
        functools.partial(pack_third_body, flux_at),
        [shape(len(HALO_FLUXES), TILE, LANES)],
        (got_b,),
        "pack_c",
        LATE,
    )
    got_c = swap(edge_c, "lat", 0, False)
    draft_ext, light = call(
        functools.partial(forcing_body, flux_at),
        [shape(7, 3 * TILE, width), shape(2, rows, width)],
        (got_a, got_b, own, state, points, weights),
        "forcing",
        0.4,
    )
    halo_near, edges_near = call(
        functools.partial(unpack_near_body, temp_at),
        [shape(levels, TILE, width), shape(2, TILE, LANES)],
        (got_a,),
        "unpack_a",
        0.0,
    )
    ext, send_a, send_b, edges_halo = call(
        functools.partial(forcing_halo_body, flux_at),
        [
            shape(7, 3 * TILE, width),
            shape(2, 3 * TILE, LANES),
            shape(2, 3 * TILE, LANES),
            shape(2, TILE, LANES),
        ],
        (draft_ext, got_a, got_b, got_c, own, edges, edges_near),
        "forcing_halo",
        0.3,
        aliases={0: 0},
    )
    lon_b = swap(send_b, "lon", 1, True)
    (send_a,) = call(
        pass_body, [shape(2, 3 * TILE, LANES)], (send_a, send_b), "pass_lon", LATE, aliases={0: 0}
    )
    lon_a = swap(send_a, "lon", 0, True)
    (hot,) = call(
        hot_body,
        [shape(links * blocks * rows, LANES, LANES, dtype=jnp.bfloat16)],
        (points,),
        "hot",
        0.0,
    )
    base, laps, halo = call(
        before_body,
        [
            shape(levels, rows, width),
            shape(levels, 3 * TILE, width),
            shape(levels, TILE, width),
        ],
        (ext, light, temp, halo_near, got_temp_b),
        "before",
        0.0,
        aliases={3: 2},
    )
    (
        advanced_elevation,
        transport_x_next,
        transport_y_next,
        limits,
        speeds,
        ends,
        sums_a,
        sums_b,
        sums_mid,
    ) = call(
        functools.partial(subcycle_body, levels),
        [shape(rows, width)] * 3
        + [shape(4, rows, width), shape(4, rows, width), shape(3, 3 * TILE, LANES)]
        + [shape(nsums, TILE, LANES)] * 3,
        (
            ext,
            edges,
            edges_halo,
            lon_a,
            lon_b,
            temp,
            halo,
            base,
            laps,
            hot,
            weights,
            tile_lines,
        ),
        "subcycles",
        2.6,
        scratch=[
            pltpu.VMEM((rows, TILE, width), f32),
            pltpu.VMEM((3 * TILE, 2 * TILE, LANES), f32),
            pltpu.SMEM((links, blocks, rows), i32),
            pltpu.SemaphoreType.DMA(()),
        ],
        hbm=(11,),
    )
    back_b = swap(sums_b, "lat", 1, False)
    (sums_a,) = call(
        pass_body, [shape(nsums, TILE, LANES)], (sums_a, sums_b), "pass_sums", LATE, aliases={0: 0}
    )
    back_a = swap(sums_a, "lat", 0, False)
    first = levels // 10 * 9
    tracer = (temp, halo, base, laps, limits, speeds, ends)
    (upper,) = call(
        functools.partial(upper_body, first),
        [shape(first, rows, width)],
        tracer,
        "tracer_upper",
        2.3,
    )
    return call(
        functools.partial(lower_body, first),
        [
            pltpu.HBM((rows, width), f32),
            pltpu.HBM((rows, width), f32),
            pltpu.HBM((rows, width), f32),
            pltpu.HBM((levels, rows, width), f32),
            pltpu.HBM((nsums - 1, band_rows, lanes), f32),
        ],
        tracer
        + (
            upper,
            advanced_elevation,
            transport_x_next,
            transport_y_next,
            sums_mid,
            back_a,
            back_b,
            flags,
        ),
        "tracer_lower",
        2.4,
        scratch=[
            pltpu.VMEM((levels - first, rows, width), f32),
            pltpu.VMEM((nsums - 1, band_rows, lanes), f32),
            pltpu.SemaphoreType.DMA((5,)),
            pltpu.SemaphoreType.DMA((levels - first,)),
        ],
    )


def solution(mesh):
    flat = P("lat", "lon")
    deep = P(None, "lat", "lon")
    return jax.shard_map(
        shards,
        mesh=mesh,
        in_specs=(flat, flat, flat, deep, flat, deep, flat, deep, deep, deep),
        out_specs=(flat, flat, flat, deep, deep),
        check_vma=False,
    )
```

```python
import functools
import math

import jax
import jax.numpy as jnp
from jax import lax
from jax.experimental import pallas as pl
from jax.experimental.pallas import tpu as pltpu
from jax.sharding import PartitionSpec as P

SUBS = 3

grav_step = 0.6
height_step = 0.6
wind_step = 0.5
fresh_step = 0.5
mixing_fourth = 0.02
advect_coef = 0.1
diapycnal_diffusion = 0.2
heat_gain = 0.3
light_gain = 0.3
light_decay = 8.0
depth_floor = 0.25
area_floor = 1.0

TILE = 8
LANES = 128
HALF = TILE // 2

f32 = jnp.float32
i32 = jnp.int32

LATE = 4.0
FLOPS_PER_US = 1150000000


def swap_pairs(count, first, periodic):
    pairs = []
    for low in range(first, count, 2):
        high = low + 1
        if high == count:
            if not periodic:
                continue
            high = 0
        pairs += [(low, high), (high, low)]
    return pairs


def swap(array, axis, first, periodic):
    return lax.ppermute(array, axis, swap_pairs(lax.axis_size(axis), first, periodic))


def lane_ids(rows, width=LANES):
    return lax.broadcasted_iota(i32, (rows, width), 1)


def row_ids(rows, width=LANES):
    return lax.broadcasted_iota(i32, (rows, width), 0)


def roll_rows(array, by):
    by = by % array.shape[0]
    return pltpu.roll(array, by, 0) if by else array


def roll_lanes(array, by):
    by = by % array.shape[1]
    return pltpu.roll(array, by, 1) if by else array


def call(body, outs, ins, name, took, aliases=None, scratch=(), hbm=()):
    specs = [
        pl.BlockSpec(memory_space=pltpu.HBM if place in hbm else pltpu.VMEM)
        for place in range(len(ins))
    ]
    ins = [
        pltpu.with_memory_space_constraint(leaf, pltpu.HBM) if place in hbm else leaf
        for place, leaf in enumerate(ins)
    ]
    return pl.pallas_call(
        body,
        out_shape=outs,
        in_specs=specs,
        out_specs=[pl.BlockSpec(memory_space=leaf.memory_space) for leaf in outs],
        scratch_shapes=list(scratch),
        input_output_aliases=aliases or {},
        compiler_params=pltpu.CompilerParams(vmem_limit_bytes=24 * 1024 * 1024),
        cost_estimate=pl.CostEstimate(
            flops=int(took * FLOPS_PER_US), bytes_accessed=1024, transcendentals=0
        ),
        name=name,
    )(*ins)


def shape(*dims, dtype=f32):
    return pltpu.VMEM(dims, dtype)


def write_edge(top, fields, out_ref):
    sub = row_ids(TILE, out_ref.shape[2])
    mine = (sub >= HALF) == top
    for place in range(len(fields) // 2):
        first = jnp.where(top, fields[2 * place][TILE:], fields[2 * place][:TILE])
        second = jnp.where(top, fields[2 * place + 1][TILE:], fields[2 * place + 1][:TILE])
        out_ref[place] = jnp.where(mine, first, roll_rows(second, HALF))


def write_planes(planes, out_ref, at):
    planes = planes + [planes[-1]] * (len(planes) % 2)
    for place in range(len(planes) // 2):
        out_ref[at + place] = jnp.concatenate(planes[2 * place : 2 * place + 2], axis=1)


def flux_planes(top, own):
    nflux = own.shape[0] - 2
    return [jnp.where(top, own[nflux + 1], own[nflux])] + [own[plane] for plane in range(nflux)]


def write_temp_edge(top, temp_ref, out_ref, at):
    levels, _, width = temp_ref.shape
    sub = row_ids(TILE, width)
    for group in range(pl.cdiv(levels, 4)):
        packed = jnp.zeros((TILE, width), f32)
        for spot in range(min(4, levels - 4 * group)):
            level = 4 * group + spot
            low = roll_rows(temp_ref[level, :TILE, :], 2 * spot)
            high = roll_rows(temp_ref[level, TILE:, :], 2 * spot + 2)
            packed = jnp.where(sub // 2 == spot, jnp.where(top, high, low), packed)
        out_ref[at + group] = packed


def goes_north(first):
    return (lax.rem(lax.axis_index("lat"), 2) == 0) == (first == 0)


def edge_fields(state, points, weights):
    links = points.shape[0]
    fields = [state[place] for place in range(4)]
    fields += [points[k].astype(f32) for k in range(links)]
    fields += [weights[k] for k in range(links)]
    return fields


def load_body(
    height,
    zonal,
    merid,
    counts,
    points,
    tile,
    weights,
    flux,
    flags,
    temp,
    edge,
    own,
    state_out,
    points_out,
    weights_out,
    flags_out,
    temp_out,
    counts_in,
    tile_in,
    flux_in,
    sems,
):
    pairs = [
        (flux, flux_in),
        (flags, flags_out),
        (tile, tile_in),
        (counts, counts_in),
        (height, state_out.at[0]),
        (zonal, state_out.at[1]),
        (merid, state_out.at[2]),
        (points, points_out),
        (weights, weights_out),
        (temp, temp_out),
    ]
    copies = [
        pltpu.make_async_copy(source, target, sems.at[place])
        for place, (source, target) in enumerate(pairs)
    ]
    for copy in copies:
        copy.start()
    for copy in copies[:-1]:
        copy.wait()
    state_out[3] = counts_in[...].astype(f32)
    links, blocks, rows = tile.shape
    open_sea = (1 - flags_out[...]).astype(f32)
    masked = [flux_in[plane] * open_sea for plane in range(flux.shape[0])]
    lane = lane_ids(rows)
    diagonal = row_ids(rows, rows) == lane_ids(rows, rows)
    tiles = jnp.zeros((rows, LANES), f32)
    for k in range(links):
        for b in range(blocks):
            line = jnp.broadcast_to(tile_in[k, b : b + 1, :].astype(f32), (rows, rows))
            upright = jnp.sum(jnp.where(diagonal, line, 0.0), axis=1, keepdims=True)
            tiles = jnp.where(lane == k * blocks + b, upright, tiles)
    for plane, values in enumerate(masked):
        own[plane] = values
    own[len(masked)] = tiles[:TILE]
    own[len(masked) + 1] = tiles[TILE:]
    top = goes_north(0)
    fields = edge_fields(state_out, points_out, weights_out)
    write_edge(top, fields, edge)
    planes = flux_planes(top, own)
    at = len(fields) // 2
    write_planes(planes, edge, at)
    copies[-1].wait()
    write_temp_edge(top, temp_out, edge, at + (len(planes) + 1) // 2)


def pack_second_body(own, state, points, weights, temp, draft, temp_edge, edges):
    top = goes_north(1)
    fields = edge_fields(state, points, weights)
    write_edge(top, fields, draft)
    planes = flux_planes(top, own)
    at = len(fields) // 2
    write_planes(planes, draft, at)
    levels, rows, _ = temp.shape
    columns = edge_columns([temp[level] for level in range(levels)], rows)
    for place in range(2):
        edges[place] = columns[place]
    both = jnp.concatenate(columns, axis=1)
    draft[at + (len(planes) + 1) // 2] = jnp.where(top, both[TILE:], both[:TILE])
    write_temp_edge(top, temp, temp_edge, 0)


def pack_flux_body(flux_at, draft, received, out):
    far = [spot_of(received, flux_at, 1 + plane) for plane in HALO_FLUXES]
    write_planes(far, out, out.shape[0] - (len(far) + 1) // 2)


def edge_columns(fields, rows):
    lane = lane_ids(rows)
    high = jnp.zeros((rows, LANES), f32)
    low = jnp.zeros((rows, LANES), f32)
    for level, field in enumerate(fields):
        ends = jnp.where(lane < HALF, field[:, :LANES], field[:, -LANES:])
        turned = roll_lanes(ends, 2 * level + 2)
        high = jnp.where(lane // 2 == level, turned, high)
        low = jnp.where(lane // 2 == (level + 1) % (LANES // 2), turned, low)
    return roll_lanes(low, -2), high


HALO_FLUXES = (0, 1, 4)


def pass_body(first, second, out):
    out[0] = first[0]


def pack_third_body(flux_at, received, out):
    for place, plane in enumerate(HALO_FLUXES):
        out[place] = spot_of(received, flux_at, 1 + plane)


def unpack_rows(top, packed, level):
    spot = level % 4
    return jnp.where(top, roll_rows(packed, -2 * spot), roll_rows(packed, 6 - 2 * spot))


def near_lanes(width):
    return (row_ids(TILE, width) < HALF) == (lax.rem(lax.axis_index("lat"), 2) == 0)


def unpack_near_body(temp_at, got_a, halo, edges):
    levels = halo.shape[0]
    even = lax.rem(lax.axis_index("lat"), 2) == 0
    fields = []
    for level in range(levels):
        rows = unpack_rows(even, got_a[temp_at + level // 4], level)
        halo[level] = rows
        fields.append(rows)
    for place, columns in enumerate(edge_columns(fields, TILE)):
        edges[place] = columns


def pick(array, rows):
    return jnp.take_along_axis(array, rows, axis=0, mode="promise_in_bounds")


def pick_lane(array, lanes):
    return jnp.take_along_axis(array, lanes, axis=1, mode="promise_in_bounds")


def spot_of(array, flux_at, place):
    return array[flux_at + place // 2, :, (place % 2) * LANES : (place % 2 + 1) * LANES]


def by_side(even, one, two):
    return jnp.where(even, one, two), jnp.where(even, two, one)


def row_numbers(numbers, column):
    number = jnp.broadcast_to(numbers[:, column : column + 1].astype(i32), (TILE, LANES))
    return number & (TILE - 1), lax.shift_right_logical(number, 3)


FORCING_AT = {0: 4, 1: 5, 4: 6}


def forcing_body(flux_at, got_a, got_b, own, state, points, weights, ext, light):
    even = lax.rem(lax.axis_index("lat"), 2) == 0
    links, rows, width = points.shape
    blocks = width // LANES
    nflux = own.shape[0] - 2
    ext[:4, :rows, :] = state[...]
    north, south = [], []
    for plane in range(nflux):
        one, two = spot_of(got_a, flux_at, 1 + plane), spot_of(got_b, flux_at, 1 + plane)
        high, low = by_side(even, one, two)
        north.append(high)
        south.append(low)
    mid = [own[plane] for plane in range(nflux)]
    for row_tile in range(rows // TILE):
        here = slice(row_tile * TILE, (row_tile + 1) * TILE)
        for b in range(blocks):
            cols = slice(b * LANES, (b + 1) * LANES)
            totals = [jnp.zeros((TILE, LANES), f32) for _ in range(nflux)]
            for k in range(links):
                within, band = row_numbers(own[nflux + row_tile], k * blocks + b)
                lanes = points[k, here, cols]
                weight = weights[k, here, cols]
                for plane in range(nflux):
                    value = jnp.where(
                        band == 0,
                        pick(south[plane], within),
                        jnp.where(band == 1, pick(mid[plane], within), pick(north[plane], within)),
                    )
                    totals[plane] = totals[plane] + weight * pick_lane(value, lanes)
            for plane in range(nflux):
                if plane in FORCING_AT:
                    ext[FORCING_AT[plane], here, cols] = totals[plane]
                else:
                    light[plane - 2, here, cols] = totals[plane]


def forcing_halo_body(
    flux_at,
    draft,
    got_a,
    got_b,
    got_c,
    own,
    edges,
    edges_near,
    ext,
    send_a,
    send_b,
    edges_halo,
):
    even = lax.rem(lax.axis_index("lat"), 2) == 0
    rows, width = 2 * TILE, ext.shape[2]
    blocks = width // LANES
    links = flux_at - 2
    sub = row_ids(TILE, width)
    halos = []
    for place in range(flux_at):
        north, south = by_side(even, got_a[place], got_b[place])
        halos.append(jnp.where(sub < HALF, north, south))
        halos.append(roll_rows(jnp.where(sub < HALF, south, north), HALF))
    for place in range(4):
        ext[place, rows:, :] = halos[place]
    tables = {}
    far_at = got_b.shape[0] - (len(HALO_FLUXES) + 1) // 2
    for place, plane in enumerate(HALO_FLUXES):
        one, two = spot_of(got_a, flux_at, 1 + plane), spot_of(got_b, flux_at, 1 + plane)
        north, south = by_side(even, one, two)
        far_north, far_south = by_side(even, got_c[place], spot_of(got_b, far_at, place))
        tables[plane] = [far_south, south, own[plane], north, far_north]
    sub_one = row_ids(TILE)
    north, south = by_side(even, spot_of(got_a, flux_at, 0), spot_of(got_b, flux_at, 0))
    numbers = jnp.where(sub_one < HALF, north, south)
    for b in range(blocks):
        cols = slice(b * LANES, (b + 1) * LANES)
        totals = {plane: jnp.zeros((TILE, LANES), f32) for plane in HALO_FLUXES}
        for k in range(links):
            within, band = row_numbers(numbers, k * blocks + b)
            band = band + jnp.where(sub_one < HALF, 2, 0)
            lanes = halos[4 + k][:, cols].astype(i32)
            weight = halos[4 + links + k][:, cols]
            for plane in HALO_FLUXES:
                value = pick(tables[plane][0], within)
                for at in range(1, 5):
                    value = jnp.where(band == at, pick(tables[plane][at], within), value)
                totals[plane] = totals[plane] + weight * pick_lane(value, lanes)
        for plane in HALO_FLUXES:
            ext[FORCING_AT[plane], rows:, cols] = totals[plane]

    lane = lane_ids(3 * TILE)
    to_west = jnp.zeros((3 * TILE, LANES), f32)
    to_east = jnp.zeros((3 * TILE, LANES), f32)
    for place in range(ext.shape[0]):
        low = roll_lanes(ext[place, :, :LANES], 3 * place)
        high = roll_lanes(ext[place, :, width - LANES :], -3 * place)
        to_west = jnp.where((lane >= 3 * place) & (lane < 3 * place + 3), low, to_west)
        edge = LANES - 3 * place
        to_east = jnp.where((lane >= edge - 3) & (lane < edge), high, to_east)
    near = near_lanes(LANES)
    for place in range(2):
        edges_halo[place] = jnp.where(near, edges_near[place], spot_of(got_b, far_at - 1, place))
    lon_even = lax.rem(lax.axis_index("lon"), 2) == 0
    send_a[0] = jnp.where(lon_even, to_east, to_west)
    send_b[0] = jnp.where(lon_even, to_west, to_east)
    for part, columns in ((slice(0, rows), edges), (slice(rows, rows + TILE), edges_halo)):
        send_a[1, part, :] = jnp.where(lon_even, columns[1], columns[0])
        send_b[1, part, :] = jnp.where(lon_even, columns[0], columns[1])


def column_depth(counts, levels):
    scale = 1.0 / (2.0 * levels)
    return counts * scale + counts * (counts - 1.0) * (scale / levels)


def sideways(array, ends):
    rows, width = array.shape
    lane = lane_ids(rows)
    parts = [array[:, at : at + LANES] for at in range(0, width, LANES)]
    right = [roll_lanes(part, -1) for part in parts] + [ends]
    left = [ends] + [roll_lanes(part, 1) for part in parts]
    east = [jnp.where(lane == LANES - 1, b, a) for a, b in zip(right, right[1:])]
    west = [jnp.where(lane == 0, a, b) for a, b in zip(left, left[1:])]
    return jnp.concatenate(east, axis=1), jnp.concatenate(west, axis=1)


def turned(ends, level):
    return pltpu.roll(ends, lax.rem(2 * LANES - 2 * level, LANES), 1)


LEVELS_AT_ONCE = 6


def before_body(ext, light, temp, halo_near, got_b, base, laps, halo):
    levels, rows, width = temp.shape
    counts = ext[3]
    own_counts = counts[:rows]
    lane = lane_ids(3 * TILE, width)
    limit_east = jnp.where(lane == width - 1, 0.0, jnp.minimum(counts, roll_lanes(counts, -1)))
    limit_north = jnp.minimum(counts, roll_rows(counts, -1))
    limits = (limit_east, roll_lanes(limit_east, 1), limit_north, roll_rows(limit_north, 1))
    step = math.gcd(levels, LEVELS_AT_ONCE)
    odd = lax.rem(lax.axis_index("lat"), 2) == 1
    near = near_lanes(width)
    for level in range(levels):
        rows_far = unpack_rows(odd, got_b[level // 4], level)
        halo[level] = jnp.where(near, halo_near[level], rows_far)

    def group(at, down_before):
        for inner in range(step):
            level = at * step + inner
            level_f = level.astype(f32)
            own = temp[level]
            whole = jnp.concatenate([own, halo[level]], axis=0)
            east, west = sideways(whole, whole[:, :LANES])
            lap = -4.0 * whole
            for around, limit in zip(
                (east, west, roll_rows(whole, -1), roll_rows(whole, 1)), limits
            ):
                lap = lap + jnp.where(level_f < limit, around, whole)
            laps[level] = lap
            beneath = temp[jnp.minimum(level + 1, levels - 1)]
            down = jnp.where(level_f + 1.0 < own_counts, beneath - own, 0.0)
            absorb = jnp.exp(jnp.full(own.shape, -1.0 / light_decay, f32) * level_f)
            absorb = absorb * (light_gain * (1.0 - math.exp(-1.0 / light_decay)))
            source = absorb * light[1] + jnp.where(level == 0, heat_gain, 0.0) * light[0]
            change = diapycnal_diffusion * (down - down_before) + source
            base[level] = own + jnp.where(level_f < own_counts, change, 0.0)
            down_before = down
        return down_before

    lax.fori_loop(0, levels // step, group, jnp.zeros((rows, width), f32))


def finish_level(level, own, halo_level, base, lap, ends, limits, speeds):
    rows, width = own.shape
    level_f = level.astype(f32)
    lane = lane_ids(3 * TILE)
    side = turned(ends[2], level)
    parts = [lap[:, at : at + LANES] for at in range(0, width, LANES)]
    parts[0] = parts[0] + jnp.where(lane == 0, side, 0.0)
    parts[-1] = parts[-1] + jnp.where(lane == LANES - 1, side, 0.0)
    lap = jnp.concatenate(parts, axis=1)
    whole = jnp.concatenate([own, halo_level], axis=0)
    own_lap = lap[:rows]
    around_temp = sideways(own, turned(ends[0][:rows], level))
    around_temp += (roll_rows(whole, -1)[:rows], roll_rows(whole, 1)[:rows])
    around_lap = sideways(own_lap, turned(ends[1][:rows], level))
    around_lap += (roll_rows(lap, -1)[:rows], roll_rows(lap, 1)[:rows])
    change = jnp.zeros((rows, width), f32)
    for place, limit in enumerate(limits):
        moved = mixing_fourth * (own_lap - around_lap[place])
        moved = moved - speeds[place] * (around_temp[place] + own)
        change = change + jnp.where(level_f < limit, moved, 0.0)
    return base + change


def hot_body(points, hot):
    links, rows, width = points.shape
    blocks = width // LANES
    cells = row_ids(LANES).astype(f32).astype(jnp.bfloat16)
    one, none = jnp.bfloat16(1.0), jnp.bfloat16(0.0)
    for k in range(links):
        for b in range(blocks):
            for row in range(rows):
                line = points[k, row : row + 1, b * LANES : (b + 1) * LANES]
                line = jnp.broadcast_to(line.astype(f32), (2 * TILE, LANES)).astype(jnp.bfloat16)
                line = jnp.concatenate([line] * (LANES // (2 * TILE)), axis=0)
                hot[k * rows + row, :, b * LANES : (b + 1) * LANES] = jnp.transpose(
                    jnp.where(line == cells, one, none)
                )


def subcycle_body(
    levels,
    ext,
    edges_own,
    edges_halo,
    got_a,
    got_b,
    temp,
    halo,
    base,
    laps,
    hot,
    weights,
    tile_hbm,
    out_height,
    out_zonal,
    out_merid,
    limits_out,
    speeds_out,
    ends_out,
    sums_a,
    sums_b,
    sums_mid,
    whole,
    values,
    table,
    tile,
    tile_sem,
):
    tile_copy = pltpu.make_async_copy(tile_hbm, tile, tile_sem)
    tile_copy.start()
    edges = [
        jnp.concatenate([edges_own[place], edges_halo[place]], axis=0) for place in range(2)
    ]
    width = ext.shape[2]
    rows = temp.shape[1]
    lon_even = lax.rem(lax.axis_index("lon"), 2) == 0
    even = lax.rem(lax.axis_index("lat"), 2) == 0
    lane = lane_ids(3 * TILE)
    from_east = [jnp.where(lon_even, got_a[place], got_b[place]) for place in range(2)]
    from_west = [jnp.where(lon_even, got_b[place], got_a[place]) for place in range(2)]
    planes = []
    for place in range(ext.shape[0]):
        third = jnp.where(
            lane < 3,
            roll_lanes(from_east[0], -3 * place),
            jnp.where(lane >= LANES - 3, roll_lanes(from_west[0], 3 * place), 0.0),
        )
        planes.append(jnp.concatenate([ext[place], third], axis=1))
    height, zonal, merid, counts, wind_east, wind_north, fresh = planes

    def east_of(array):
        return roll_lanes(array, -1)

    def west_of(array):
        return roll_lanes(array, 1)

    def north_of(array):
        return roll_rows(array, -1)

    def south_of(array):
        return roll_rows(array, 1)

    depth = column_depth(counts, levels)
    wet = (counts > 0.5).astype(f32)
    east_wet = wet * east_of(wet)
    north_wet = wet * north_of(wet)
    east_depth = jnp.minimum(depth, east_of(depth))
    north_depth = jnp.minimum(depth, north_of(depth))
    east_pull = grav_step * east_depth
    north_pull = grav_step * north_depth
    wind_east = wind_step * wind_east
    wind_north = wind_step * wind_north
    fresh = fresh_step * fresh
    for _ in range(SUBS):
        zonal = east_wet * (zonal - east_pull * (east_of(height) - height) + wind_east)
        merid = north_wet * (merid - north_pull * (north_of(height) - height) + wind_north)
        spread = zonal - west_of(zonal) + merid - south_of(merid)
        height = height + wet * (fresh - height_step * spread)
    out_height[...] = height[:rows, :width]
    out_zonal[...] = zonal[:rows, :width]
    out_merid[...] = merid[:rows, :width]

    limit_east = jnp.minimum(counts, east_of(counts))
    limit_north = jnp.minimum(counts, north_of(counts))
    limit_west, limit_south = west_of(limit_east), south_of(limit_north)
    limits = [
        limit[:rows, :width] for limit in (limit_east, limit_west, limit_north, limit_south)
    ]
    speed_east = 0.5 * advect_coef * zonal / jnp.maximum(east_depth, depth_floor)
    speed_north = 0.5 * advect_coef * merid / jnp.maximum(north_depth, depth_floor)
    speeds = [
        speed[:rows, :width]
        for speed in (speed_east, -west_of(speed_east), speed_north, -south_of(speed_north))
    ]
    for place in range(4):
        limits_out[place] = limits[place]
        speeds_out[place] = speeds[place]

    lane_level = (lane // 2).astype(f32)
    odd_lane = (lane & 1) == 1
    far_east, far_west = from_east[1], from_west[1]

    def column(limit, at):
        return jnp.broadcast_to(limit[:, at : at + 1], (3 * TILE, LANES))

    def edge_lap(center, toward_east, toward_west, at, at_west):
        total = -4.0 * center
        for around, limit in (
            (toward_east, column(limit_east, at)),
            (toward_west, column(limit_east, at_west)),
            (north_of(center), column(limit_north, at)),
            (south_of(center), column(limit_south, at)),
        ):
            total = total + jnp.where(lane_level < limit, around, center)
        return total

    total_lanes = width + LANES
    lap_west = edge_lap(
        far_west,
        roll_lanes(edges[0], 1),
        roll_lanes(far_west, 1),
        total_lanes - 1,
        total_lanes - 2,
    )
    lap_east = edge_lap(
        far_east, roll_lanes(far_east, -1), roll_lanes(edges[1], -1), width, width - 1
    )
    side_west = far_west - roll_lanes(edges[0], 1)
    side_west = jnp.where(lane_level < column(limit_east, total_lanes - 1), side_west, 0.0)
    side_east = far_east - roll_lanes(edges[1], -1)
    side_east = jnp.where(lane_level < column(limit_east, width - 1), side_east, 0.0)
    ends = []
    for west, east in ((far_west, far_east), (lap_west, lap_east), (side_west, side_east)):
        ends.append(roll_lanes(jnp.where(odd_lane, west, east), -1))
    for place in range(3):
        ends_out[place] = ends[place]

    zero = jnp.zeros((), i32)
    top = finish_level(zero, temp[0], halo[0], base[0], laps[0], ends, limits, speeds)
    own_wet = wet[:rows, :width]
    thick = jnp.maximum(depth[:rows, :width], depth_floor)
    surface = [
        top * own_wet,
        height[:rows, :width] * own_wet,
        zonal[:rows, :width] / thick * own_wet,
        merid[:rows, :width] / thick * own_wet,
        own_wet,
    ]
    nsums = len(surface)
    values[...] = jnp.zeros(values.shape, f32)
    for place in range(nsums):
        values[:, place, :] = surface[place]
    table[...] = jnp.zeros(table.shape, f32)
    links = weights.shape[0]
    blocks = width // LANES
    tile_copy.wait()

    for row in range(rows):
        held = values[row]
        for k in range(links):
            shares = held * weights[k, row : row + 1, :]
            upper = shares.astype(jnp.bfloat16)
            lower = (shares - upper.astype(f32)).astype(jnp.bfloat16)
            both = jnp.concatenate([upper, lower], axis=0)
            stacked = jnp.concatenate(
                [both[:, b * LANES : (b + 1) * LANES] for b in range(blocks)], axis=0
            )
            found = jnp.dot(stacked, hot[k * rows + row], preferred_element_type=f32)
            for b in range(blocks):
                target = tile[k, b, row]
                mine = found[b * 2 * TILE : (b + 1) * 2 * TILE, b * LANES : (b + 1) * LANES]
                table[target] = table[target] + mine
    for place in range(nsums):
        total = table[:, place, :] + table[:, TILE + place, :]
        south, middle, north = total[:TILE], total[TILE : 2 * TILE], total[2 * TILE :]
        sums_mid[place] = middle
        sums_a[place] = jnp.where(even, north, south)
        sums_b[place] = jnp.where(even, south, north)

    run_levels(
        0,
        early_groups(levels),
        temp,
        halo,
        base,
        laps,
        limits_out,
        speeds_out,
        ends_out,
        whole,
    )


def level_step(levels):
    return math.gcd(levels, LEVELS_AT_ONCE)


def early_groups(levels):
    groups = levels // level_step(levels)
    place = lax.axis_index("lat")
    inner = jnp.where(lax.rem(place, 2) == 1, groups // 5, 0)
    return jnp.where(place == 0, groups // 2, inner)


LAST_GROUPS = 2


def run_levels(start, stop, temp, halo, base, laps, limits, speeds, ends, out, done=None):
    step = level_step(temp.shape[0])

    def group(at, carry):
        for inner in range(step):
            level = jnp.int32(at * step + inner)
            out[level] = finish_level(
                level,
                temp[level],
                halo[level],
                base[level],
                laps[level],
                [ends[place] for place in range(3)],
                [limits[place] for place in range(4)],
                [speeds[place] for place in range(4)],
            )
        if done is not None:
            done(at)
        return carry

    lax.fori_loop(start, stop, group, 0)


def tracer_body(
    temp,
    halo,
    base,
    laps,
    limits,
    speeds,
    ends,
    draft,
    height,
    zonal,
    merid,
    out_height,
    out_zonal,
    out_merid,
    out,
    whole,
    sems,
    level_sems,
):
    levels = temp.shape[0]
    step = level_step(levels)
    groups = levels // step
    pairs = [(height, out_height), (zonal, out_zonal), (merid, out_merid)]
    copies = [
        pltpu.make_async_copy(source, target, sems.at[place])
        for place, (source, target) in enumerate(pairs)
    ]
    for copy in copies:
        copy.start()

    def level_copy(at):
        part = pl.ds(at * step, step)
        return pltpu.make_async_copy(whole.at[part], out.at[part], level_sems.at[at])

    early = early_groups(levels)

    def start(at, carry):
        level_copy(at).start()
        return carry

    lax.fori_loop(0, early, start, 0)
    inside = max(groups - LAST_GROUPS, 0)
    refs = (temp, halo, base, laps, limits, speeds, ends, whole)
    run_levels(early, inside, *refs, lambda at: level_copy(at).start())
    run_levels(inside, groups, *refs)
    for at in range(inside):
        level_copy(at).wait()
    for copy in copies:
        copy.wait()


def merge_body(mid, got_a, got_b, flags, whole, draft, out, out_temp, surface, sems):
    levels = whole.shape[0]
    step = level_step(levels)
    first = step * max(levels // step - LAST_GROUPS, 0)
    part = pl.ds(first, levels - first)
    rest = pltpu.make_async_copy(whole.at[part], out_temp.at[part], sems.at[0])
    rest.start()
    open_sea = (1 - flags[...]).astype(f32)
    nsurf = out.shape[0]
    area = mid[nsurf] + got_a[nsurf] + got_b[nsurf]
    scale = open_sea / jnp.maximum(area, area_floor)
    for place in range(nsurf):
        surface[place] = (mid[place] + got_a[place] + got_b[place]) * scale
    copy = pltpu.make_async_copy(surface, out, sems.at[1])
    copy.start()
    copy.wait()
    rest.wait()


def shards(
    free_elevation,
    zonal_volume_carriage,
    meridional_volume_carriage,
    thermal_field,
    flooded_strata_number,
    aerial_exchanges,
    aerial_terrain_flags,
    donor_tile_number,
    donor_point_number,
    pairing_coefficients,
):
    levels, rows, width = thermal_field.shape
    nflux, band_rows, lanes = aerial_exchanges.shape
    links, _, blocks = donor_tile_number.shape
    assert rows == 2 * TILE and band_rows == TILE and lanes == LANES
    assert 2 * levels <= LANES and lax.axis_size("lon") % 2 == 0
    nsums = 5
    fields = 4 + 2 * links
    flux_at = fields // 2
    flux_tiles = (nflux + 2) // 2
    temp_at = flux_at + flux_tiles
    groups = pl.cdiv(levels, 4)
    tile_lines = jnp.swapaxes(donor_tile_number, 1, 2)
    edge_a, own, state, points, weights, flags, temp = call(
        load_body,
        [
            shape(temp_at + groups, TILE, width),
            shape(nflux + 2, TILE, LANES),
            shape(4, rows, width),
            shape(links, rows, width, dtype=i32),
            shape(links, rows, width),
            shape(band_rows, lanes, dtype=i32),
            shape(levels, rows, width),
        ],
        (
            free_elevation,
            zonal_volume_carriage,
            meridional_volume_carriage,
            flooded_strata_number,
            donor_point_number,
            tile_lines,
            pairing_coefficients,
            aerial_exchanges,
            aerial_terrain_flags,
            thermal_field,
        ),
        "load",
        1.6,
        scratch=[
            pltpu.VMEM((rows, width), i32),
            pltpu.VMEM((links, blocks, rows), i32),
            pltpu.VMEM((nflux, band_rows, lanes), f32),
            pltpu.SemaphoreType.DMA((10,)),
        ],
        hbm=range(10),
    )
    got_a = swap(edge_a, "lat", 0, False)
    edge_tiles = temp_at + 1 + (len(HALO_FLUXES) + 1) // 2
    draft_b, temp_b, edges = call(
        pack_second_body,
        [
            shape(edge_tiles, TILE, width),
            shape(groups, TILE, width),
            shape(2, rows, LANES),
        ],
        (own, state, points, weights, temp),
        "pack_b",
        0.3,
    )
    (edge_b,) = call(
        functools.partial(pack_flux_body, flux_at),
        [shape(edge_tiles, TILE, width)],
        (draft_b, got_a),
        "pack_flux",
        0.0,
        aliases={0: 0},
    )
    got_b = swap(edge_b, "lat", 1, False)
    (temp_b,) = call(
        pass_body, [shape(groups, TILE, width)], (temp_b, edge_b), "pass_temp", LATE, aliases={0: 0}
    )
    got_temp_b = swap(temp_b, "lat", 1, False)
    (edge_c,) = call(
        functools.partial(pack_third_body, flux_at),
        [shape(len(HALO_FLUXES), TILE, LANES)],
        (got_b,),
        "pack_c",
        LATE,
    )
    got_c = swap(edge_c, "lat", 0, False)
    draft_ext, light = call(
        functools.partial(forcing_body, flux_at),
        [shape(7, 3 * TILE, width), shape(2, rows, width)],
        (got_a, got_b, own, state, points, weights),
        "forcing",
        0.4,
    )
    halo_near, edges_near = call(
        functools.partial(unpack_near_body, temp_at),
        [shape(levels, TILE, width), shape(2, TILE, LANES)],
        (got_a,),
        "unpack_a",
        0.0,
    )
    ext, send_a, send_b, edges_halo = call(
        functools.partial(forcing_halo_body, flux_at),
        [
            shape(7, 3 * TILE, width),
            shape(2, 3 * TILE, LANES),
            shape(2, 3 * TILE, LANES),
            shape(2, TILE, LANES),
        ],
        (draft_ext, got_a, got_b, got_c, own, edges, edges_near),
        "forcing_halo",
        0.3,
        aliases={0: 0},
    )
    lon_b = swap(send_b, "lon", 1, True)
    (send_a,) = call(
        pass_body, [shape(2, 3 * TILE, LANES)], (send_a, send_b), "pass_lon", LATE, aliases={0: 0}
    )
    lon_a = swap(send_a, "lon", 0, True)
    (hot,) = call(
        hot_body,
        [shape(links * rows, LANES, blocks * LANES, dtype=jnp.bfloat16)],
        (points,),
        "hot",
        0.0,
    )
    base, laps, halo = call(
        before_body,
        [
            shape(levels, rows, width),
            shape(levels, 3 * TILE, width),
            shape(levels, TILE, width),
        ],
        (ext, light, temp, halo_near, got_temp_b),
        "before",
        0.0,
        aliases={3: 2},
    )
    (
        advanced_elevation,
        transport_x_next,
        transport_y_next,
        limits,
        speeds,
        ends,
        sums_a,
        sums_b,
        sums_mid,
        draft,
    ) = call(
        functools.partial(subcycle_body, levels),
        [shape(rows, width)] * 3
        + [shape(4, rows, width), shape(4, rows, width), shape(3, 3 * TILE, LANES)]
        + [shape(nsums, TILE, LANES)] * 3
        + [shape(levels, rows, width)],
        (
            ext,
            edges,
            edges_halo,
            lon_a,
            lon_b,
            temp,
            halo,
            base,
            laps,
            hot,
            weights,
            tile_lines,
        ),
        "subcycles",
        2.6,
        scratch=[
            pltpu.VMEM((rows, TILE, width), f32),
            pltpu.VMEM((3 * TILE, 2 * TILE, LANES), f32),
            pltpu.SMEM((links, blocks, rows), i32),
            pltpu.SemaphoreType.DMA(()),
        ],
        hbm=(11,),
    )
    back_b = swap(sums_b, "lat", 1, False)
    (sums_a,) = call(
        pass_body, [shape(nsums, TILE, LANES)], (sums_a, sums_b), "pass_sums", LATE, aliases={0: 0}
    )
    back_a = swap(sums_a, "lat", 0, False)
    advanced_elevation, transport_x_next, transport_y_next, draft_field, draft = call(
        tracer_body,
        [
            pltpu.HBM((rows, width), f32),
            pltpu.HBM((rows, width), f32),
            pltpu.HBM((rows, width), f32),
            pltpu.HBM((levels, rows, width), f32),
            shape(levels, rows, width),
        ],
        (
            temp,
            halo,
            base,
            laps,
            limits,
            speeds,
            ends,
            draft,
            advanced_elevation,
            transport_x_next,
            transport_y_next,
        ),
        "tracer",
        2.5,
        aliases={7: 4},
        scratch=[
            pltpu.SemaphoreType.DMA((3,)),
            pltpu.SemaphoreType.DMA((levels // level_step(levels),)),
        ],
    )
    marine_skin_condition, advanced_thermal_field = call(
        merge_body,
        [
            pltpu.HBM((nsums - 1, band_rows, lanes), f32),
            pltpu.HBM((levels, rows, width), f32),
        ],
        (sums_mid, back_a, back_b, flags, draft, draft_field),
        "merge",
        0.1,
        aliases={5: 1},
        hbm=(5,),
        scratch=[
            pltpu.VMEM((nsums - 1, band_rows, lanes), f32),
            pltpu.SemaphoreType.DMA((2,)),
        ],
    )
    return (
        advanced_elevation,
        transport_x_next,
        transport_y_next,
        advanced_thermal_field,
        marine_skin_condition,
    )


def solution(mesh):
    flat = P("lat", "lon")
    deep = P(None, "lat", "lon")
    return jax.shard_map(
        shards,
        mesh=mesh,
        in_specs=(flat, flat, flat, deep, flat, deep, flat, deep, deep, deep),
        out_specs=(flat, flat, flat, deep, deep),
        check_vma=False,
    )
```

```python
import functools
import math

import jax
import jax.numpy as jnp
from jax import lax
from jax.experimental import pallas as pl
from jax.experimental.pallas import tpu as pltpu
from jax.sharding import PartitionSpec as P

SUBS = 3

grav_step = 0.6
height_step = 0.6
wind_step = 0.5
fresh_step = 0.5
mixing_fourth = 0.02
advect_coef = 0.1
diapycnal_diffusion = 0.2
heat_gain = 0.3
light_gain = 0.3
light_decay = 8.0
depth_floor = 0.25
area_floor = 1.0

TILE = 8
LANES = 128
HALF = TILE // 2

f32 = jnp.float32
i32 = jnp.int32

LATE = 4.0
FLOPS_PER_US = 1150000000


def swap_pairs(count, first, periodic):
    pairs = []
    for low in range(first, count, 2):
        high = low + 1
        if high == count:
            if not periodic:
                continue
            high = 0
        pairs += [(low, high), (high, low)]
    return pairs


def swap(array, axis, first, periodic):
    return lax.ppermute(array, axis, swap_pairs(lax.axis_size(axis), first, periodic))


def lane_ids(rows, width=LANES):
    return lax.broadcasted_iota(i32, (rows, width), 1)


def row_ids(rows, width=LANES):
    return lax.broadcasted_iota(i32, (rows, width), 0)


def roll_rows(array, by):
    by = by % array.shape[0]
    return pltpu.roll(array, by, 0) if by else array


def roll_lanes(array, by):
    by = by % array.shape[1]
    return pltpu.roll(array, by, 1) if by else array


def call(body, outs, ins, name, took, aliases=None, scratch=(), hbm=()):
    specs = [
        pl.BlockSpec(memory_space=pltpu.HBM if place in hbm else pltpu.VMEM)
        for place in range(len(ins))
    ]
    ins = [
        pltpu.with_memory_space_constraint(leaf, pltpu.HBM) if place in hbm else leaf
        for place, leaf in enumerate(ins)
    ]
    return pl.pallas_call(
        body,
        out_shape=outs,
        in_specs=specs,
        out_specs=[pl.BlockSpec(memory_space=leaf.memory_space) for leaf in outs],
        scratch_shapes=list(scratch),
        input_output_aliases=aliases or {},
        compiler_params=pltpu.CompilerParams(vmem_limit_bytes=12 * 1024 * 1024),
        cost_estimate=pl.CostEstimate(
            flops=int(took * FLOPS_PER_US), bytes_accessed=1024, transcendentals=0
        ),
        name=name,
    )(*ins)


def shape(*dims, dtype=f32):
    return pltpu.VMEM(dims, dtype)


def write_edge(top, fields, out_ref):
    sub = row_ids(TILE, out_ref.shape[2])
    mine = (sub >= HALF) == top
    for place in range(len(fields) // 2):
        first = jnp.where(top, fields[2 * place][TILE:], fields[2 * place][:TILE])
        second = jnp.where(top, fields[2 * place + 1][TILE:], fields[2 * place + 1][:TILE])
        out_ref[place] = jnp.where(mine, first, roll_rows(second, HALF))


def write_planes(planes, out_ref, at):
    planes = planes + [planes[-1]] * (len(planes) % 2)
    for place in range(len(planes) // 2):
        out_ref[at + place] = jnp.concatenate(planes[2 * place : 2 * place + 2], axis=1)


def flux_planes(top, own):
    nflux = own.shape[0] - 2
    return [jnp.where(top, own[nflux + 1], own[nflux])] + [own[plane] for plane in range(nflux)]


def write_temp_edge(top, temp_ref, out_ref, at):
    levels, _, width = temp_ref.shape
    sub = row_ids(TILE, width)
    for group in range(pl.cdiv(levels, 4)):
        packed = jnp.zeros((TILE, width), f32)
        for spot in range(min(4, levels - 4 * group)):
            level = 4 * group + spot
            low = roll_rows(temp_ref[level, :TILE, :], 2 * spot)
            high = roll_rows(temp_ref[level, TILE:, :], 2 * spot + 2)
            packed = jnp.where(sub // 2 == spot, jnp.where(top, high, low), packed)
        out_ref[at + group] = packed


def goes_north(first):
    return (lax.rem(lax.axis_index("lat"), 2) == 0) == (first == 0)


def edge_fields(state, points, weights):
    links = points.shape[0]
    fields = [state[place] for place in range(4)]
    fields += [points[k].astype(f32) for k in range(links)]
    fields += [weights[k] for k in range(links)]
    return fields


def load_body(
    height,
    zonal,
    merid,
    counts,
    points,
    tile,
    weights,
    flux,
    flags,
    edge,
    own,
    state_out,
    points_out,
    weights_out,
    flags_out,
    counts_in,
    tile_in,
    flux_in,
    sems,
):
    pairs = [
        (flux, flux_in),
        (flags, flags_out),
        (tile, tile_in),
        (counts, counts_in),
        (height, state_out.at[0]),
        (zonal, state_out.at[1]),
        (merid, state_out.at[2]),
        (points, points_out),
        (weights, weights_out),
    ]
    copies = [
        pltpu.make_async_copy(source, target, sems.at[place])
        for place, (source, target) in enumerate(pairs)
    ]
    for copy in copies:
        copy.start()
    for copy in copies:
        copy.wait()
    state_out[3] = counts_in[...].astype(f32)
    links, blocks, rows = tile.shape
    open_sea = (1 - flags_out[...]).astype(f32)
    masked = [flux_in[plane] * open_sea for plane in range(flux.shape[0])]
    lane = lane_ids(rows)
    diagonal = row_ids(rows, rows) == lane_ids(rows, rows)
    tiles = jnp.zeros((rows, LANES), f32)
    for k in range(links):
        for b in range(blocks):
            line = jnp.broadcast_to(tile_in[k, b : b + 1, :].astype(f32), (rows, rows))
            upright = jnp.sum(jnp.where(diagonal, line, 0.0), axis=1, keepdims=True)
            tiles = jnp.where(lane == k * blocks + b, upright, tiles)
    for plane, values in enumerate(masked):
        own[plane] = values
    own[len(masked)] = tiles[:TILE]
    own[len(masked) + 1] = tiles[TILE:]
    top = goes_north(0)
    fields = edge_fields(state_out, points_out, weights_out)
    write_edge(top, fields, edge)
    write_planes(flux_planes(top, own), edge, len(fields) // 2)


def pack_second_body(own, state, points, weights, temp, draft, edges):
    top = goes_north(1)
    fields = edge_fields(state, points, weights)
    write_edge(top, fields, draft)
    write_planes(flux_planes(top, own), draft, len(fields) // 2)
    levels, rows, _ = temp.shape
    for place, columns in enumerate(edge_columns([temp[level] for level in range(levels)], rows)):
        edges[place] = columns


def corner_plane(top, edges):
    west = jnp.where(top, edges[0, TILE:, :], edges[0, :TILE, :])
    east = jnp.where(top, edges[1, TILE:, :], edges[1, :TILE, :])
    return jnp.where((row_ids(TILE) >= HALF) == top, west, roll_rows(east, HALF))


def far_planes(flux_at, received):
    return [spot_of(received, flux_at, 1 + plane) for plane in HALO_FLUXES]


def pack_flux_body(flux_at, draft, received, edges, out):
    planes = far_planes(flux_at, received) + [corner_plane(goes_north(1), edges)]
    at = out.shape[0] - len(planes) // 2
    out[:at] = draft[:at]
    write_planes(planes, out, at)


def edge_columns(fields, rows):
    lane = lane_ids(rows)
    high = jnp.zeros((rows, LANES), f32)
    low = jnp.zeros((rows, LANES), f32)
    for level, field in enumerate(fields):
        ends = jnp.where(lane < HALF, field[:, :LANES], field[:, -LANES:])
        turned = roll_lanes(ends, 2 * level + 2)
        high = jnp.where(lane // 2 == level, turned, high)
        low = jnp.where(lane // 2 == (level + 1) % (LANES // 2), turned, low)
    return roll_lanes(low, -2), high


HALO_FLUXES = (0, 1, 4)


def pass_body(first, second, out):
    out[...] = first[...]


def pack_temp_body(first, temp, other, out):
    write_temp_edge(goes_north(first), temp, out, 0)


def pack_third_body(flux_at, received, edges, out):
    write_planes(far_planes(flux_at, received) + [corner_plane(goes_north(0), edges)], out, 0)


def unpack_rows(top, packed, level):
    spot = level % 4
    return jnp.where(top, roll_rows(packed, -2 * spot), roll_rows(packed, 6 - 2 * spot))


def near_lanes(width):
    return (row_ids(TILE, width) < HALF) == (lax.rem(lax.axis_index("lat"), 2) == 0)


def pick(array, rows):
    return jnp.take_along_axis(array, rows, axis=0, mode="promise_in_bounds")


def pick_lane(array, lanes):
    return jnp.take_along_axis(array, lanes, axis=1, mode="promise_in_bounds")


def spot_of(array, flux_at, place):
    return array[flux_at + place // 2, :, (place % 2) * LANES : (place % 2 + 1) * LANES]


def by_side(even, one, two):
    return jnp.where(even, one, two), jnp.where(even, two, one)


def row_numbers(numbers, column):
    number = jnp.broadcast_to(numbers[:, column : column + 1].astype(i32), (TILE, LANES))
    return number & (TILE - 1), lax.shift_right_logical(number, 3)


FORCING_AT = {0: 4, 1: 5, 4: 6}


def forcing_body(flux_at, got_a, got_b, own, state, points, weights, ext, light):
    even = lax.rem(lax.axis_index("lat"), 2) == 0
    links, rows, width = points.shape
    blocks = width // LANES
    nflux = own.shape[0] - 2
    ext[:4, :rows, :] = state[...]
    north, south = [], []
    for plane in range(nflux):
        one, two = spot_of(got_a, flux_at, 1 + plane), spot_of(got_b, flux_at, 1 + plane)
        high, low = by_side(even, one, two)
        north.append(high)
        south.append(low)
    mid = [own[plane] for plane in range(nflux)]
    for row_tile in range(rows // TILE):
        here = slice(row_tile * TILE, (row_tile + 1) * TILE)
        for b in range(blocks):
            cols = slice(b * LANES, (b + 1) * LANES)
            totals = [jnp.zeros((TILE, LANES), f32) for _ in range(nflux)]
            for k in range(links):
                within, band = row_numbers(own[nflux + row_tile], k * blocks + b)
                lanes = points[k, here, cols]
                weight = weights[k, here, cols]
                for plane in range(nflux):
                    value = jnp.where(
                        band == 0,
                        pick(south[plane], within),
                        jnp.where(band == 1, pick(mid[plane], within), pick(north[plane], within)),
                    )
                    totals[plane] = totals[plane] + weight * pick_lane(value, lanes)
            for plane in range(nflux):
                if plane in FORCING_AT:
                    ext[FORCING_AT[plane], here, cols] = totals[plane]
                else:
                    light[plane - 2, here, cols] = totals[plane]


def both_fields(even, near, far):
    north, south = by_side(even, near, far)
    sub = row_ids(*near.shape)
    return [
        jnp.where(sub < HALF, north, south),
        roll_rows(jnp.where(sub < HALF, south, north), HALF),
    ]


def forcing_halo_body(
    flux_at,
    draft,
    got_a,
    got_b,
    got_c,
    own,
    edges,
    ext,
    send_a,
    send_b,
    edges_halo,
):
    even = lax.rem(lax.axis_index("lat"), 2) == 0
    rows, width = 2 * TILE, ext.shape[2]
    blocks = width // LANES
    links = flux_at - 2
    halos = []
    for place in range(flux_at):
        halos += both_fields(even, got_a[place], got_b[place])
    ext[:, :rows, :] = draft[:, :rows, :]
    for place in range(4):
        ext[place, rows:, :] = halos[place]
    tables = {}
    far_at = got_b.shape[0] - (len(HALO_FLUXES) + 1) // 2
    for place, plane in enumerate(HALO_FLUXES):
        one, two = spot_of(got_a, flux_at, 1 + plane), spot_of(got_b, flux_at, 1 + plane)
        north, south = by_side(even, one, two)
        far_north, far_south = by_side(
            even, spot_of(got_c, 0, place), spot_of(got_b, far_at, place)
        )
        tables[plane] = [far_south, south, own[plane], north, far_north]
    sub_one = row_ids(TILE)
    north, south = by_side(even, spot_of(got_a, flux_at, 0), spot_of(got_b, flux_at, 0))
    numbers = jnp.where(sub_one < HALF, north, south)
    for b in range(blocks):
        cols = slice(b * LANES, (b + 1) * LANES)
        totals = {plane: jnp.zeros((TILE, LANES), f32) for plane in HALO_FLUXES}
        for k in range(links):
            within, band = row_numbers(numbers, k * blocks + b)
            band = band + jnp.where(sub_one < HALF, 2, 0)
            lanes = halos[4 + k][:, cols].astype(i32)
            weight = halos[4 + links + k][:, cols]
            for plane in HALO_FLUXES:
                value = pick(tables[plane][0], within)
                for at in range(1, 5):
                    value = jnp.where(band == at, pick(tables[plane][at], within), value)
                totals[plane] = totals[plane] + weight * pick_lane(value, lanes)
        for plane in HALO_FLUXES:
            ext[FORCING_AT[plane], rows:, cols] = totals[plane]

    lane = lane_ids(3 * TILE)
    to_west = jnp.zeros((3 * TILE, LANES), f32)
    to_east = jnp.zeros((3 * TILE, LANES), f32)
    for place in range(ext.shape[0]):
        low = roll_lanes(ext[place, :, :LANES], 3 * place)
        high = roll_lanes(ext[place, :, width - LANES :], -3 * place)
        to_west = jnp.where((lane >= 3 * place) & (lane < 3 * place + 3), low, to_west)
        edge = LANES - 3 * place
        to_east = jnp.where((lane >= edge - 3) & (lane < edge), high, to_east)
    corner = len(HALO_FLUXES)
    corners = both_fields(even, spot_of(got_c, 0, corner), spot_of(got_b, far_at, corner))
    for place in range(2):
        edges_halo[place] = corners[place]
    lon_even = lax.rem(lax.axis_index("lon"), 2) == 0
    send_a[0] = jnp.where(lon_even, to_east, to_west)
    send_b[0] = jnp.where(lon_even, to_west, to_east)
    for part, columns in ((slice(0, rows), edges), (slice(rows, rows + TILE), edges_halo)):
        send_a[1, part, :] = jnp.where(lon_even, columns[1], columns[0])
        send_b[1, part, :] = jnp.where(lon_even, columns[0], columns[1])


def column_depth(counts, levels):
    scale = 1.0 / (2.0 * levels)
    return counts * scale + counts * (counts - 1.0) * (scale / levels)


def sideways(array, ends):
    rows, width = array.shape
    lane = lane_ids(rows)
    parts = [array[:, at : at + LANES] for at in range(0, width, LANES)]
    right = [roll_lanes(part, -1) for part in parts] + [ends]
    left = [ends] + [roll_lanes(part, 1) for part in parts]
    east = [jnp.where(lane == LANES - 1, b, a) for a, b in zip(right, right[1:])]
    west = [jnp.where(lane == 0, a, b) for a, b in zip(left, left[1:])]
    return jnp.concatenate(east, axis=1), jnp.concatenate(west, axis=1)


def turned(ends, level):
    return pltpu.roll(ends, lax.rem(2 * LANES - 2 * level, LANES), 1)


LEVELS_AT_ONCE = 6


def before_body(ext, light, temp, got_a, got_b, base, laps, halo):
    levels, rows, width = temp.shape
    counts = ext[3]
    own_counts = counts[:rows]
    lane = lane_ids(3 * TILE, width)
    limit_east = jnp.where(lane == width - 1, 0.0, jnp.minimum(counts, roll_lanes(counts, -1)))
    limit_north = jnp.minimum(counts, roll_rows(counts, -1))
    limits = (limit_east, roll_lanes(limit_east, 1), limit_north, roll_rows(limit_north, 1))
    step = math.gcd(levels, LEVELS_AT_ONCE)
    odd = lax.rem(lax.axis_index("lat"), 2) == 1
    near = near_lanes(width)
    for level in range(levels):
        rows_near = unpack_rows(jnp.logical_not(odd), got_a[level // 4], level)
        rows_far = unpack_rows(odd, got_b[level // 4], level)
        halo[level] = jnp.where(near, rows_near, rows_far)

    def group(at, down_before):
        for inner in range(step):
            level = at * step + inner
            level_f = level.astype(f32)
            own = temp[level]
            whole = jnp.concatenate([own, halo[level]], axis=0)
            east, west = sideways(whole, whole[:, :LANES])
            lap = -4.0 * whole
            for around, limit in zip(
                (east, west, roll_rows(whole, -1), roll_rows(whole, 1)), limits
            ):
                lap = lap + jnp.where(level_f < limit, around, whole)
            laps[level] = lap
            beneath = temp[jnp.minimum(level + 1, levels - 1)]
            down = jnp.where(level_f + 1.0 < own_counts, beneath - own, 0.0)
            absorb = jnp.exp(jnp.full(own.shape, -1.0 / light_decay, f32) * level_f)
            absorb = absorb * (light_gain * (1.0 - math.exp(-1.0 / light_decay)))
            source = absorb * light[1] + jnp.where(level == 0, heat_gain, 0.0) * light[0]
            change = diapycnal_diffusion * (down - down_before) + source
            base[level] = own + jnp.where(level_f < own_counts, change, 0.0)
            down_before = down
        return down_before

    lax.fori_loop(0, levels // step, group, jnp.zeros((rows, width), f32))


def finish_level(level, own, halo_level, base, lap, ends, limits, speeds):
    rows, width = own.shape
    level_f = level.astype(f32)
    lane = lane_ids(3 * TILE)
    side = turned(ends[2], level)
    parts = [lap[:, at : at + LANES] for at in range(0, width, LANES)]
    parts[0] = parts[0] + jnp.where(lane == 0, side, 0.0)
    parts[-1] = parts[-1] + jnp.where(lane == LANES - 1, side, 0.0)
    lap = jnp.concatenate(parts, axis=1)
    whole = jnp.concatenate([own, halo_level], axis=0)
    own_lap = lap[:rows]
    around_temp = sideways(own, turned(ends[0][:rows], level))
    around_temp += (roll_rows(whole, -1)[:rows], roll_rows(whole, 1)[:rows])
    around_lap = sideways(own_lap, turned(ends[1][:rows], level))
    around_lap += (roll_rows(lap, -1)[:rows], roll_rows(lap, 1)[:rows])
    change = jnp.zeros((rows, width), f32)
    for place, limit in enumerate(limits):
        moved = mixing_fourth * (own_lap - around_lap[place])
        moved = moved - speeds[place] * (around_temp[place] + own)
        change = change + jnp.where(level_f < limit, moved, 0.0)
    return base + change


def hot_body(points, hot):
    links, rows, width = points.shape
    blocks = width // LANES
    cells = row_ids(LANES).astype(f32).astype(jnp.bfloat16)
    one, none = jnp.bfloat16(1.0), jnp.bfloat16(0.0)
    for k in range(links):
        for b in range(blocks):
            for row in range(rows):
                line = points[k, row : row + 1, b * LANES : (b + 1) * LANES]
                line = jnp.broadcast_to(line.astype(f32), (2 * TILE, LANES)).astype(jnp.bfloat16)
                line = jnp.concatenate([line] * (LANES // (2 * TILE)), axis=0)
                hot[k * rows + row, :, b * LANES : (b + 1) * LANES] = jnp.transpose(
                    jnp.where(line == cells, one, none)
                )


def subcycle_body(
    levels,
    ext,
    edges_own,
    edges_halo,
    got_a,
    got_b,
    temp,
    halo,
    base,
    laps,
    hot,
    weights,
    tile_hbm,
    out_height,
    out_zonal,
    out_merid,
    limits_out,
    speeds_out,
    ends_out,
    sums_a,
    sums_b,
    sums_mid,
    whole,
    values,
    table,
    tile,
    tile_sem,
):
    tile_copy = pltpu.make_async_copy(tile_hbm, tile, tile_sem)
    tile_copy.start()
    edges = [
        jnp.concatenate([edges_own[place], edges_halo[place]], axis=0) for place in range(2)
    ]
    width = ext.shape[2]
    rows = temp.shape[1]
    lon_even = lax.rem(lax.axis_index("lon"), 2) == 0
    even = lax.rem(lax.axis_index("lat"), 2) == 0
    lane = lane_ids(3 * TILE)
    from_east = [jnp.where(lon_even, got_a[place], got_b[place]) for place in range(2)]
    from_west = [jnp.where(lon_even, got_b[place], got_a[place]) for place in range(2)]
    planes = []
    for place in range(ext.shape[0]):
        third = jnp.where(
            lane < 3,
            roll_lanes(from_east[0], -3 * place),
            jnp.where(lane >= LANES - 3, roll_lanes(from_west[0], 3 * place), 0.0),
        )
        planes.append(jnp.concatenate([ext[place], third], axis=1))
    height, zonal, merid, counts, wind_east, wind_north, fresh = planes

    def east_of(array):
        return roll_lanes(array, -1)

    def west_of(array):
        return roll_lanes(array, 1)

    def north_of(array):
        return roll_rows(array, -1)

    def south_of(array):
        return roll_rows(array, 1)

    depth = column_depth(counts, levels)
    wet = (counts > 0.5).astype(f32)
    east_wet = wet * east_of(wet)
    north_wet = wet * north_of(wet)
    east_depth = jnp.minimum(depth, east_of(depth))
    north_depth = jnp.minimum(depth, north_of(depth))
    east_pull = grav_step * east_depth
    north_pull = grav_step * north_depth
    wind_east = wind_step * wind_east
    wind_north = wind_step * wind_north
    fresh = fresh_step * fresh
    for _ in range(SUBS):
        zonal = east_wet * (zonal - east_pull * (east_of(height) - height) + wind_east)
        merid = north_wet * (merid - north_pull * (north_of(height) - height) + wind_north)
        spread = zonal - west_of(zonal) + merid - south_of(merid)
        height = height + wet * (fresh - height_step * spread)
    out_height[...] = height[:rows, :width]
    out_zonal[...] = zonal[:rows, :width]
    out_merid[...] = merid[:rows, :width]

    limit_east = jnp.minimum(counts, east_of(counts))
    limit_north = jnp.minimum(counts, north_of(counts))
    limit_west, limit_south = west_of(limit_east), south_of(limit_north)
    limits = [
        limit[:rows, :width] for limit in (limit_east, limit_west, limit_north, limit_south)
    ]
    speed_east = 0.5 * advect_coef * zonal / jnp.maximum(east_depth, depth_floor)
    speed_north = 0.5 * advect_coef * merid / jnp.maximum(north_depth, depth_floor)
    speeds = [
        speed[:rows, :width]
        for speed in (speed_east, -west_of(speed_east), speed_north, -south_of(speed_north))
    ]
    for place in range(4):
        limits_out[place] = limits[place]
        speeds_out[place] = speeds[place]

    lane_level = (lane // 2).astype(f32)
    odd_lane = (lane & 1) == 1
    far_east, far_west = from_east[1], from_west[1]

    def column(limit, at):
        return jnp.broadcast_to(limit[:, at : at + 1], (3 * TILE, LANES))

    def edge_lap(center, toward_east, toward_west, at, at_west):
        total = -4.0 * center
        for around, limit in (
            (toward_east, column(limit_east, at)),
            (toward_west, column(limit_east, at_west)),
            (north_of(center), column(limit_north, at)),
            (south_of(center), column(limit_south, at)),
        ):
            total = total + jnp.where(lane_level < limit, around, center)
        return total

    total_lanes = width + LANES
    lap_west = edge_lap(
        far_west,
        roll_lanes(edges[0], 1),
        roll_lanes(far_west, 1),
        total_lanes - 1,
        total_lanes - 2,
    )
    lap_east = edge_lap(
        far_east, roll_lanes(far_east, -1), roll_lanes(edges[1], -1), width, width - 1
    )
    side_west = far_west - roll_lanes(edges[0], 1)
    side_west = jnp.where(lane_level < column(limit_east, total_lanes - 1), side_west, 0.0)
    side_east = far_east - roll_lanes(edges[1], -1)
    side_east = jnp.where(lane_level < column(limit_east, width - 1), side_east, 0.0)
    ends = []
    for west, east in ((far_west, far_east), (lap_west, lap_east), (side_west, side_east)):
        ends.append(roll_lanes(jnp.where(odd_lane, west, east), -1))
    for place in range(3):
        ends_out[place] = ends[place]

    zero = jnp.zeros((), i32)
    top = finish_level(zero, temp[0], halo[0], base[0], laps[0], ends, limits, speeds)
    own_wet = wet[:rows, :width]
    thick = jnp.maximum(depth[:rows, :width], depth_floor)
    surface = [
        top * own_wet,
        height[:rows, :width] * own_wet,
        zonal[:rows, :width] / thick * own_wet,
        merid[:rows, :width] / thick * own_wet,
        own_wet,
    ]
    nsums = len(surface)
    values[...] = jnp.zeros(values.shape, f32)
    for place in range(nsums):
        values[:, place, :] = surface[place]
    table[...] = jnp.zeros(table.shape, f32)
    links = weights.shape[0]
    blocks = width // LANES
    tile_copy.wait()

    for row in range(rows):
        held = values[row]
        for k in range(links):
            shares = held * weights[k, row : row + 1, :]
            upper = shares.astype(jnp.bfloat16)
            lower = (shares - upper.astype(f32)).astype(jnp.bfloat16)
            both = jnp.concatenate([upper, lower], axis=0)
            stacked = jnp.concatenate(
                [both[:, b * LANES : (b + 1) * LANES] for b in range(blocks)], axis=0
            )
            found = jnp.dot(stacked, hot[k * rows + row], preferred_element_type=f32)
            for b in range(blocks):
                target = tile[k, b, row]
                mine = found[b * 2 * TILE : (b + 1) * 2 * TILE, b * LANES : (b + 1) * LANES]
                table[target] = table[target] + mine
    for place in range(nsums):
        total = table[:, place, :] + table[:, TILE + place, :]
        south, middle, north = total[:TILE], total[TILE : 2 * TILE], total[2 * TILE :]
        sums_mid[place] = middle
        sums_a[place] = jnp.where(even, north, south)
        sums_b[place] = jnp.where(even, south, north)

    run_levels(
        0,
        early_groups(levels),
        temp,
        halo,
        base,
        laps,
        limits_out,
        speeds_out,
        ends_out,
        whole,
    )


def level_step(levels):
    return math.gcd(levels, LEVELS_AT_ONCE)


def early_groups(levels):
    groups = levels // level_step(levels)
    place = lax.axis_index("lat")
    inner = jnp.where(lax.rem(place, 2) == 1, groups // 5, 0)
    return jnp.where(place == 0, groups // 2, inner)


LAST_GROUPS = 2


def run_levels(start, stop, temp, halo, base, laps, limits, speeds, ends, out, done=None):
    step = level_step(temp.shape[0])

    def group(at, carry):
        for inner in range(step):
            level = jnp.int32(at * step + inner)
            out[level] = finish_level(
                level,
                temp[level],
                halo[level],
                base[level],
                laps[level],
                [ends[place] for place in range(3)],
                [limits[place] for place in range(4)],
                [speeds[place] for place in range(4)],
            )
        if done is not None:
            done(at)
        return carry

    lax.fori_loop(start, stop, group, 0)


def tracer_body(
    temp,
    halo,
    base,
    laps,
    limits,
    speeds,
    ends,
    draft,
    height,
    zonal,
    merid,
    out_height,
    out_zonal,
    out_merid,
    out,
    whole,
    sems,
    level_sems,
):
    levels = temp.shape[0]
    step = level_step(levels)
    groups = levels // step
    pairs = [(height, out_height), (zonal, out_zonal), (merid, out_merid)]
    copies = [
        pltpu.make_async_copy(source, target, sems.at[place])
        for place, (source, target) in enumerate(pairs)
    ]
    for copy in copies:
        copy.start()

    def level_copy(at, source=whole):
        part = pl.ds(at * step, step)
        return pltpu.make_async_copy(source.at[part], out.at[part], level_sems.at[at])

    early = early_groups(levels)

    def start(at, carry):
        level_copy(at, draft).start()
        return carry

    lax.fori_loop(0, early, start, 0)
    inside = max(groups - LAST_GROUPS, 0)
    refs = (temp, halo, base, laps, limits, speeds, ends, whole)
    run_levels(early, inside, *refs, lambda at: level_copy(at).start())
    run_levels(inside, groups, *refs)
    for at in range(inside):
        level_copy(at).wait()
    for copy in copies:
        copy.wait()


def merge_body(mid, got_a, got_b, flags, whole, draft, out, out_temp, surface, sems):
    levels = whole.shape[0]
    step = level_step(levels)
    first = step * max(levels // step - LAST_GROUPS, 0)
    part = pl.ds(first, levels - first)
    rest = pltpu.make_async_copy(whole.at[part], out_temp.at[part], sems.at[0])
    rest.start()
    open_sea = (1 - flags[...]).astype(f32)
    nsurf = out.shape[0]
    area = mid[nsurf] + got_a[nsurf] + got_b[nsurf]
    scale = open_sea / jnp.maximum(area, area_floor)
    for place in range(nsurf):
        surface[place] = (mid[place] + got_a[place] + got_b[place]) * scale
    copy = pltpu.make_async_copy(surface, out, sems.at[1])
    copy.start()
    copy.wait()
    rest.wait()


def shards(
    free_elevation,
    zonal_volume_carriage,
    meridional_volume_carriage,
    thermal_field,
    flooded_strata_number,
    aerial_exchanges,
    aerial_terrain_flags,
    donor_tile_number,
    donor_point_number,
    pairing_coefficients,
):
    levels, rows, width = thermal_field.shape
    nflux, band_rows, lanes = aerial_exchanges.shape
    links, _, blocks = donor_tile_number.shape
    assert rows == 2 * TILE and band_rows == TILE and lanes == LANES
    assert 2 * levels <= LANES and lax.axis_size("lon") % 2 == 0
    nsums = 5
    fields = 4 + 2 * links
    flux_at = fields // 2
    flux_tiles = (nflux + 2) // 2
    temp_at = flux_at + flux_tiles
    groups = pl.cdiv(levels, 4)
    tile_lines = jnp.swapaxes(donor_tile_number, 1, 2)
    temp = thermal_field
    edge_a, own, state, points, weights, flags = call(
        load_body,
        [
            shape(temp_at, TILE, width),
            shape(nflux + 2, TILE, LANES),
            shape(4, rows, width),
            shape(links, rows, width, dtype=i32),
            shape(links, rows, width),
            shape(band_rows, lanes, dtype=i32),
        ],
        (
            free_elevation,
            zonal_volume_carriage,
            meridional_volume_carriage,
            flooded_strata_number,
            donor_point_number,
            tile_lines,
            pairing_coefficients,
            aerial_exchanges,
            aerial_terrain_flags,
        ),
        "load",
        1.6,
        scratch=[
            pltpu.VMEM((rows, width), i32),
            pltpu.VMEM((links, blocks, rows), i32),
            pltpu.VMEM((nflux, band_rows, lanes), f32),
            pltpu.SemaphoreType.DMA((9,)),
        ],
        hbm=range(9),
    )
    got_a = swap(edge_a, "lat", 0, False)
    far_tiles = (len(HALO_FLUXES) + 1) // 2
    edge_tiles = temp_at + far_tiles
    draft_b, edges = call(
        pack_second_body,
        [
            shape(edge_tiles, TILE, width),
            shape(2, rows, LANES),
        ],
        (own, state, points, weights, temp),
        "pack_b",
        0.3,
    )
    (edge_b,) = call(
        functools.partial(pack_flux_body, flux_at),
        [shape(edge_tiles, TILE, width)],
        (draft_b, got_a, edges),
        "pack_flux",
        0.0,
    )
    got_b = swap(edge_b, "lat", 1, False)
    (temp_b,) = call(
        functools.partial(pack_temp_body, 1),
        [shape(groups, TILE, width)],
        (temp, edge_b),
        "pack_temp_b",
        LATE,
    )
    got_temp_b = swap(temp_b, "lat", 1, False)
    (temp_a,) = call(
        functools.partial(pack_temp_body, 0),
        [shape(groups, TILE, width)],
        (temp, temp_b),
        "pack_temp_a",
        0.0,
    )
    got_temp_a = swap(temp_a, "lat", 0, False)
    (edge_c,) = call(
        functools.partial(pack_third_body, flux_at),
        [shape(far_tiles, TILE, width)],
        (got_b, edges),
        "pack_c",
        LATE,
    )
    got_c = swap(edge_c, "lat", 0, False)
    draft_ext, light = call(
        functools.partial(forcing_body, flux_at),
        [shape(7, 3 * TILE, width), shape(2, rows, width)],
        (got_a, got_b, own, state, points, weights),
        "forcing",
        0.4,
    )
    ext, send_a, send_b, edges_halo = call(
        functools.partial(forcing_halo_body, flux_at),
        [
            shape(7, 3 * TILE, width),
            shape(2, 3 * TILE, LANES),
            shape(2, 3 * TILE, LANES),
            shape(2, TILE, LANES),
        ],
        (draft_ext, got_a, got_b, got_c, own, edges),
        "forcing_halo",
        0.3,
    )
    lon_b = swap(send_b, "lon", 1, True)
    (send_a,) = call(
        pass_body, [shape(2, 3 * TILE, LANES)], (send_a, send_b), "pass_lon", LATE
    )
    lon_a = swap(send_a, "lon", 0, True)
    (hot,) = call(
        hot_body,
        [shape(links * rows, LANES, blocks * LANES, dtype=jnp.bfloat16)],
        (points,),
        "hot",
        0.0,
    )
    base, laps, halo = call(
        before_body,
        [
            shape(levels, rows, width),
            shape(levels, 3 * TILE, width),
            shape(levels, TILE, width),
        ],
        (ext, light, temp, got_temp_a, got_temp_b),
        "before",
        0.0,
    )
    (
        advanced_elevation,
        transport_x_next,
        transport_y_next,
        limits,
        speeds,
        ends,
        sums_a,
        sums_b,
        sums_mid,
        draft,
    ) = call(
        functools.partial(subcycle_body, levels),
        [shape(rows, width)] * 3
        + [shape(4, rows, width), shape(4, rows, width), shape(3, 3 * TILE, LANES)]
        + [shape(nsums, TILE, LANES)] * 3
        + [shape(levels, rows, width)],
        (
            ext,
            edges,
            edges_halo,
            lon_a,
            lon_b,
            temp,
            halo,
            base,
            laps,
            hot,
            weights,
            tile_lines,
        ),
        "subcycles",
        2.6,
        scratch=[
            pltpu.VMEM((rows, TILE, width), f32),
            pltpu.VMEM((3 * TILE, 2 * TILE, LANES), f32),
            pltpu.SMEM((links, blocks, rows), i32),
            pltpu.SemaphoreType.DMA(()),
        ],
        hbm=(11,),
    )
    back_b = swap(sums_b, "lat", 1, False)
    (sums_a,) = call(
        pass_body, [shape(nsums, TILE, LANES)], (sums_a, sums_b), "pass_sums", LATE
    )
    back_a = swap(sums_a, "lat", 0, False)
    advanced_elevation, transport_x_next, transport_y_next, draft_field, draft = call(
        tracer_body,
        [
            pltpu.HBM((rows, width), f32),
            pltpu.HBM((rows, width), f32),
            pltpu.HBM((rows, width), f32),
            pltpu.HBM((levels, rows, width), f32),
            shape(levels, rows, width),
        ],
        (
            temp,
            halo,
            base,
            laps,
            limits,
            speeds,
            ends,
            draft,
            advanced_elevation,
            transport_x_next,
            transport_y_next,
        ),
        "tracer",
        2.5,
        scratch=[
            pltpu.SemaphoreType.DMA((3,)),
            pltpu.SemaphoreType.DMA((levels // level_step(levels),)),
        ],
    )
    marine_skin_condition, advanced_thermal_field = call(
        merge_body,
        [
            pltpu.HBM((nsums - 1, band_rows, lanes), f32),
            pltpu.HBM((levels, rows, width), f32),
        ],
        (sums_mid, back_a, back_b, flags, draft, draft_field),
        "merge",
        0.1,
        aliases={5: 1},
        hbm=(5,),
        scratch=[
            pltpu.VMEM((nsums - 1, band_rows, lanes), f32),
            pltpu.SemaphoreType.DMA((2,)),
        ],
    )
    return (
        advanced_elevation,
        transport_x_next,
        transport_y_next,
        advanced_thermal_field,
        marine_skin_condition,
    )


def solution(mesh):
    flat = P("lat", "lon")
    deep = P(None, "lat", "lon")
    return jax.shard_map(
        shards,
        mesh=mesh,
        in_specs=(flat, flat, flat, deep, flat, deep, flat, deep, deep, deep),
        out_specs=(flat, flat, flat, deep, deep),
        check_vma=False,
    )
```

```python
import functools
import math

import jax
import jax.numpy as jnp
from jax import lax
from jax.experimental import pallas as pl
from jax.experimental.pallas import tpu as pltpu
from jax.sharding import PartitionSpec as P

SUBS = 3

grav_step = 0.6
height_step = 0.6
wind_step = 0.5
fresh_step = 0.5
mixing_fourth = 0.02
advect_coef = 0.1
diapycnal_diffusion = 0.2
heat_gain = 0.3
light_gain = 0.3
light_decay = 8.0
depth_floor = 0.25
area_floor = 1.0

TILE = 8
LANES = 128
HALF = TILE // 2

f32 = jnp.float32
i32 = jnp.int32

LATE = 4.0
FLOPS_PER_US = 1150000000


def swap_pairs(count, first, periodic):
    pairs = []
    for low in range(first, count, 2):
        high = low + 1
        if high == count:
            if not periodic:
                continue
            high = 0
        pairs += [(low, high), (high, low)]
    return pairs


def swap(array, axis, first, periodic):
    return lax.ppermute(array, axis, swap_pairs(lax.axis_size(axis), first, periodic))


def lane_ids(rows, width=LANES):
    return lax.broadcasted_iota(i32, (rows, width), 1)


def row_ids(rows, width=LANES):
    return lax.broadcasted_iota(i32, (rows, width), 0)


def roll_rows(array, by):
    by = by % array.shape[0]
    return pltpu.roll(array, by, 0) if by else array


def roll_lanes(array, by):
    by = by % array.shape[1]
    return pltpu.roll(array, by, 1) if by else array


def call(body, outs, ins, name, took, aliases=None, scratch=(), hbm=()):
    specs = [
        pl.BlockSpec(memory_space=pltpu.HBM if place in hbm else pltpu.VMEM)
        for place in range(len(ins))
    ]
    ins = [
        pltpu.with_memory_space_constraint(leaf, pltpu.HBM) if place in hbm else leaf
        for place, leaf in enumerate(ins)
    ]
    return pl.pallas_call(
        body,
        out_shape=outs,
        in_specs=specs,
        out_specs=[pl.BlockSpec(memory_space=leaf.memory_space) for leaf in outs],
        scratch_shapes=list(scratch),
        input_output_aliases=aliases or {},
        compiler_params=pltpu.CompilerParams(vmem_limit_bytes=12 * 1024 * 1024),
        cost_estimate=pl.CostEstimate(
            flops=int(took * FLOPS_PER_US), bytes_accessed=1024, transcendentals=0
        ),
        name=name,
    )(*ins)


def shape(*dims, dtype=f32):
    return pltpu.VMEM(dims, dtype)


def write_edge(top, fields, out_ref):
    sub = row_ids(TILE, out_ref.shape[2])
    mine = (sub >= HALF) == top
    for place in range(len(fields) // 2):
        first = jnp.where(top, fields[2 * place][TILE:], fields[2 * place][:TILE])
        second = jnp.where(top, fields[2 * place + 1][TILE:], fields[2 * place + 1][:TILE])
        out_ref[place] = jnp.where(mine, first, roll_rows(second, HALF))


def write_planes(planes, out_ref, at):
    planes = planes + [planes[-1]] * (len(planes) % 2)
    for place in range(len(planes) // 2):
        out_ref[at + place] = jnp.concatenate(planes[2 * place : 2 * place + 2], axis=1)


def edge_numbers(top, numbers):
    return jnp.where(top, numbers[1], numbers[0])


def write_temp_edge(top, temp_ref, out_ref, at):
    levels, _, width = temp_ref.shape
    sub = row_ids(TILE, width)
    for group in range(pl.cdiv(levels, 4)):
        packed = jnp.zeros((TILE, width), f32)
        for spot in range(min(4, levels - 4 * group)):
            level = 4 * group + spot
            low = roll_rows(temp_ref[level, :TILE, :], 2 * spot)
            high = roll_rows(temp_ref[level, TILE:, :], 2 * spot + 2)
            packed = jnp.where(sub // 2 == spot, jnp.where(top, high, low), packed)
        out_ref[at + group] = packed


def goes_north(first):
    return (lax.rem(lax.axis_index("lat"), 2) == 0) == (first == 0)


def edge_fields(state, points, weights):
    links = points.shape[0]
    fields = [state[place] for place in range(4)]
    fields += [points[k].astype(f32) for k in range(links)]
    fields += [weights[k] for k in range(links)]
    return fields


def load_body(
    height,
    zonal,
    merid,
    counts,
    points,
    tile,
    weights,
    flux,
    flags,
    edge,
    own,
    state_out,
    points_out,
    weights_out,
    flags_out,
    tile_out,
    counts_in,
    flux_in,
    sems,
):
    pairs = [
        (flux, flux_in),
        (flags, flags_out),
        (tile, tile_out),
        (counts, counts_in),
        (height, state_out.at[0]),
        (zonal, state_out.at[1]),
        (merid, state_out.at[2]),
        (points, points_out),
        (weights, weights_out),
    ]
    copies = [
        pltpu.make_async_copy(source, target, sems.at[place])
        for place, (source, target) in enumerate(pairs)
    ]
    for copy in copies:
        copy.start()
    for copy in copies:
        copy.wait()
    state_out[3] = counts_in[...].astype(f32)
    open_sea = (1 - flags_out[...]).astype(f32)
    masked = [flux_in[plane] * open_sea for plane in range(flux.shape[0])]
    for plane, values in enumerate(masked):
        own[plane] = values
    top = goes_north(0)
    fields = edge_fields(state_out, points_out, weights_out)
    write_edge(top, fields, edge)
    write_planes(masked[:1] + masked, edge, len(fields) // 2)


def pack_second_body(own, state, points, weights, tile, temp, draft, edges, numbers):
    top = goes_north(1)
    fields = edge_fields(state, points, weights)
    write_edge(top, fields, draft)
    links, blocks, rows = tile.shape
    lane = lane_ids(rows)
    diagonal = row_ids(rows, rows) == lane_ids(rows, rows)
    tiles = jnp.zeros((rows, LANES), f32)
    for k in range(links):
        for b in range(blocks):
            line = jnp.broadcast_to(tile[k, b : b + 1, :].astype(f32), (rows, rows))
            upright = jnp.sum(jnp.where(diagonal, line, 0.0), axis=1, keepdims=True)
            tiles = jnp.where(lane == k * blocks + b, upright, tiles)
    numbers[0] = tiles[:TILE]
    numbers[1] = tiles[TILE:]
    masked = [own[plane] for plane in range(own.shape[0])]
    write_planes([edge_numbers(top, numbers)] + masked, draft, len(fields) // 2)
    levels, rows, _ = temp.shape
    for place, columns in enumerate(edge_columns([temp[level] for level in range(levels)], rows)):
        edges[place] = columns


def corner_plane(top, edges):
    west = jnp.where(top, edges[0, TILE:, :], edges[0, :TILE, :])
    east = jnp.where(top, edges[1, TILE:, :], edges[1, :TILE, :])
    return jnp.where((row_ids(TILE) >= HALF) == top, west, roll_rows(east, HALF))


def far_planes(flux_at, received):
    return [spot_of(received, flux_at, 1 + plane) for plane in HALO_FLUXES]


def pack_flux_body(flux_at, draft, received, edges, out):
    planes = far_planes(flux_at, received) + [corner_plane(goes_north(1), edges)]
    at = out.shape[0] - len(planes) // 2
    out[:at] = draft[:at]
    write_planes(planes, out, at)


def edge_columns(fields, rows):
    lane = lane_ids(rows)
    high = jnp.zeros((rows, LANES), f32)
    low = jnp.zeros((rows, LANES), f32)
    for level, field in enumerate(fields):
        ends = jnp.where(lane < HALF, field[:, :LANES], field[:, -LANES:])
        turned = roll_lanes(ends, 2 * level + 2)
        high = jnp.where(lane // 2 == level, turned, high)
        low = jnp.where(lane // 2 == (level + 1) % (LANES // 2), turned, low)
    return roll_lanes(low, -2), high


HALO_FLUXES = (0, 1, 4)


def pass_body(first, second, out):
    out[...] = first[...]


def pack_temp_body(first, temp, other, out):
    write_temp_edge(goes_north(first), temp, out, 0)


def pack_third_body(flux_at, received, edges, numbers, out):
    top = goes_north(0)
    planes = far_planes(flux_at, received)
    write_planes(planes + [corner_plane(top, edges), edge_numbers(top, numbers)], out, 0)


def unpack_rows(top, packed, level):
    spot = level % 4
    return jnp.where(top, roll_rows(packed, -2 * spot), roll_rows(packed, 6 - 2 * spot))


def near_lanes(width):
    return (row_ids(TILE, width) < HALF) == (lax.rem(lax.axis_index("lat"), 2) == 0)


def pick(array, rows):
    return jnp.take_along_axis(array, rows, axis=0, mode="promise_in_bounds")


def pick_lane(array, lanes):
    return jnp.take_along_axis(array, lanes, axis=1, mode="promise_in_bounds")


def spot_of(array, flux_at, place):
    return array[flux_at + place // 2, :, (place % 2) * LANES : (place % 2 + 1) * LANES]


def by_side(even, one, two):
    return jnp.where(even, one, two), jnp.where(even, two, one)


def row_numbers(numbers, column):
    number = jnp.broadcast_to(numbers[:, column : column + 1].astype(i32), (TILE, LANES))
    return number & (TILE - 1), lax.shift_right_logical(number, 3)


FORCING_AT = {0: 4, 1: 5, 4: 6}


def forcing_body(flux_at, got_a, got_b, own, numbers, state, points, weights, ext, light):
    even = lax.rem(lax.axis_index("lat"), 2) == 0
    links, rows, width = points.shape
    blocks = width // LANES
    nflux = own.shape[0]
    ext[:4, :rows, :] = state[...]
    north, south = [], []
    for plane in range(nflux):
        one, two = spot_of(got_a, flux_at, 1 + plane), spot_of(got_b, flux_at, 1 + plane)
        high, low = by_side(even, one, two)
        north.append(high)
        south.append(low)
    mid = [own[plane] for plane in range(nflux)]
    for row_tile in range(rows // TILE):
        here = slice(row_tile * TILE, (row_tile + 1) * TILE)
        for b in range(blocks):
            cols = slice(b * LANES, (b + 1) * LANES)
            totals = [jnp.zeros((TILE, LANES), f32) for _ in range(nflux)]
            for k in range(links):
                within, band = row_numbers(numbers[row_tile], k * blocks + b)
                lanes = points[k, here, cols]
                weight = weights[k, here, cols]
                for plane in range(nflux):
                    value = jnp.where(
                        band == 0,
                        pick(south[plane], within),
                        jnp.where(band == 1, pick(mid[plane], within), pick(north[plane], within)),
                    )
                    totals[plane] = totals[plane] + weight * pick_lane(value, lanes)
            for plane in range(nflux):
                if plane in FORCING_AT:
                    ext[FORCING_AT[plane], here, cols] = totals[plane]
                else:
                    light[plane - 2, here, cols] = totals[plane]


def both_fields(even, near, far):
    north, south = by_side(even, near, far)
    sub = row_ids(*near.shape)
    return [
        jnp.where(sub < HALF, north, south),
        roll_rows(jnp.where(sub < HALF, south, north), HALF),
    ]


def forcing_halo_body(
    flux_at,
    draft,
    got_a,
    got_b,
    got_c,
    own,
    edges,
    ext,
    send_a,
    send_b,
    edges_halo,
):
    even = lax.rem(lax.axis_index("lat"), 2) == 0
    rows, width = 2 * TILE, ext.shape[2]
    blocks = width // LANES
    links = flux_at - 2
    halos = []
    for place in range(flux_at):
        halos += both_fields(even, got_a[place], got_b[place])
    ext[:, :rows, :] = draft[:, :rows, :]
    for place in range(4):
        ext[place, rows:, :] = halos[place]
    tables = {}
    far_at = got_b.shape[0] - (len(HALO_FLUXES) + 1) // 2
    for place, plane in enumerate(HALO_FLUXES):
        one, two = spot_of(got_a, flux_at, 1 + plane), spot_of(got_b, flux_at, 1 + plane)
        north, south = by_side(even, one, two)
        far_north, far_south = by_side(
            even, spot_of(got_c, 0, place), spot_of(got_b, far_at, place)
        )
        tables[plane] = [far_south, south, own[plane], north, far_north]
    sub_one = row_ids(TILE)
    north, south = by_side(
        even, spot_of(got_c, 0, len(HALO_FLUXES) + 1), spot_of(got_b, flux_at, 0)
    )
    numbers = jnp.where(sub_one < HALF, north, south)
    for b in range(blocks):
        cols = slice(b * LANES, (b + 1) * LANES)
        totals = {plane: jnp.zeros((TILE, LANES), f32) for plane in HALO_FLUXES}
        for k in range(links):
            within, band = row_numbers(numbers, k * blocks + b)
            band = band + jnp.where(sub_one < HALF, 2, 0)
            lanes = halos[4 + k][:, cols].astype(i32)
            weight = halos[4 + links + k][:, cols]
            for plane in HALO_FLUXES:
                value = pick(tables[plane][0], within)
                for at in range(1, 5):
                    value = jnp.where(band == at, pick(tables[plane][at], within), value)
                totals[plane] = totals[plane] + weight * pick_lane(value, lanes)
        for plane in HALO_FLUXES:
            ext[FORCING_AT[plane], rows:, cols] = totals[plane]

    lane = lane_ids(3 * TILE)
    to_west = jnp.zeros((3 * TILE, LANES), f32)
    to_east = jnp.zeros((3 * TILE, LANES), f32)
    for place in range(ext.shape[0]):
        low = roll_lanes(ext[place, :, :LANES], 3 * place)
        high = roll_lanes(ext[place, :, width - LANES :], -3 * place)
        to_west = jnp.where((lane >= 3 * place) & (lane < 3 * place + 3), low, to_west)
        edge = LANES - 3 * place
        to_east = jnp.where((lane >= edge - 3) & (lane < edge), high, to_east)
    corner = len(HALO_FLUXES)
    corners = both_fields(even, spot_of(got_c, 0, corner), spot_of(got_b, far_at, corner))
    for place in range(2):
        edges_halo[place] = corners[place]
    lon_even = lax.rem(lax.axis_index("lon"), 2) == 0
    send_a[0] = jnp.where(lon_even, to_east, to_west)
    send_b[0] = jnp.where(lon_even, to_west, to_east)
    for part, columns in ((slice(0, rows), edges), (slice(rows, rows + TILE), edges_halo)):
        send_a[1, part, :] = jnp.where(lon_even, columns[1], columns[0])
        send_b[1, part, :] = jnp.where(lon_even, columns[0], columns[1])


def column_depth(counts, levels):
    scale = 1.0 / (2.0 * levels)
    return counts * scale + counts * (counts - 1.0) * (scale / levels)


def sideways(array, ends):
    rows, width = array.shape
    lane = lane_ids(rows)
    parts = [array[:, at : at + LANES] for at in range(0, width, LANES)]
    right = [roll_lanes(part, -1) for part in parts] + [ends]
    left = [ends] + [roll_lanes(part, 1) for part in parts]
    east = [jnp.where(lane == LANES - 1, b, a) for a, b in zip(right, right[1:])]
    west = [jnp.where(lane == 0, a, b) for a, b in zip(left, left[1:])]
    return jnp.concatenate(east, axis=1), jnp.concatenate(west, axis=1)


def turned(ends, level):
    return pltpu.roll(ends, lax.rem(2 * LANES - 2 * level, LANES), 1)


LEVELS_AT_ONCE = 6


def before_body(ext, light, temp, got_a, got_b, base, laps, halo):
    levels, rows, width = temp.shape
    counts = ext[3]
    own_counts = counts[:rows]
    lane = lane_ids(3 * TILE, width)
    limit_east = jnp.where(lane == width - 1, 0.0, jnp.minimum(counts, roll_lanes(counts, -1)))
    limit_north = jnp.minimum(counts, roll_rows(counts, -1))
    limits = (limit_east, roll_lanes(limit_east, 1), limit_north, roll_rows(limit_north, 1))
    step = math.gcd(levels, LEVELS_AT_ONCE)
    odd = lax.rem(lax.axis_index("lat"), 2) == 1
    near = near_lanes(width)
    for level in range(levels):
        rows_near = unpack_rows(jnp.logical_not(odd), got_a[level // 4], level)
        rows_far = unpack_rows(odd, got_b[level // 4], level)
        halo[level] = jnp.where(near, rows_near, rows_far)

    def group(at, down_before):
        for inner in range(step):
            level = at * step + inner
            level_f = level.astype(f32)
            own = temp[level]
            whole = jnp.concatenate([own, halo[level]], axis=0)
            east, west = sideways(whole, whole[:, :LANES])
            lap = -4.0 * whole
            for around, limit in zip(
                (east, west, roll_rows(whole, -1), roll_rows(whole, 1)), limits
            ):
                lap = lap + jnp.where(level_f < limit, around, whole)
            laps[level] = lap
            beneath = temp[jnp.minimum(level + 1, levels - 1)]
            down = jnp.where(level_f + 1.0 < own_counts, beneath - own, 0.0)
            absorb = jnp.exp(jnp.full(own.shape, -1.0 / light_decay, f32) * level_f)
            absorb = absorb * (light_gain * (1.0 - math.exp(-1.0 / light_decay)))
            source = absorb * light[1] + jnp.where(level == 0, heat_gain, 0.0) * light[0]
            change = diapycnal_diffusion * (down - down_before) + source
            base[level] = own + jnp.where(level_f < own_counts, change, 0.0)
            down_before = down
        return down_before

    lax.fori_loop(0, levels // step, group, jnp.zeros((rows, width), f32))


def finish_level(level, own, halo_level, base, lap, ends, limits, speeds):
    rows, width = own.shape
    level_f = level.astype(f32)
    lane = lane_ids(3 * TILE)
    side = turned(ends[2], level)
    parts = [lap[:, at : at + LANES] for at in range(0, width, LANES)]
    parts[0] = parts[0] + jnp.where(lane == 0, side, 0.0)
    parts[-1] = parts[-1] + jnp.where(lane == LANES - 1, side, 0.0)
    lap = jnp.concatenate(parts, axis=1)
    whole = jnp.concatenate([own, halo_level], axis=0)
    own_lap = lap[:rows]
    around_temp = sideways(own, turned(ends[0][:rows], level))
    around_temp += (roll_rows(whole, -1)[:rows], roll_rows(whole, 1)[:rows])
    around_lap = sideways(own_lap, turned(ends[1][:rows], level))
    around_lap += (roll_rows(lap, -1)[:rows], roll_rows(lap, 1)[:rows])
    change = jnp.zeros((rows, width), f32)
    for place, limit in enumerate(limits):
        moved = mixing_fourth * (own_lap - around_lap[place])
        moved = moved - speeds[place] * (around_temp[place] + own)
        change = change + jnp.where(level_f < limit, moved, 0.0)
    return base + change


def hot_body(points, hot):
    links, rows, width = points.shape
    blocks = width // LANES
    cells = row_ids(LANES).astype(f32).astype(jnp.bfloat16)
    one, none = jnp.bfloat16(1.0), jnp.bfloat16(0.0)
    for k in range(links):
        for b in range(blocks):
            for row in range(rows):
                line = points[k, row : row + 1, b * LANES : (b + 1) * LANES]
                line = jnp.broadcast_to(line.astype(f32), (2 * TILE, LANES)).astype(jnp.bfloat16)
                line = jnp.concatenate([line] * (LANES // (2 * TILE)), axis=0)
                hot[k * rows + row, :, b * LANES : (b + 1) * LANES] = jnp.transpose(
                    jnp.where(line == cells, one, none)
                )


def subcycle_body(
    levels,
    ext,
    edges_own,
    edges_halo,
    got_a,
    got_b,
    temp,
    halo,
    base,
    laps,
    hot,
    weights,
    tile_hbm,
    out_height,
    out_zonal,
    out_merid,
    limits_out,
    speeds_out,
    ends_out,
    sums_a,
    sums_b,
    sums_mid,
    whole,
    values,
    table,
    tile,
    tile_sem,
):
    tile_copy = pltpu.make_async_copy(tile_hbm, tile, tile_sem)
    tile_copy.start()
    edges = [
        jnp.concatenate([edges_own[place], edges_halo[place]], axis=0) for place in range(2)
    ]
    width = ext.shape[2]
    rows = temp.shape[1]
    lon_even = lax.rem(lax.axis_index("lon"), 2) == 0
    even = lax.rem(lax.axis_index("lat"), 2) == 0
    lane = lane_ids(3 * TILE)
    from_east = [jnp.where(lon_even, got_a[place], got_b[place]) for place in range(2)]
    from_west = [jnp.where(lon_even, got_b[place], got_a[place]) for place in range(2)]
    planes = []
    for place in range(ext.shape[0]):
        third = jnp.where(
            lane < 3,
            roll_lanes(from_east[0], -3 * place),
            jnp.where(lane >= LANES - 3, roll_lanes(from_west[0], 3 * place), 0.0),
        )
        planes.append(jnp.concatenate([ext[place], third], axis=1))
    height, zonal, merid, counts, wind_east, wind_north, fresh = planes

    def east_of(array):
        return roll_lanes(array, -1)

    def west_of(array):
        return roll_lanes(array, 1)

    def north_of(array):
        return roll_rows(array, -1)

    def south_of(array):
        return roll_rows(array, 1)

    depth = column_depth(counts, levels)
    wet = (counts > 0.5).astype(f32)
    east_wet = wet * east_of(wet)
    north_wet = wet * north_of(wet)
    east_depth = jnp.minimum(depth, east_of(depth))
    north_depth = jnp.minimum(depth, north_of(depth))
    east_pull = grav_step * east_depth
    north_pull = grav_step * north_depth
    wind_east = wind_step * wind_east
    wind_north = wind_step * wind_north
    fresh = fresh_step * fresh
    for _ in range(SUBS):
        zonal = east_wet * (zonal - east_pull * (east_of(height) - height) + wind_east)
        merid = north_wet * (merid - north_pull * (north_of(height) - height) + wind_north)
        spread = zonal - west_of(zonal) + merid - south_of(merid)
        height = height + wet * (fresh - height_step * spread)
    out_height[...] = height[:rows, :width]
    out_zonal[...] = zonal[:rows, :width]
    out_merid[...] = merid[:rows, :width]

    limit_east = jnp.minimum(counts, east_of(counts))
    limit_north = jnp.minimum(counts, north_of(counts))
    limit_west, limit_south = west_of(limit_east), south_of(limit_north)
    limits = [
        limit[:rows, :width] for limit in (limit_east, limit_west, limit_north, limit_south)
    ]
    speed_east = 0.5 * advect_coef * zonal / jnp.maximum(east_depth, depth_floor)
    speed_north = 0.5 * advect_coef * merid / jnp.maximum(north_depth, depth_floor)
    speeds = [
        speed[:rows, :width]
        for speed in (speed_east, -west_of(speed_east), speed_north, -south_of(speed_north))
    ]
    for place in range(4):
        limits_out[place] = limits[place]
        speeds_out[place] = speeds[place]

    lane_level = (lane // 2).astype(f32)
    odd_lane = (lane & 1) == 1
    far_east, far_west = from_east[1], from_west[1]

    def column(limit, at):
        return jnp.broadcast_to(limit[:, at : at + 1], (3 * TILE, LANES))

    def edge_lap(center, toward_east, toward_west, at, at_west):
        total = -4.0 * center
        for around, limit in (
            (toward_east, column(limit_east, at)),
            (toward_west, column(limit_east, at_west)),
            (north_of(center), column(limit_north, at)),
            (south_of(center), column(limit_south, at)),
        ):
            total = total + jnp.where(lane_level < limit, around, center)
        return total

    total_lanes = width + LANES
    lap_west = edge_lap(
        far_west,
        roll_lanes(edges[0], 1),
        roll_lanes(far_west, 1),
        total_lanes - 1,
        total_lanes - 2,
    )
    lap_east = edge_lap(
        far_east, roll_lanes(far_east, -1), roll_lanes(edges[1], -1), width, width - 1
    )
    side_west = far_west - roll_lanes(edges[0], 1)
    side_west = jnp.where(lane_level < column(limit_east, total_lanes - 1), side_west, 0.0)
    side_east = far_east - roll_lanes(edges[1], -1)
    side_east = jnp.where(lane_level < column(limit_east, width - 1), side_east, 0.0)
    ends = []
    for west, east in ((far_west, far_east), (lap_west, lap_east), (side_west, side_east)):
        ends.append(roll_lanes(jnp.where(odd_lane, west, east), -1))
    for place in range(3):
        ends_out[place] = ends[place]

    zero = jnp.zeros((), i32)
    top = finish_level(zero, temp[0], halo[0], base[0], laps[0], ends, limits, speeds)
    own_wet = wet[:rows, :width]
    thick = jnp.maximum(depth[:rows, :width], depth_floor)
    surface = [
        top * own_wet,
        height[:rows, :width] * own_wet,
        zonal[:rows, :width] / thick * own_wet,
        merid[:rows, :width] / thick * own_wet,
        own_wet,
    ]
    nsums = len(surface)
    values[...] = jnp.zeros(values.shape, f32)
    for place in range(nsums):
        values[:, place, :] = surface[place]
    table[...] = jnp.zeros(table.shape, f32)
    links = weights.shape[0]
    blocks = width // LANES
    tile_copy.wait()

    for row in range(rows):
        held = values[row]
        for k in range(links):
            shares = held * weights[k, row : row + 1, :]
            upper = shares.astype(jnp.bfloat16)
            lower = (shares - upper.astype(f32)).astype(jnp.bfloat16)
            both = jnp.concatenate([upper, lower], axis=0)
            stacked = jnp.concatenate(
                [both[:, b * LANES : (b + 1) * LANES] for b in range(blocks)], axis=0
            )
            found = jnp.dot(stacked, hot[k * rows + row], preferred_element_type=f32)
            for b in range(blocks):
                target = tile[k, b, row]
                mine = found[b * 2 * TILE : (b + 1) * 2 * TILE, b * LANES : (b + 1) * LANES]
                table[target] = table[target] + mine
    for place in range(nsums):
        total = table[:, place, :] + table[:, TILE + place, :]
        south, middle, north = total[:TILE], total[TILE : 2 * TILE], total[2 * TILE :]
        sums_mid[place] = middle
        sums_a[place] = jnp.where(even, north, south)
        sums_b[place] = jnp.where(even, south, north)

    run_levels(
        0,
        early_groups(levels),
        temp,
        halo,
        base,
        laps,
        limits_out,
        speeds_out,
        ends_out,
        whole,
    )


def level_step(levels):
    return math.gcd(levels, LEVELS_AT_ONCE)


def early_groups(levels):
    groups = levels // level_step(levels)
    place = lax.axis_index("lat")
    inner = jnp.where(lax.rem(place, 2) == 1, groups // 5, 0)
    return jnp.where(place == 0, groups // 2, jnp.where(place == 1, groups * 2 // 5, inner))


LAST_GROUPS = 2


def run_levels(start, stop, temp, halo, base, laps, limits, speeds, ends, out, done=None):
    step = level_step(temp.shape[0])

    def group(at, carry):
        for inner in range(step):
            level = jnp.int32(at * step + inner)
            out[level] = finish_level(
                level,
                temp[level],
                halo[level],
                base[level],
                laps[level],
                [ends[place] for place in range(3)],
                [limits[place] for place in range(4)],
                [speeds[place] for place in range(4)],
            )
        if done is not None:
            done(at)
        return carry

    lax.fori_loop(start, stop, group, 0)


def tracer_body(
    temp,
    halo,
    base,
    laps,
    limits,
    speeds,
    ends,
    draft,
    height,
    zonal,
    merid,
    out_height,
    out_zonal,
    out_merid,
    out,
    whole,
    sems,
    level_sems,
):
    levels = temp.shape[0]
    step = level_step(levels)
    groups = levels // step
    pairs = [(height, out_height), (zonal, out_zonal), (merid, out_merid)]
    copies = [
        pltpu.make_async_copy(source, target, sems.at[place])
        for place, (source, target) in enumerate(pairs)
    ]
    for copy in copies:
        copy.start()

    def level_copy(at, source=whole):
        part = pl.ds(at * step, step)
        return pltpu.make_async_copy(source.at[part], out.at[part], level_sems.at[at])

    early = early_groups(levels)

    def start(at, carry):
        level_copy(at, draft).start()
        return carry

    lax.fori_loop(0, early, start, 0)
    inside = max(groups - LAST_GROUPS, 0)
    refs = (temp, halo, base, laps, limits, speeds, ends, whole)
    run_levels(early, inside, *refs, lambda at: level_copy(at).start())
    run_levels(inside, groups, *refs)
    for at in range(inside):
        level_copy(at).wait()
    for copy in copies:
        copy.wait()


def merge_body(mid, got_a, got_b, flags, whole, draft, out, out_temp, surface, sems):
    levels = whole.shape[0]
    step = level_step(levels)
    first = step * max(levels // step - LAST_GROUPS, 0)
    part = pl.ds(first, levels - first)
    rest = pltpu.make_async_copy(whole.at[part], out_temp.at[part], sems.at[0])
    rest.start()
    open_sea = (1 - flags[...]).astype(f32)
    nsurf = out.shape[0]
    area = mid[nsurf] + got_a[nsurf] + got_b[nsurf]
    scale = open_sea / jnp.maximum(area, area_floor)
    for place in range(nsurf):
        surface[place] = (mid[place] + got_a[place] + got_b[place]) * scale
    copy = pltpu.make_async_copy(surface, out, sems.at[1])
    copy.start()
    copy.wait()
    rest.wait()


def shards(
    free_elevation,
    zonal_volume_carriage,
    meridional_volume_carriage,
    thermal_field,
    flooded_strata_number,
    aerial_exchanges,
    aerial_terrain_flags,
    donor_tile_number,
    donor_point_number,
    pairing_coefficients,
):
    levels, rows, width = thermal_field.shape
    nflux, band_rows, lanes = aerial_exchanges.shape
    links, _, blocks = donor_tile_number.shape
    assert rows == 2 * TILE and band_rows == TILE and lanes == LANES
    assert 2 * levels <= LANES and lax.axis_size("lon") % 2 == 0
    nsums = 5
    fields = 4 + 2 * links
    flux_at = fields // 2
    flux_tiles = (nflux + 2) // 2
    temp_at = flux_at + flux_tiles
    groups = pl.cdiv(levels, 4)
    tile_lines = jnp.swapaxes(donor_tile_number, 1, 2)
    temp = thermal_field
    edge_a, own, state, points, weights, flags, tile = call(
        load_body,
        [
            shape(temp_at, TILE, width),
            shape(nflux, TILE, LANES),
            shape(4, rows, width),
            shape(links, rows, width, dtype=i32),
            shape(links, rows, width),
            shape(band_rows, lanes, dtype=i32),
            shape(links, blocks, rows, dtype=i32),
        ],
        (
            free_elevation,
            zonal_volume_carriage,
            meridional_volume_carriage,
            flooded_strata_number,
            donor_point_number,
            tile_lines,
            pairing_coefficients,
            aerial_exchanges,
            aerial_terrain_flags,
        ),
        "load",
        1.6,
        scratch=[
            pltpu.VMEM((rows, width), i32),
            pltpu.VMEM((nflux, band_rows, lanes), f32),
            pltpu.SemaphoreType.DMA((9,)),
        ],
        hbm=range(9),
    )
    got_a = swap(edge_a, "lat", 0, False)
    far_tiles = (len(HALO_FLUXES) + 1) // 2
    edge_tiles = temp_at + far_tiles
    draft_b, edges, numbers = call(
        pack_second_body,
        [
            shape(edge_tiles, TILE, width),
            shape(2, rows, LANES),
            shape(2, TILE, LANES),
        ],
        (own, state, points, weights, tile, temp),
        "pack_b",
        0.3,
    )
    (edge_b,) = call(
        functools.partial(pack_flux_body, flux_at),
        [shape(edge_tiles, TILE, width)],
        (draft_b, got_a, edges),
        "pack_flux",
        0.0,
    )
    got_b = swap(edge_b, "lat", 1, False)
    (temp_b,) = call(
        functools.partial(pack_temp_body, 1),
        [shape(groups, TILE, width)],
        (temp, edge_b),
        "pack_temp_b",
        LATE,
    )
    got_temp_b = swap(temp_b, "lat", 1, False)
    (temp_a,) = call(
        functools.partial(pack_temp_body, 0),
        [shape(groups, TILE, width)],
        (temp, temp_b),
        "pack_temp_a",
        0.0,
    )
    got_temp_a = swap(temp_a, "lat", 0, False)
    (edge_c,) = call(
        functools.partial(pack_third_body, flux_at),
        [shape((len(HALO_FLUXES) + 3) // 2, TILE, width)],
        (got_b, edges, numbers),
        "pack_c",
        LATE,
    )
    got_c = swap(edge_c, "lat", 0, False)
    draft_ext, light = call(
        functools.partial(forcing_body, flux_at),
        [shape(7, 3 * TILE, width), shape(2, rows, width)],
        (got_a, got_b, own, numbers, state, points, weights),
        "forcing",
        0.4,
    )
    ext, send_a, send_b, edges_halo = call(
        functools.partial(forcing_halo_body, flux_at),
        [
            shape(7, 3 * TILE, width),
            shape(2, 3 * TILE, LANES),
            shape(2, 3 * TILE, LANES),
            shape(2, TILE, LANES),
        ],
        (draft_ext, got_a, got_b, got_c, own, edges),
        "forcing_halo",
        0.3,
    )
    lon_b = swap(send_b, "lon", 1, True)
    (send_a,) = call(
        pass_body, [shape(2, 3 * TILE, LANES)], (send_a, send_b), "pass_lon", LATE
    )
    lon_a = swap(send_a, "lon", 0, True)
    (hot,) = call(
        hot_body,
        [shape(links * rows, LANES, blocks * LANES, dtype=jnp.bfloat16)],
        (points,),
        "hot",
        0.0,
    )
    base, laps, halo = call(
        before_body,
        [
            shape(levels, rows, width),
            shape(levels, 3 * TILE, width),
            shape(levels, TILE, width),
        ],
        (ext, light, temp, got_temp_a, got_temp_b),
        "before",
        0.0,
    )
    (
        advanced_elevation,
        transport_x_next,
        transport_y_next,
        limits,
        speeds,
        ends,
        sums_a,
        sums_b,
        sums_mid,
        draft,
    ) = call(
        functools.partial(subcycle_body, levels),
        [shape(rows, width)] * 3
        + [shape(4, rows, width), shape(4, rows, width), shape(3, 3 * TILE, LANES)]
        + [shape(nsums, TILE, LANES)] * 3
        + [shape(levels, rows, width)],
        (
            ext,
            edges,
            edges_halo,
            lon_a,
            lon_b,
            temp,
            halo,
            base,
            laps,
            hot,
            weights,
            tile_lines,
        ),
        "subcycles",
        2.6,
        scratch=[
            pltpu.VMEM((rows, TILE, width), f32),
            pltpu.VMEM((3 * TILE, 2 * TILE, LANES), f32),
            pltpu.SMEM((links, blocks, rows), i32),
            pltpu.SemaphoreType.DMA(()),
        ],
        hbm=(11,),
    )
    back_b = swap(sums_b, "lat", 1, False)
    (sums_a,) = call(
        pass_body, [shape(nsums, TILE, LANES)], (sums_a, sums_b), "pass_sums", LATE
    )
    back_a = swap(sums_a, "lat", 0, False)
    advanced_elevation, transport_x_next, transport_y_next, draft_field, draft = call(
        tracer_body,
        [
            pltpu.HBM((rows, width), f32),
            pltpu.HBM((rows, width), f32),
            pltpu.HBM((rows, width), f32),
            pltpu.HBM((levels, rows, width), f32),
            shape(levels, rows, width),
        ],
        (
            temp,
            halo,
            base,
            laps,
            limits,
            speeds,
            ends,
            draft,
            advanced_elevation,
            transport_x_next,
            transport_y_next,
        ),
        "tracer",
        2.5,
        scratch=[
            pltpu.SemaphoreType.DMA((3,)),
            pltpu.SemaphoreType.DMA((levels // level_step(levels),)),
        ],
    )
    marine_skin_condition, advanced_thermal_field = call(
        merge_body,
        [
            pltpu.HBM((nsums - 1, band_rows, lanes), f32),
            pltpu.HBM((levels, rows, width), f32),
        ],
        (sums_mid, back_a, back_b, flags, draft, draft_field),
        "merge",
        0.1,
        aliases={5: 1},
        hbm=(5,),
        scratch=[
            pltpu.VMEM((nsums - 1, band_rows, lanes), f32),
            pltpu.SemaphoreType.DMA((2,)),
        ],
    )
    return (
        advanced_elevation,
        transport_x_next,
        transport_y_next,
        advanced_thermal_field,
        marine_skin_condition,
    )


def solution(mesh):
    flat = P("lat", "lon")
    deep = P(None, "lat", "lon")
    return jax.shard_map(
        shards,
        mesh=mesh,
        in_specs=(flat, flat, flat, deep, flat, deep, flat, deep, deep, deep),
        out_specs=(flat, flat, flat, deep, deep),
        check_vma=False,
    )
```

```python
import functools
import math

import jax
import jax.numpy as jnp
from jax import lax
from jax.experimental import pallas as pl
from jax.experimental.pallas import tpu as pltpu
from jax.sharding import PartitionSpec as P

SUBS = 3

grav_step = 0.6
height_step = 0.6
wind_step = 0.5
fresh_step = 0.5
mixing_fourth = 0.02
advect_coef = 0.1
diapycnal_diffusion = 0.2
heat_gain = 0.3
light_gain = 0.3
light_decay = 8.0
depth_floor = 0.25
area_floor = 1.0

TILE = 8
LANES = 128
HALF = TILE // 2

f32 = jnp.float32
i32 = jnp.int32

LATE = 4.0
FLOPS_PER_US = 1150000000


def swap_pairs(count, first, periodic):
    pairs = []
    for low in range(first, count, 2):
        high = low + 1
        if high == count:
            if not periodic:
                continue
            high = 0
        pairs += [(low, high), (high, low)]
    return pairs


def swap(array, axis, first, periodic):
    return lax.ppermute(array, axis, swap_pairs(lax.axis_size(axis), first, periodic))


def lane_ids(rows, width=LANES):
    return lax.broadcasted_iota(i32, (rows, width), 1)


def row_ids(rows, width=LANES):
    return lax.broadcasted_iota(i32, (rows, width), 0)


def roll_rows(array, by):
    by = by % array.shape[0]
    return pltpu.roll(array, by, 0) if by else array


def roll_lanes(array, by):
    by = by % array.shape[1]
    return pltpu.roll(array, by, 1) if by else array


def call(body, outs, ins, name, took, aliases=None, scratch=(), hbm=()):
    specs = [
        pl.BlockSpec(memory_space=pltpu.HBM if place in hbm else pltpu.VMEM)
        for place in range(len(ins))
    ]
    ins = [
        pltpu.with_memory_space_constraint(leaf, pltpu.HBM) if place in hbm else leaf
        for place, leaf in enumerate(ins)
    ]
    return pl.pallas_call(
        body,
        out_shape=outs,
        in_specs=specs,
        out_specs=[pl.BlockSpec(memory_space=leaf.memory_space) for leaf in outs],
        scratch_shapes=list(scratch),
        input_output_aliases=aliases or {},
        compiler_params=pltpu.CompilerParams(vmem_limit_bytes=12 * 1024 * 1024),
        cost_estimate=pl.CostEstimate(
            flops=int(took * FLOPS_PER_US), bytes_accessed=1024, transcendentals=0
        ),
        name=name,
    )(*ins)


def shape(*dims, dtype=f32):
    return pltpu.VMEM(dims, dtype)


def write_edge(top, fields, out_ref):
    sub = row_ids(TILE, out_ref.shape[2])
    mine = (sub >= HALF) == top
    for place in range(len(fields) // 2):
        first = jnp.where(top, fields[2 * place][TILE:], fields[2 * place][:TILE])
        second = jnp.where(top, fields[2 * place + 1][TILE:], fields[2 * place + 1][:TILE])
        out_ref[place] = jnp.where(mine, first, roll_rows(second, HALF))


def write_planes(planes, out_ref, at):
    planes = planes + [planes[-1]] * (len(planes) % 2)
    for place in range(len(planes) // 2):
        out_ref[at + place] = jnp.concatenate(planes[2 * place : 2 * place + 2], axis=1)


def edge_numbers(top, numbers):
    return jnp.where(top, numbers[1], numbers[0])


def write_temp_edge(top, temp_ref, out_ref, at):
    levels, _, width = temp_ref.shape
    sub = row_ids(TILE, width)
    for group in range(pl.cdiv(levels, 4)):
        packed = jnp.zeros((TILE, width), f32)
        for spot in range(min(4, levels - 4 * group)):
            level = 4 * group + spot
            low = roll_rows(temp_ref[level, :TILE, :], 2 * spot)
            high = roll_rows(temp_ref[level, TILE:, :], 2 * spot + 2)
            packed = jnp.where(sub // 2 == spot, jnp.where(top, high, low), packed)
        out_ref[at + group] = packed


def goes_north(first):
    return (lax.rem(lax.axis_index("lat"), 2) == 0) == (first == 0)


def edge_fields(state, points, weights):
    links = points.shape[0]
    fields = [state[place] for place in range(4)]
    fields += [points[k].astype(f32) for k in range(links)]
    fields += [weights[k] for k in range(links)]
    return fields


def load_body(
    height,
    zonal,
    merid,
    counts,
    points,
    tile,
    weights,
    flux,
    flags,
    edge,
    own,
    state_out,
    points_out,
    weights_out,
    flags_out,
    tile_out,
    counts_in,
    flux_in,
    sems,
):
    pairs = [
        (flux, flux_in),
        (flags, flags_out),
        (tile, tile_out),
        (counts, counts_in),
        (height, state_out.at[0]),
        (zonal, state_out.at[1]),
        (merid, state_out.at[2]),
        (points, points_out),
        (weights, weights_out),
    ]
    copies = [
        pltpu.make_async_copy(source, target, sems.at[place])
        for place, (source, target) in enumerate(pairs)
    ]
    for copy in copies:
        copy.start()
    for copy in copies:
        copy.wait()
    state_out[3] = counts_in[...].astype(f32)
    open_sea = (1 - flags_out[...]).astype(f32)
    masked = [flux_in[plane] * open_sea for plane in range(flux.shape[0])]
    for plane, values in enumerate(masked):
        own[plane] = values
    top = goes_north(0)
    fields = edge_fields(state_out, points_out, weights_out)
    write_edge(top, fields, edge)
    write_planes(masked[:1] + masked, edge, len(fields) // 2)


def pack_second_body(own, state, points, weights, tile, temp, draft, edges, numbers):
    top = goes_north(1)
    fields = edge_fields(state, points, weights)
    write_edge(top, fields, draft)
    links, blocks, rows = tile.shape
    lane = lane_ids(rows)
    diagonal = row_ids(rows, rows) == lane_ids(rows, rows)
    tiles = jnp.zeros((rows, LANES), f32)
    for k in range(links):
        for b in range(blocks):
            line = jnp.broadcast_to(tile[k, b : b + 1, :].astype(f32), (rows, rows))
            upright = jnp.sum(jnp.where(diagonal, line, 0.0), axis=1, keepdims=True)
            tiles = jnp.where(lane == k * blocks + b, upright, tiles)
    numbers[0] = tiles[:TILE]
    numbers[1] = tiles[TILE:]
    masked = [own[plane] for plane in range(own.shape[0])]
    write_planes([edge_numbers(top, numbers)] + masked, draft, len(fields) // 2)
    levels, rows, _ = temp.shape
    for place, columns in enumerate(edge_columns([temp[level] for level in range(levels)], rows)):
        edges[place] = columns


def corner_plane(top, edges):
    west = jnp.where(top, edges[0, TILE:, :], edges[0, :TILE, :])
    east = jnp.where(top, edges[1, TILE:, :], edges[1, :TILE, :])
    return jnp.where((row_ids(TILE) >= HALF) == top, west, roll_rows(east, HALF))


def far_planes(flux_at, received):
    return [spot_of(received, flux_at, 1 + plane) for plane in HALO_FLUXES]


def pack_flux_body(flux_at, draft, received, edges, out):
    planes = far_planes(flux_at, received) + [corner_plane(goes_north(1), edges)]
    at = out.shape[0] - len(planes) // 2
    out[:at] = draft[:at]
    write_planes(planes, out, at)


def edge_columns(fields, rows):
    lane = lane_ids(rows)
    high = jnp.zeros((rows, LANES), f32)
    low = jnp.zeros((rows, LANES), f32)
    for level, field in enumerate(fields):
        ends = jnp.where(lane < HALF, field[:, :LANES], field[:, -LANES:])
        turned = roll_lanes(ends, 2 * level + 2)
        high = jnp.where(lane // 2 == level, turned, high)
        low = jnp.where(lane // 2 == (level + 1) % (LANES // 2), turned, low)
    return roll_lanes(low, -2), high


HALO_FLUXES = (0, 1, 4)


def pass_body(first, second, out):
    out[...] = first[...]


def pack_temp_body(first, temp, other, out):
    write_temp_edge(goes_north(first), temp, out, 0)


def pack_third_body(flux_at, received, edges, numbers, out):
    top = goes_north(0)
    planes = far_planes(flux_at, received)
    write_planes(planes + [corner_plane(top, edges), edge_numbers(top, numbers)], out, 0)


def unpack_rows(top, packed, level):
    spot = level % 4
    return jnp.where(top, roll_rows(packed, -2 * spot), roll_rows(packed, 6 - 2 * spot))


def near_lanes(width):
    return (row_ids(TILE, width) < HALF) == (lax.rem(lax.axis_index("lat"), 2) == 0)


def pick(array, rows):
    return jnp.take_along_axis(array, rows, axis=0, mode="promise_in_bounds")


def pick_lane(array, lanes):
    return jnp.take_along_axis(array, lanes, axis=1, mode="promise_in_bounds")


def spot_of(array, flux_at, place):
    return array[flux_at + place // 2, :, (place % 2) * LANES : (place % 2 + 1) * LANES]


def by_side(even, one, two):
    return jnp.where(even, one, two), jnp.where(even, two, one)


def row_numbers(numbers, column):
    number = jnp.broadcast_to(numbers[:, column : column + 1].astype(i32), (TILE, LANES))
    return number & (TILE - 1), lax.shift_right_logical(number, 3)


FORCING_AT = {0: 4, 1: 5, 4: 6}


def forcing_body(flux_at, got_a, got_b, own, numbers, state, points, weights, ext, light):
    even = lax.rem(lax.axis_index("lat"), 2) == 0
    links, rows, width = points.shape
    blocks = width // LANES
    nflux = own.shape[0]
    ext[:4, :rows, :] = state[...]
    north, south = [], []
    for plane in range(nflux):
        one, two = spot_of(got_a, flux_at, 1 + plane), spot_of(got_b, flux_at, 1 + plane)
        high, low = by_side(even, one, two)
        north.append(high)
        south.append(low)
    mid = [own[plane] for plane in range(nflux)]
    for row_tile in range(rows // TILE):
        here = slice(row_tile * TILE, (row_tile + 1) * TILE)
        for b in range(blocks):
            cols = slice(b * LANES, (b + 1) * LANES)
            totals = [jnp.zeros((TILE, LANES), f32) for _ in range(nflux)]
            for k in range(links):
                within, band = row_numbers(numbers[row_tile], k * blocks + b)
                lanes = points[k, here, cols]
                weight = weights[k, here, cols]
                for plane in range(nflux):
                    value = jnp.where(
                        band == 0,
                        pick(south[plane], within),
                        jnp.where(band == 1, pick(mid[plane], within), pick(north[plane], within)),
                    )
                    totals[plane] = totals[plane] + weight * pick_lane(value, lanes)
            for plane in range(nflux):
                if plane in FORCING_AT:
                    ext[FORCING_AT[plane], here, cols] = totals[plane]
                else:
                    light[plane - 2, here, cols] = totals[plane]


def both_fields(even, near, far):
    north, south = by_side(even, near, far)
    sub = row_ids(*near.shape)
    return [
        jnp.where(sub < HALF, north, south),
        roll_rows(jnp.where(sub < HALF, south, north), HALF),
    ]


def forcing_halo_body(
    flux_at,
    draft,
    got_a,
    got_b,
    got_c,
    own,
    edges,
    ext,
    send_a,
    send_b,
    edges_halo,
):
    even = lax.rem(lax.axis_index("lat"), 2) == 0
    rows, width = 2 * TILE, ext.shape[2]
    blocks = width // LANES
    links = flux_at - 2
    halos = []
    for place in range(flux_at):
        halos += both_fields(even, got_a[place], got_b[place])
    ext[:, :rows, :] = draft[:, :rows, :]
    for place in range(4):
        ext[place, rows:, :] = halos[place]
    tables = {}
    far_at = got_b.shape[0] - (len(HALO_FLUXES) + 1) // 2
    for place, plane in enumerate(HALO_FLUXES):
        one, two = spot_of(got_a, flux_at, 1 + plane), spot_of(got_b, flux_at, 1 + plane)
        north, south = by_side(even, one, two)
        far_north, far_south = by_side(
            even, spot_of(got_c, 0, place), spot_of(got_b, far_at, place)
        )
        tables[plane] = [far_south, south, own[plane], north, far_north]
    sub_one = row_ids(TILE)
    north, south = by_side(
        even, spot_of(got_c, 0, len(HALO_FLUXES) + 1), spot_of(got_b, flux_at, 0)
    )
    numbers = jnp.where(sub_one < HALF, north, south)
    for b in range(blocks):
        cols = slice(b * LANES, (b + 1) * LANES)
        totals = {plane: jnp.zeros((TILE, LANES), f32) for plane in HALO_FLUXES}
        for k in range(links):
            within, band = row_numbers(numbers, k * blocks + b)
            band = band + jnp.where(sub_one < HALF, 2, 0)
            lanes = halos[4 + k][:, cols].astype(i32)
            weight = halos[4 + links + k][:, cols]
            for plane in HALO_FLUXES:
                value = pick(tables[plane][0], within)
                for at in range(1, 5):
                    value = jnp.where(band == at, pick(tables[plane][at], within), value)
                totals[plane] = totals[plane] + weight * pick_lane(value, lanes)
        for plane in HALO_FLUXES:
            ext[FORCING_AT[plane], rows:, cols] = totals[plane]

    lane = lane_ids(3 * TILE)
    to_west = jnp.zeros((3 * TILE, LANES), f32)
    to_east = jnp.zeros((3 * TILE, LANES), f32)
    for place in range(ext.shape[0]):
        low = roll_lanes(ext[place, :, :LANES], 3 * place)
        high = roll_lanes(ext[place, :, width - LANES :], -3 * place)
        to_west = jnp.where((lane >= 3 * place) & (lane < 3 * place + 3), low, to_west)
        edge = LANES - 3 * place
        to_east = jnp.where((lane >= edge - 3) & (lane < edge), high, to_east)
    corner = len(HALO_FLUXES)
    corners = both_fields(even, spot_of(got_c, 0, corner), spot_of(got_b, far_at, corner))
    for place in range(2):
        edges_halo[place] = corners[place]
    lon_even = lax.rem(lax.axis_index("lon"), 2) == 0
    send_a[0] = jnp.where(lon_even, to_east, to_west)
    send_b[0] = jnp.where(lon_even, to_west, to_east)
    for part, columns in ((slice(0, rows), edges), (slice(rows, rows + TILE), edges_halo)):
        send_a[1, part, :] = jnp.where(lon_even, columns[1], columns[0])
        send_b[1, part, :] = jnp.where(lon_even, columns[0], columns[1])


def column_depth(counts, levels):
    scale = 1.0 / (2.0 * levels)
    return counts * scale + counts * (counts - 1.0) * (scale / levels)


def sideways(array, ends):
    rows, width = array.shape
    lane = lane_ids(rows)
    parts = [array[:, at : at + LANES] for at in range(0, width, LANES)]
    right = [roll_lanes(part, -1) for part in parts] + [ends]
    left = [ends] + [roll_lanes(part, 1) for part in parts]
    east = [jnp.where(lane == LANES - 1, b, a) for a, b in zip(right, right[1:])]
    west = [jnp.where(lane == 0, a, b) for a, b in zip(left, left[1:])]
    return jnp.concatenate(east, axis=1), jnp.concatenate(west, axis=1)


def turned(ends, level):
    return pltpu.roll(ends, lax.rem(2 * LANES - 2 * level, LANES), 1)


LEVELS_AT_ONCE = 6
LEVELS_BEFORE = 10


def before_body(ext, light, temp, got_a, got_b, base, laps, halo):
    levels, rows, width = temp.shape
    counts = ext[3]
    own_counts = counts[:rows]
    lane = lane_ids(3 * TILE, width)
    limit_east = jnp.where(lane == width - 1, 0.0, jnp.minimum(counts, roll_lanes(counts, -1)))
    limit_north = jnp.minimum(counts, roll_rows(counts, -1))
    limits = (limit_east, roll_lanes(limit_east, 1), limit_north, roll_rows(limit_north, 1))
    step = math.gcd(levels, LEVELS_BEFORE)
    odd = lax.rem(lax.axis_index("lat"), 2) == 1
    near = near_lanes(width)
    for level in range(levels):
        rows_near = unpack_rows(jnp.logical_not(odd), got_a[level // 4], level)
        rows_far = unpack_rows(odd, got_b[level // 4], level)
        halo[level] = jnp.where(near, rows_near, rows_far)

    def group(at, down_before):
        for inner in range(step):
            level = at * step + inner
            level_f = level.astype(f32)
            own = temp[level]
            whole = jnp.concatenate([own, halo[level]], axis=0)
            east, west = sideways(whole, whole[:, :LANES])
            lap = -4.0 * whole
            for around, limit in zip(
                (east, west, roll_rows(whole, -1), roll_rows(whole, 1)), limits
            ):
                lap = lap + jnp.where(level_f < limit, around, whole)
            laps[level] = lap
            beneath = temp[jnp.minimum(level + 1, levels - 1)]
            down = jnp.where(level_f + 1.0 < own_counts, beneath - own, 0.0)
            absorb = jnp.exp(jnp.full(own.shape, -1.0 / light_decay, f32) * level_f)
            absorb = absorb * (light_gain * (1.0 - math.exp(-1.0 / light_decay)))
            source = absorb * light[1] + jnp.where(level == 0, heat_gain, 0.0) * light[0]
            change = diapycnal_diffusion * (down - down_before) + source
            base[level] = own + jnp.where(level_f < own_counts, change, 0.0)
            down_before = down
        return down_before

    lax.fori_loop(0, levels // step, group, jnp.zeros((rows, width), f32))


def finish_level(level, own, halo_level, base, lap, ends, limits, speeds):
    rows, width = own.shape
    level_f = level.astype(f32)
    lane = lane_ids(3 * TILE)
    side = turned(ends[2], level)
    parts = [lap[:, at : at + LANES] for at in range(0, width, LANES)]
    parts[0] = parts[0] + jnp.where(lane == 0, side, 0.0)
    parts[-1] = parts[-1] + jnp.where(lane == LANES - 1, side, 0.0)
    lap = jnp.concatenate(parts, axis=1)
    whole = jnp.concatenate([own, halo_level], axis=0)
    own_lap = lap[:rows]
    around_temp = sideways(own, turned(ends[0][:rows], level))
    around_temp += (roll_rows(whole, -1)[:rows], roll_rows(whole, 1)[:rows])
    around_lap = sideways(own_lap, turned(ends[1][:rows], level))
    around_lap += (roll_rows(lap, -1)[:rows], roll_rows(lap, 1)[:rows])
    change = jnp.zeros((rows, width), f32)
    for place, limit in enumerate(limits):
        moved = mixing_fourth * (own_lap - around_lap[place])
        moved = moved - speeds[place] * (around_temp[place] + own)
        change = change + jnp.where(level_f < limit, moved, 0.0)
    return base + change


def hot_body(points, hot):
    links, rows, width = points.shape
    blocks = width // LANES
    cells = row_ids(LANES).astype(f32).astype(jnp.bfloat16)
    one, none = jnp.bfloat16(1.0), jnp.bfloat16(0.0)
    for k in range(links):
        for b in range(blocks):
            for row in range(rows):
                line = points[k, row : row + 1, b * LANES : (b + 1) * LANES]
                line = jnp.broadcast_to(line.astype(f32), (2 * TILE, LANES)).astype(jnp.bfloat16)
                line = jnp.concatenate([line] * (LANES // (2 * TILE)), axis=0)
                hot[k * rows + row, :, b * LANES : (b + 1) * LANES] = jnp.transpose(
                    jnp.where(line == cells, one, none)
                )


def subcycle_body(
    levels,
    ext,
    edges_own,
    edges_halo,
    got_a,
    got_b,
    temp,
    halo,
    base,
    laps,
    hot,
    weights,
    tile_hbm,
    out_height,
    out_zonal,
    out_merid,
    limits_out,
    speeds_out,
    ends_out,
    sums_a,
    sums_b,
    sums_mid,
    whole,
    values,
    table,
    tile,
    tile_sem,
):
    tile_copy = pltpu.make_async_copy(tile_hbm, tile, tile_sem)
    tile_copy.start()
    edges = [
        jnp.concatenate([edges_own[place], edges_halo[place]], axis=0) for place in range(2)
    ]
    width = ext.shape[2]
    rows = temp.shape[1]
    lon_even = lax.rem(lax.axis_index("lon"), 2) == 0
    even = lax.rem(lax.axis_index("lat"), 2) == 0
    lane = lane_ids(3 * TILE)
    from_east = [jnp.where(lon_even, got_a[place], got_b[place]) for place in range(2)]
    from_west = [jnp.where(lon_even, got_b[place], got_a[place]) for place in range(2)]
    planes = []
    for place in range(ext.shape[0]):
        third = jnp.where(
            lane < 3,
            roll_lanes(from_east[0], -3 * place),
            jnp.where(lane >= LANES - 3, roll_lanes(from_west[0], 3 * place), 0.0),
        )
        planes.append(jnp.concatenate([ext[place], third], axis=1))
    height, zonal, merid, counts, wind_east, wind_north, fresh = planes

    def east_of(array):
        return roll_lanes(array, -1)

    def west_of(array):
        return roll_lanes(array, 1)

    def north_of(array):
        return roll_rows(array, -1)

    def south_of(array):
        return roll_rows(array, 1)

    depth = column_depth(counts, levels)
    wet = (counts > 0.5).astype(f32)
    east_wet = wet * east_of(wet)
    north_wet = wet * north_of(wet)
    east_depth = jnp.minimum(depth, east_of(depth))
    north_depth = jnp.minimum(depth, north_of(depth))
    east_pull = grav_step * east_depth
    north_pull = grav_step * north_depth
    wind_east = wind_step * wind_east
    wind_north = wind_step * wind_north
    fresh = fresh_step * fresh
    for _ in range(SUBS):
        zonal = east_wet * (zonal - east_pull * (east_of(height) - height) + wind_east)
        merid = north_wet * (merid - north_pull * (north_of(height) - height) + wind_north)
        spread = zonal - west_of(zonal) + merid - south_of(merid)
        height = height + wet * (fresh - height_step * spread)
    out_height[...] = height[:rows, :width]
    out_zonal[...] = zonal[:rows, :width]
    out_merid[...] = merid[:rows, :width]

    limit_east = jnp.minimum(counts, east_of(counts))
    limit_north = jnp.minimum(counts, north_of(counts))
    limit_west, limit_south = west_of(limit_east), south_of(limit_north)
    limits = [
        limit[:rows, :width] for limit in (limit_east, limit_west, limit_north, limit_south)
    ]
    speed_east = 0.5 * advect_coef * zonal / jnp.maximum(east_depth, depth_floor)
    speed_north = 0.5 * advect_coef * merid / jnp.maximum(north_depth, depth_floor)
    speeds = [
        speed[:rows, :width]
        for speed in (speed_east, -west_of(speed_east), speed_north, -south_of(speed_north))
    ]
    for place in range(4):
        limits_out[place] = limits[place]
        speeds_out[place] = speeds[place]

    lane_level = (lane // 2).astype(f32)
    odd_lane = (lane & 1) == 1
    far_east, far_west = from_east[1], from_west[1]

    def column(limit, at):
        return jnp.broadcast_to(limit[:, at : at + 1], (3 * TILE, LANES))

    def edge_lap(center, toward_east, toward_west, at, at_west):
        total = -4.0 * center
        for around, limit in (
            (toward_east, column(limit_east, at)),
            (toward_west, column(limit_east, at_west)),
            (north_of(center), column(limit_north, at)),
            (south_of(center), column(limit_south, at)),
        ):
            total = total + jnp.where(lane_level < limit, around, center)
        return total

    total_lanes = width + LANES
    lap_west = edge_lap(
        far_west,
        roll_lanes(edges[0], 1),
        roll_lanes(far_west, 1),
        total_lanes - 1,
        total_lanes - 2,
    )
    lap_east = edge_lap(
        far_east, roll_lanes(far_east, -1), roll_lanes(edges[1], -1), width, width - 1
    )
    side_west = far_west - roll_lanes(edges[0], 1)
    side_west = jnp.where(lane_level < column(limit_east, total_lanes - 1), side_west, 0.0)
    side_east = far_east - roll_lanes(edges[1], -1)
    side_east = jnp.where(lane_level < column(limit_east, width - 1), side_east, 0.0)
    ends = []
    for west, east in ((far_west, far_east), (lap_west, lap_east), (side_west, side_east)):
        ends.append(roll_lanes(jnp.where(odd_lane, west, east), -1))
    for place in range(3):
        ends_out[place] = ends[place]

    zero = jnp.zeros((), i32)
    top = finish_level(zero, temp[0], halo[0], base[0], laps[0], ends, limits, speeds)
    own_wet = wet[:rows, :width]
    thick = jnp.maximum(depth[:rows, :width], depth_floor)
    surface = [
        top * own_wet,
        height[:rows, :width] * own_wet,
        zonal[:rows, :width] / thick * own_wet,
        merid[:rows, :width] / thick * own_wet,
        own_wet,
    ]
    nsums = len(surface)
    values[...] = jnp.zeros(values.shape, f32)
    for place in range(nsums):
        values[:, place, :] = surface[place]
    table[...] = jnp.zeros(table.shape, f32)
    links = weights.shape[0]
    blocks = width // LANES
    tile_copy.wait()

    for row in range(rows):
        held = values[row]
        for k in range(links):
            shares = held * weights[k, row : row + 1, :]
            upper = shares.astype(jnp.bfloat16)
            lower = (shares - upper.astype(f32)).astype(jnp.bfloat16)
            both = jnp.concatenate([upper, lower], axis=0)
            stacked = jnp.concatenate(
                [both[:, b * LANES : (b + 1) * LANES] for b in range(blocks)], axis=0
            )
            found = jnp.dot(stacked, hot[k * rows + row], preferred_element_type=f32)
            for b in range(blocks):
                target = tile[k, b, row]
                mine = found[b * 2 * TILE : (b + 1) * 2 * TILE, b * LANES : (b + 1) * LANES]
                table[target] = table[target] + mine
    for place in range(nsums):
        total = table[:, place, :] + table[:, TILE + place, :]
        south, middle, north = total[:TILE], total[TILE : 2 * TILE], total[2 * TILE :]
        sums_mid[place] = middle
        sums_a[place] = jnp.where(even, north, south)
        sums_b[place] = jnp.where(even, south, north)

    run_levels(
        0,
        early_groups(levels),
        temp,
        halo,
        base,
        laps,
        limits_out,
        speeds_out,
        ends_out,
        whole,
    )


def level_step(levels):
    return math.gcd(levels, LEVELS_AT_ONCE)


def early_groups(levels):
    groups = levels // level_step(levels)
    place = lax.axis_index("lat")
    inner = jnp.where(lax.rem(place, 2) == 1, groups // 5, 0)
    return jnp.where(place == 0, groups // 2, jnp.where(place == 1, groups * 2 // 5, inner))


LAST_GROUPS = 2


def run_levels(start, stop, temp, halo, base, laps, limits, speeds, ends, out, done=None):
    step = level_step(temp.shape[0])

    def group(at, carry):
        for inner in range(step):
            level = jnp.int32(at * step + inner)
            out[level] = finish_level(
                level,
                temp[level],
                halo[level],
                base[level],
                laps[level],
                [ends[place] for place in range(3)],
                [limits[place] for place in range(4)],
                [speeds[place] for place in range(4)],
            )
        if done is not None:
            done(at)
        return carry

    lax.fori_loop(start, stop, group, 0)


def tracer_body(
    temp,
    halo,
    base,
    laps,
    limits,
    speeds,
    ends,
    draft,
    height,
    zonal,
    merid,
    out_height,
    out_zonal,
    out_merid,
    out,
    whole,
    sems,
    level_sems,
):
    levels = temp.shape[0]
    step = level_step(levels)
    groups = levels // step
    pairs = [(height, out_height), (zonal, out_zonal), (merid, out_merid)]
    copies = [
        pltpu.make_async_copy(source, target, sems.at[place])
        for place, (source, target) in enumerate(pairs)
    ]
    for copy in copies:
        copy.start()

    def level_copy(at, source=whole):
        part = pl.ds(at * step, step)
        return pltpu.make_async_copy(source.at[part], out.at[part], level_sems.at[at])

    early = early_groups(levels)

    def start(at, carry):
        level_copy(at, draft).start()
        return carry

    lax.fori_loop(0, early, start, 0)
    inside = max(groups - LAST_GROUPS, 0)
    refs = (temp, halo, base, laps, limits, speeds, ends, whole)
    run_levels(early, inside, *refs, lambda at: level_copy(at).start())
    run_levels(inside, groups, *refs)
    for at in range(inside):
        level_copy(at).wait()
    for copy in copies:
        copy.wait()


def merge_body(mid, got_a, got_b, flags, whole, draft, out, out_temp, surface, sems):
    levels = whole.shape[0]
    step = level_step(levels)
    first = step * max(levels // step - LAST_GROUPS, 0)
    part = pl.ds(first, levels - first)
    rest = pltpu.make_async_copy(whole.at[part], out_temp.at[part], sems.at[0])
    rest.start()
    open_sea = (1 - flags[...]).astype(f32)
    nsurf = out.shape[0]
    area = mid[nsurf] + got_a[nsurf] + got_b[nsurf]
    scale = open_sea / jnp.maximum(area, area_floor)
    for place in range(nsurf):
        surface[place] = (mid[place] + got_a[place] + got_b[place]) * scale
    copy = pltpu.make_async_copy(surface, out, sems.at[1])
    copy.start()
    copy.wait()
    rest.wait()


def shards(
    free_elevation,
    zonal_volume_carriage,
    meridional_volume_carriage,
    thermal_field,
    flooded_strata_number,
    aerial_exchanges,
    aerial_terrain_flags,
    donor_tile_number,
    donor_point_number,
    pairing_coefficients,
):
    levels, rows, width = thermal_field.shape
    nflux, band_rows, lanes = aerial_exchanges.shape
    links, _, blocks = donor_tile_number.shape
    assert rows == 2 * TILE and band_rows == TILE and lanes == LANES
    assert 2 * levels <= LANES and lax.axis_size("lon") % 2 == 0
    nsums = 5
    fields = 4 + 2 * links
    flux_at = fields // 2
    flux_tiles = (nflux + 2) // 2
    temp_at = flux_at + flux_tiles
    groups = pl.cdiv(levels, 4)
    tile_lines = jnp.swapaxes(donor_tile_number, 1, 2)
    temp = thermal_field
    edge_a, own, state, points, weights, flags, tile = call(
        load_body,
        [
            shape(temp_at, TILE, width),
            shape(nflux, TILE, LANES),
            shape(4, rows, width),
            shape(links, rows, width, dtype=i32),
            shape(links, rows, width),
            shape(band_rows, lanes, dtype=i32),
            shape(links, blocks, rows, dtype=i32),
        ],
        (
            free_elevation,
            zonal_volume_carriage,
            meridional_volume_carriage,
            flooded_strata_number,
            donor_point_number,
            tile_lines,
            pairing_coefficients,
            aerial_exchanges,
            aerial_terrain_flags,
        ),
        "load",
        1.6,
        scratch=[
            pltpu.VMEM((rows, width), i32),
            pltpu.VMEM((nflux, band_rows, lanes), f32),
            pltpu.SemaphoreType.DMA((9,)),
        ],
        hbm=range(9),
    )
    got_a = swap(edge_a, "lat", 0, False)
    far_tiles = (len(HALO_FLUXES) + 1) // 2
    edge_tiles = temp_at + far_tiles
    draft_b, edges, numbers = call(
        pack_second_body,
        [
            shape(edge_tiles, TILE, width),
            shape(2, rows, LANES),
            shape(2, TILE, LANES),
        ],
        (own, state, points, weights, tile, temp),
        "pack_b",
        0.3,
    )
    (edge_b,) = call(
        functools.partial(pack_flux_body, flux_at),
        [shape(edge_tiles, TILE, width)],
        (draft_b, got_a, edges),
        "pack_flux",
        0.0,
    )
    got_b = swap(edge_b, "lat", 1, False)
    (temp_b,) = call(
        functools.partial(pack_temp_body, 1),
        [shape(groups, TILE, width)],
        (temp, edge_b),
        "pack_temp_b",
        LATE,
    )
    got_temp_b = swap(temp_b, "lat", 1, False)
    (temp_a,) = call(
        functools.partial(pack_temp_body, 0),
        [shape(groups, TILE, width)],
        (temp, temp_b),
        "pack_temp_a",
        0.0,
    )
    got_temp_a = swap(temp_a, "lat", 0, False)
    (edge_c,) = call(
        functools.partial(pack_third_body, flux_at),
        [shape((len(HALO_FLUXES) + 3) // 2, TILE, width)],
        (got_b, edges, numbers),
        "pack_c",
        LATE,
    )
    got_c = swap(edge_c, "lat", 0, False)
    draft_ext, light = call(
        functools.partial(forcing_body, flux_at),
        [shape(7, 3 * TILE, width), shape(2, rows, width)],
        (got_a, got_b, own, numbers, state, points, weights),
        "forcing",
        0.4,
    )
    ext, send_a, send_b, edges_halo = call(
        functools.partial(forcing_halo_body, flux_at),
        [
            shape(7, 3 * TILE, width),
            shape(2, 3 * TILE, LANES),
            shape(2, 3 * TILE, LANES),
            shape(2, TILE, LANES),
        ],
        (draft_ext, got_a, got_b, got_c, own, edges),
        "forcing_halo",
        0.3,
    )
    lon_b = swap(send_b, "lon", 1, True)
    (send_a,) = call(
        pass_body, [shape(2, 3 * TILE, LANES)], (send_a, send_b), "pass_lon", LATE
    )
    lon_a = swap(send_a, "lon", 0, True)
    (hot,) = call(
        hot_body,
        [shape(links * rows, LANES, blocks * LANES, dtype=jnp.bfloat16)],
        (points,),
        "hot",
        0.0,
    )
    base, laps, halo = call(
        before_body,
        [
            shape(levels, rows, width),
            shape(levels, 3 * TILE, width),
            shape(levels, TILE, width),
        ],
        (ext, light, temp, got_temp_a, got_temp_b),
        "before",
        0.0,
    )
    (
        advanced_elevation,
        transport_x_next,
        transport_y_next,
        limits,
        speeds,
        ends,
        sums_a,
        sums_b,
        sums_mid,
        draft,
    ) = call(
        functools.partial(subcycle_body, levels),
        [shape(rows, width)] * 3
        + [shape(4, rows, width), shape(4, rows, width), shape(3, 3 * TILE, LANES)]
        + [shape(nsums, TILE, LANES)] * 3
        + [shape(levels, rows, width)],
        (
            ext,
            edges,
            edges_halo,
            lon_a,
            lon_b,
            temp,
            halo,
            base,
            laps,
            hot,
            weights,
            tile_lines,
        ),
        "subcycles",
        2.6,
        scratch=[
            pltpu.VMEM((rows, TILE, width), f32),
            pltpu.VMEM((3 * TILE, 2 * TILE, LANES), f32),
            pltpu.SMEM((links, blocks, rows), i32),
            pltpu.SemaphoreType.DMA(()),
        ],
        hbm=(11,),
    )
    back_b = swap(sums_b, "lat", 1, False)
    (sums_a,) = call(
        pass_body, [shape(nsums, TILE, LANES)], (sums_a, sums_b), "pass_sums", LATE
    )
    back_a = swap(sums_a, "lat", 0, False)
    advanced_elevation, transport_x_next, transport_y_next, draft_field, draft = call(
        tracer_body,
        [
            pltpu.HBM((rows, width), f32),
            pltpu.HBM((rows, width), f32),
            pltpu.HBM((rows, width), f32),
            pltpu.HBM((levels, rows, width), f32),
            shape(levels, rows, width),
        ],
        (
            temp,
            halo,
            base,
            laps,
            limits,
            speeds,
            ends,
            draft,
            advanced_elevation,
            transport_x_next,
            transport_y_next,
        ),
        "tracer",
        2.5,
        scratch=[
            pltpu.SemaphoreType.DMA((3,)),
            pltpu.SemaphoreType.DMA((levels // level_step(levels),)),
        ],
    )
    marine_skin_condition, advanced_thermal_field = call(
        merge_body,
        [
            pltpu.HBM((nsums - 1, band_rows, lanes), f32),
            pltpu.HBM((levels, rows, width), f32),
        ],
        (sums_mid, back_a, back_b, flags, draft, draft_field),
        "merge",
        0.1,
        aliases={5: 1},
        hbm=(5,),
        scratch=[
            pltpu.VMEM((nsums - 1, band_rows, lanes), f32),
            pltpu.SemaphoreType.DMA((2,)),
        ],
    )
    return (
        advanced_elevation,
        transport_x_next,
        transport_y_next,
        advanced_thermal_field,
        marine_skin_condition,
    )


def solution(mesh):
    flat = P("lat", "lon")
    deep = P(None, "lat", "lon")
    return jax.shard_map(
        shards,
        mesh=mesh,
        in_specs=(flat, flat, flat, deep, flat, deep, flat, deep, deep, deep),
        out_specs=(flat, flat, flat, deep, deep),
        check_vma=False,
    )
```

```python
import functools
import math

import jax
import jax.numpy as jnp
from jax import lax
from jax.experimental import pallas as pl
from jax.experimental.pallas import tpu as pltpu
from jax.sharding import PartitionSpec as P

SUBS = 3

grav_step = 0.6
height_step = 0.6
wind_step = 0.5
fresh_step = 0.5
mixing_fourth = 0.02
advect_coef = 0.1
diapycnal_diffusion = 0.2
heat_gain = 0.3
light_gain = 0.3
light_decay = 8.0
depth_floor = 0.25
area_floor = 1.0

TILE = 8
LANES = 128
HALF = TILE // 2

f32 = jnp.float32
i32 = jnp.int32

LATE = 4.0
FLOPS_PER_US = 1150000000


def swap_pairs(count, first, periodic):
    pairs = []
    for low in range(first, count, 2):
        high = low + 1
        if high == count:
            if not periodic:
                continue
            high = 0
        pairs += [(low, high), (high, low)]
    return pairs


def swap(array, axis, first, periodic):
    return lax.ppermute(array, axis, swap_pairs(lax.axis_size(axis), first, periodic))


def lane_ids(rows, width=LANES):
    return lax.broadcasted_iota(i32, (rows, width), 1)


def row_ids(rows, width=LANES):
    return lax.broadcasted_iota(i32, (rows, width), 0)


def roll_rows(array, by):
    by = by % array.shape[0]
    return pltpu.roll(array, by, 0) if by else array


def roll_lanes(array, by):
    by = by % array.shape[1]
    return pltpu.roll(array, by, 1) if by else array


def call(body, outs, ins, name, took, aliases=None, scratch=(), hbm=()):
    specs = [
        pl.BlockSpec(memory_space=pltpu.HBM if place in hbm else pltpu.VMEM)
        for place in range(len(ins))
    ]
    ins = [
        pltpu.with_memory_space_constraint(leaf, pltpu.HBM) if place in hbm else leaf
        for place, leaf in enumerate(ins)
    ]
    return pl.pallas_call(
        body,
        out_shape=outs,
        in_specs=specs,
        out_specs=[pl.BlockSpec(memory_space=leaf.memory_space) for leaf in outs],
        scratch_shapes=list(scratch),
        input_output_aliases=aliases or {},
        compiler_params=pltpu.CompilerParams(vmem_limit_bytes=12 * 1024 * 1024),
        cost_estimate=pl.CostEstimate(
            flops=int(took * FLOPS_PER_US), bytes_accessed=1024, transcendentals=0
        ),
        name=name,
    )(*ins)


def shape(*dims, dtype=f32):
    return pltpu.VMEM(dims, dtype)


def write_edge(top, fields, out_ref):
    sub = row_ids(TILE, out_ref.shape[2])
    mine = (sub >= HALF) == top
    for place in range(len(fields) // 2):
        first = jnp.where(top, fields[2 * place][TILE:], fields[2 * place][:TILE])
        second = jnp.where(top, fields[2 * place + 1][TILE:], fields[2 * place + 1][:TILE])
        out_ref[place] = jnp.where(mine, first, roll_rows(second, HALF))


def write_planes(planes, out_ref, at):
    planes = planes + [planes[-1]] * (len(planes) % 2)
    for place in range(len(planes) // 2):
        out_ref[at + place] = jnp.concatenate(planes[2 * place : 2 * place + 2], axis=1)


def edge_numbers(top, numbers):
    return jnp.where(top, numbers[1], numbers[0])


def write_temp_edge(top, temp_ref, out_ref, at):
    levels, _, width = temp_ref.shape
    sub = row_ids(TILE, width)
    for group in range(pl.cdiv(levels, 4)):
        packed = jnp.zeros((TILE, width), f32)
        for spot in range(min(4, levels - 4 * group)):
            level = 4 * group + spot
            low = roll_rows(temp_ref[level, :TILE, :], 2 * spot)
            high = roll_rows(temp_ref[level, TILE:, :], 2 * spot + 2)
            packed = jnp.where(sub // 2 == spot, jnp.where(top, high, low), packed)
        out_ref[at + group] = packed


def goes_north(first):
    return (lax.rem(lax.axis_index("lat"), 2) == 0) == (first == 0)


def edge_fields(state, points, weights):
    links = points.shape[0]
    fields = [state[place] for place in range(4)]
    fields += [points[k].astype(f32) for k in range(links)]
    fields += [weights[k] for k in range(links)]
    return fields


def load_body(
    height,
    zonal,
    merid,
    counts,
    points,
    tile,
    weights,
    flux,
    flags,
    edge,
    own,
    state_out,
    points_out,
    weights_out,
    flags_out,
    tile_out,
    counts_in,
    flux_in,
    sems,
):
    pairs = [
        (flux, flux_in),
        (flags, flags_out),
        (tile, tile_out),
        (counts, counts_in),
        (height, state_out.at[0]),
        (zonal, state_out.at[1]),
        (merid, state_out.at[2]),
        (points, points_out),
        (weights, weights_out),
    ]
    copies = [
        pltpu.make_async_copy(source, target, sems.at[place])
        for place, (source, target) in enumerate(pairs)
    ]
    for copy in copies:
        copy.start()
    for copy in copies:
        copy.wait()
    state_out[3] = counts_in[...].astype(f32)
    open_sea = (1 - flags_out[...]).astype(f32)
    masked = [flux_in[plane] * open_sea for plane in range(flux.shape[0])]
    for plane, values in enumerate(masked):
        own[plane] = values
    top = goes_north(0)
    fields = edge_fields(state_out, points_out, weights_out)
    write_edge(top, fields, edge)
    write_planes(masked[:1] + masked, edge, len(fields) // 2)


def pack_second_body(own, state, points, weights, tile, temp, draft, edges, numbers):
    top = goes_north(1)
    fields = edge_fields(state, points, weights)
    write_edge(top, fields, draft)
    links, blocks, rows = tile.shape
    lane = lane_ids(rows)
    diagonal = row_ids(rows, rows) == lane_ids(rows, rows)
    tiles = jnp.zeros((rows, LANES), f32)
    for k in range(links):
        for b in range(blocks):
            line = jnp.broadcast_to(tile[k, b : b + 1, :].astype(f32), (rows, rows))
            upright = jnp.sum(jnp.where(diagonal, line, 0.0), axis=1, keepdims=True)
            tiles = jnp.where(lane == k * blocks + b, upright, tiles)
    numbers[0] = tiles[:TILE]
    numbers[1] = tiles[TILE:]
    masked = [own[plane] for plane in range(own.shape[0])]
    write_planes([edge_numbers(top, numbers)] + masked, draft, len(fields) // 2)
    levels, rows, _ = temp.shape
    for place, columns in enumerate(edge_columns([temp[level] for level in range(levels)], rows)):
        edges[place] = columns


def corner_plane(top, edges):
    west = jnp.where(top, edges[0, TILE:, :], edges[0, :TILE, :])
    east = jnp.where(top, edges[1, TILE:, :], edges[1, :TILE, :])
    return jnp.where((row_ids(TILE) >= HALF) == top, west, roll_rows(east, HALF))


def far_planes(flux_at, received):
    return [spot_of(received, flux_at, 1 + plane) for plane in HALO_FLUXES]


def pack_flux_body(flux_at, draft, received, edges, out):
    planes = far_planes(flux_at, received) + [corner_plane(goes_north(1), edges)]
    at = out.shape[0] - len(planes) // 2
    out[:at] = draft[:at]
    write_planes(planes, out, at)


def edge_columns(fields, rows):
    lane = lane_ids(rows)
    high = jnp.zeros((rows, LANES), f32)
    low = jnp.zeros((rows, LANES), f32)
    for level, field in enumerate(fields):
        ends = jnp.where(lane < HALF, field[:, :LANES], field[:, -LANES:])
        turned = roll_lanes(ends, 2 * level + 2)
        high = jnp.where(lane // 2 == level, turned, high)
        low = jnp.where(lane // 2 == (level + 1) % (LANES // 2), turned, low)
    return roll_lanes(low, -2), high


HALO_FLUXES = (0, 1, 4)


def pass_body(first, second, out):
    out[...] = first[...]


def pack_temp_body(first, temp, other, out):
    write_temp_edge(goes_north(first), temp, out, 0)


def pack_third_body(flux_at, received, edges, numbers, out):
    top = goes_north(0)
    planes = far_planes(flux_at, received)
    write_planes(planes + [corner_plane(top, edges), edge_numbers(top, numbers)], out, 0)


def unpack_rows(top, packed, level):
    spot = level % 4
    return jnp.where(top, roll_rows(packed, -2 * spot), roll_rows(packed, 6 - 2 * spot))


def near_lanes(width):
    return (row_ids(TILE, width) < HALF) == (lax.rem(lax.axis_index("lat"), 2) == 0)


def pick(array, rows):
    return jnp.take_along_axis(array, rows, axis=0, mode="promise_in_bounds")


def pick_lane(array, lanes):
    return jnp.take_along_axis(array, lanes, axis=1, mode="promise_in_bounds")


def spot_of(array, flux_at, place):
    return array[flux_at + place // 2, :, (place % 2) * LANES : (place % 2 + 1) * LANES]


def by_side(even, one, two):
    return jnp.where(even, one, two), jnp.where(even, two, one)


def row_numbers(numbers, column):
    number = jnp.broadcast_to(numbers[:, column : column + 1].astype(i32), (TILE, LANES))
    return number & (TILE - 1), lax.shift_right_logical(number, 3)


FORCING_AT = {0: 4, 1: 5, 4: 6}


def forcing_body(flux_at, got_a, got_b, own, numbers, state, points, weights, ext, light):
    even = lax.rem(lax.axis_index("lat"), 2) == 0
    links, rows, width = points.shape
    blocks = width // LANES
    nflux = own.shape[0]
    ext[:4, :rows, :] = state[...]
    north, south = [], []
    for plane in range(nflux):
        one, two = spot_of(got_a, flux_at, 1 + plane), spot_of(got_b, flux_at, 1 + plane)
        high, low = by_side(even, one, two)
        north.append(high)
        south.append(low)
    mid = [own[plane] for plane in range(nflux)]
    for row_tile in range(rows // TILE):
        here = slice(row_tile * TILE, (row_tile + 1) * TILE)
        for b in range(blocks):
            cols = slice(b * LANES, (b + 1) * LANES)
            totals = [jnp.zeros((TILE, LANES), f32) for _ in range(nflux)]
            for k in range(links):
                within, band = row_numbers(numbers[row_tile], k * blocks + b)
                lanes = points[k, here, cols]
                weight = weights[k, here, cols]
                for plane in range(nflux):
                    value = jnp.where(
                        band == 0,
                        pick(south[plane], within),
                        jnp.where(band == 1, pick(mid[plane], within), pick(north[plane], within)),
                    )
                    totals[plane] = totals[plane] + weight * pick_lane(value, lanes)
            for plane in range(nflux):
                if plane in FORCING_AT:
                    ext[FORCING_AT[plane], here, cols] = totals[plane]
                else:
                    light[plane - 2, here, cols] = totals[plane]


def both_fields(even, near, far):
    north, south = by_side(even, near, far)
    sub = row_ids(*near.shape)
    return [
        jnp.where(sub < HALF, north, south),
        roll_rows(jnp.where(sub < HALF, south, north), HALF),
    ]


def forcing_halo_body(
    flux_at,
    draft,
    got_a,
    got_b,
    got_c,
    own,
    edges,
    ext,
    send_a,
    send_b,
    edges_halo,
):
    even = lax.rem(lax.axis_index("lat"), 2) == 0
    rows, width = 2 * TILE, ext.shape[2]
    blocks = width // LANES
    links = flux_at - 2
    halos = []
    for place in range(flux_at):
        halos += both_fields(even, got_a[place], got_b[place])
    ext[:, :rows, :] = draft[:, :rows, :]
    for place in range(4):
        ext[place, rows:, :] = halos[place]
    tables = {}
    far_at = got_b.shape[0] - (len(HALO_FLUXES) + 1) // 2
    for place, plane in enumerate(HALO_FLUXES):
        one, two = spot_of(got_a, flux_at, 1 + plane), spot_of(got_b, flux_at, 1 + plane)
        north, south = by_side(even, one, two)
        far_north, far_south = by_side(
            even, spot_of(got_c, 0, place), spot_of(got_b, far_at, place)
        )
        tables[plane] = [far_south, south, own[plane], north, far_north]
    sub_one = row_ids(TILE)
    north, south = by_side(
        even, spot_of(got_c, 0, len(HALO_FLUXES) + 1), spot_of(got_b, flux_at, 0)
    )
    numbers = jnp.where(sub_one < HALF, north, south)
    for b in range(blocks):
        cols = slice(b * LANES, (b + 1) * LANES)
        totals = {plane: jnp.zeros((TILE, LANES), f32) for plane in HALO_FLUXES}
        for k in range(links):
            within, band = row_numbers(numbers, k * blocks + b)
            band = band + jnp.where(sub_one < HALF, 2, 0)
            lanes = halos[4 + k][:, cols].astype(i32)
            weight = halos[4 + links + k][:, cols]
            for plane in HALO_FLUXES:
                value = pick(tables[plane][0], within)
                for at in range(1, 5):
                    value = jnp.where(band == at, pick(tables[plane][at], within), value)
                totals[plane] = totals[plane] + weight * pick_lane(value, lanes)
        for plane in HALO_FLUXES:
            ext[FORCING_AT[plane], rows:, cols] = totals[plane]

    lane = lane_ids(3 * TILE)
    to_west = jnp.zeros((3 * TILE, LANES), f32)
    to_east = jnp.zeros((3 * TILE, LANES), f32)
    for place in range(ext.shape[0]):
        low = roll_lanes(ext[place, :, :LANES], 3 * place)
        high = roll_lanes(ext[place, :, width - LANES :], -3 * place)
        to_west = jnp.where((lane >= 3 * place) & (lane < 3 * place + 3), low, to_west)
        edge = LANES - 3 * place
        to_east = jnp.where((lane >= edge - 3) & (lane < edge), high, to_east)
    corner = len(HALO_FLUXES)
    corners = both_fields(even, spot_of(got_c, 0, corner), spot_of(got_b, far_at, corner))
    for place in range(2):
        edges_halo[place] = corners[place]
    lon_even = lax.rem(lax.axis_index("lon"), 2) == 0
    send_a[0] = jnp.where(lon_even, to_east, to_west)
    send_b[0] = jnp.where(lon_even, to_west, to_east)
    for part, columns in ((slice(0, rows), edges), (slice(rows, rows + TILE), edges_halo)):
        send_a[1, part, :] = jnp.where(lon_even, columns[1], columns[0])
        send_b[1, part, :] = jnp.where(lon_even, columns[0], columns[1])


def column_depth(counts, levels):
    scale = 1.0 / (2.0 * levels)
    return counts * scale + counts * (counts - 1.0) * (scale / levels)


def sideways(array, ends):
    rows, width = array.shape
    lane = lane_ids(rows)
    parts = [array[:, at : at + LANES] for at in range(0, width, LANES)]
    right = [roll_lanes(part, -1) for part in parts] + [ends]
    left = [ends] + [roll_lanes(part, 1) for part in parts]
    east = [jnp.where(lane == LANES - 1, b, a) for a, b in zip(right, right[1:])]
    west = [jnp.where(lane == 0, a, b) for a, b in zip(left, left[1:])]
    return jnp.concatenate(east, axis=1), jnp.concatenate(west, axis=1)


def turned(ends, level):
    return pltpu.roll(ends, lax.rem(2 * LANES - 2 * level, LANES), 1)


LEVELS_AT_ONCE = 6
LEVELS_BEFORE = 10


def before_body(ext, light, temp, got_a, got_b, base, laps, halo):
    levels, rows, width = temp.shape
    counts = ext[3]
    own_counts = counts[:rows]
    lane = lane_ids(3 * TILE, width)
    limit_east = jnp.where(lane == width - 1, 0.0, jnp.minimum(counts, roll_lanes(counts, -1)))
    limit_north = jnp.minimum(counts, roll_rows(counts, -1))
    limits = (limit_east, roll_lanes(limit_east, 1), limit_north, roll_rows(limit_north, 1))
    step = math.gcd(levels, LEVELS_BEFORE)
    odd = lax.rem(lax.axis_index("lat"), 2) == 1
    near = near_lanes(width)
    for level in range(levels):
        rows_near = unpack_rows(jnp.logical_not(odd), got_a[level // 4], level)
        rows_far = unpack_rows(odd, got_b[level // 4], level)
        halo[level] = jnp.where(near, rows_near, rows_far)

    def group(at, down_before):
        for inner in range(step):
            level = at * step + inner
            level_f = level.astype(f32)
            own = temp[level]
            whole = jnp.concatenate([own, halo[level]], axis=0)
            east, west = sideways(whole, whole[:, :LANES])
            lap = -4.0 * whole
            for around, limit in zip(
                (east, west, roll_rows(whole, -1), roll_rows(whole, 1)), limits
            ):
                lap = lap + jnp.where(level_f < limit, around, whole)
            laps[level] = lap
            beneath = temp[jnp.minimum(level + 1, levels - 1)]
            down = jnp.where(level_f + 1.0 < own_counts, beneath - own, 0.0)
            absorb = jnp.exp(jnp.full(own.shape, -1.0 / light_decay, f32) * level_f)
            absorb = absorb * (light_gain * (1.0 - math.exp(-1.0 / light_decay)))
            source = absorb * light[1] + jnp.where(level == 0, heat_gain, 0.0) * light[0]
            change = diapycnal_diffusion * (down - down_before) + source
            base[level] = own + jnp.where(level_f < own_counts, change, 0.0)
            down_before = down
        return down_before

    lax.fori_loop(0, levels // step, group, jnp.zeros((rows, width), f32))


def finish_level(level, own, halo_level, base, lap, ends, limits, speeds):
    rows, width = own.shape
    level_f = level.astype(f32)
    lane = lane_ids(3 * TILE)
    side = turned(ends[2], level)
    parts = [lap[:, at : at + LANES] for at in range(0, width, LANES)]
    parts[0] = parts[0] + jnp.where(lane == 0, side, 0.0)
    parts[-1] = parts[-1] + jnp.where(lane == LANES - 1, side, 0.0)
    lap = jnp.concatenate(parts, axis=1)
    whole = jnp.concatenate([own, halo_level], axis=0)
    own_lap = lap[:rows]
    around_temp = sideways(own, turned(ends[0][:rows], level))
    around_temp += (roll_rows(whole, -1)[:rows], roll_rows(whole, 1)[:rows])
    around_lap = sideways(own_lap, turned(ends[1][:rows], level))
    around_lap += (roll_rows(lap, -1)[:rows], roll_rows(lap, 1)[:rows])
    change = jnp.zeros((rows, width), f32)
    for place, limit in enumerate(limits):
        moved = mixing_fourth * (own_lap - around_lap[place])
        moved = moved - speeds[place] * (around_temp[place] + own)
        change = change + jnp.where(level_f < limit, moved, 0.0)
    return base + change


def hot_body(points, hot):
    links, rows, width = points.shape
    blocks = width // LANES
    cells = row_ids(LANES).astype(f32).astype(jnp.bfloat16)
    one, none = jnp.bfloat16(1.0), jnp.bfloat16(0.0)
    for k in range(links):
        for b in range(blocks):
            for row in range(rows):
                line = points[k, row : row + 1, b * LANES : (b + 1) * LANES]
                line = jnp.broadcast_to(line.astype(f32), (2 * TILE, LANES)).astype(jnp.bfloat16)
                line = jnp.concatenate([line] * (LANES // (2 * TILE)), axis=0)
                hot[k * rows + row, :, b * LANES : (b + 1) * LANES] = jnp.transpose(
                    jnp.where(line == cells, one, none)
                )


def subcycle_body(
    levels,
    ext,
    edges_own,
    edges_halo,
    got_a,
    got_b,
    temp,
    halo,
    base,
    laps,
    hot,
    weights,
    tile_hbm,
    out_height,
    out_zonal,
    out_merid,
    limits_out,
    speeds_out,
    ends_out,
    sums_a,
    sums_b,
    sums_mid,
    whole,
    values,
    table,
    tile,
    tile_sem,
):
    tile_copy = pltpu.make_async_copy(tile_hbm, tile, tile_sem)
    tile_copy.start()
    edges = [
        jnp.concatenate([edges_own[place], edges_halo[place]], axis=0) for place in range(2)
    ]
    width = ext.shape[2]
    rows = temp.shape[1]
    lon_even = lax.rem(lax.axis_index("lon"), 2) == 0
    even = lax.rem(lax.axis_index("lat"), 2) == 0
    lane = lane_ids(3 * TILE)
    from_east = [jnp.where(lon_even, got_a[place], got_b[place]) for place in range(2)]
    from_west = [jnp.where(lon_even, got_b[place], got_a[place]) for place in range(2)]
    planes = []
    for place in range(ext.shape[0]):
        third = jnp.where(
            lane < 3,
            roll_lanes(from_east[0], -3 * place),
            jnp.where(lane >= LANES - 3, roll_lanes(from_west[0], 3 * place), 0.0),
        )
        planes.append(jnp.concatenate([ext[place], third], axis=1))
    height, zonal, merid, counts, wind_east, wind_north, fresh = planes

    def east_of(array):
        return roll_lanes(array, -1)

    def west_of(array):
        return roll_lanes(array, 1)

    def north_of(array):
        return roll_rows(array, -1)

    def south_of(array):
        return roll_rows(array, 1)

    depth = column_depth(counts, levels)
    wet = (counts > 0.5).astype(f32)
    east_wet = wet * east_of(wet)
    north_wet = wet * north_of(wet)
    east_depth = jnp.minimum(depth, east_of(depth))
    north_depth = jnp.minimum(depth, north_of(depth))
    east_pull = grav_step * east_depth
    north_pull = grav_step * north_depth
    wind_east = wind_step * wind_east
    wind_north = wind_step * wind_north
    fresh = fresh_step * fresh
    for _ in range(SUBS):
        zonal = east_wet * (zonal - east_pull * (east_of(height) - height) + wind_east)
        merid = north_wet * (merid - north_pull * (north_of(height) - height) + wind_north)
        spread = zonal - west_of(zonal) + merid - south_of(merid)
        height = height + wet * (fresh - height_step * spread)
    out_height[...] = height[:rows, :width]
    out_zonal[...] = zonal[:rows, :width]
    out_merid[...] = merid[:rows, :width]

    limit_east = jnp.minimum(counts, east_of(counts))
    limit_north = jnp.minimum(counts, north_of(counts))
    limit_west, limit_south = west_of(limit_east), south_of(limit_north)
    limits = [
        limit[:rows, :width] for limit in (limit_east, limit_west, limit_north, limit_south)
    ]
    speed_east = 0.5 * advect_coef * zonal / jnp.maximum(east_depth, depth_floor)
    speed_north = 0.5 * advect_coef * merid / jnp.maximum(north_depth, depth_floor)
    speeds = [
        speed[:rows, :width]
        for speed in (speed_east, -west_of(speed_east), speed_north, -south_of(speed_north))
    ]
    for place in range(4):
        limits_out[place] = limits[place]
        speeds_out[place] = speeds[place]

    lane_level = (lane // 2).astype(f32)
    odd_lane = (lane & 1) == 1
    far_east, far_west = from_east[1], from_west[1]

    def column(limit, at):
        return jnp.broadcast_to(limit[:, at : at + 1], (3 * TILE, LANES))

    def edge_lap(center, toward_east, toward_west, at, at_west):
        total = -4.0 * center
        for around, limit in (
            (toward_east, column(limit_east, at)),
            (toward_west, column(limit_east, at_west)),
            (north_of(center), column(limit_north, at)),
            (south_of(center), column(limit_south, at)),
        ):
            total = total + jnp.where(lane_level < limit, around, center)
        return total

    total_lanes = width + LANES
    lap_west = edge_lap(
        far_west,
        roll_lanes(edges[0], 1),
        roll_lanes(far_west, 1),
        total_lanes - 1,
        total_lanes - 2,
    )
    lap_east = edge_lap(
        far_east, roll_lanes(far_east, -1), roll_lanes(edges[1], -1), width, width - 1
    )
    side_west = far_west - roll_lanes(edges[0], 1)
    side_west = jnp.where(lane_level < column(limit_east, total_lanes - 1), side_west, 0.0)
    side_east = far_east - roll_lanes(edges[1], -1)
    side_east = jnp.where(lane_level < column(limit_east, width - 1), side_east, 0.0)
    ends = []
    for west, east in ((far_west, far_east), (lap_west, lap_east), (side_west, side_east)):
        ends.append(roll_lanes(jnp.where(odd_lane, west, east), -1))
    for place in range(3):
        ends_out[place] = ends[place]

    zero = jnp.zeros((), i32)
    top = finish_level(zero, temp[0], halo[0], base[0], laps[0], ends, limits, speeds)
    own_wet = wet[:rows, :width]
    thick = jnp.maximum(depth[:rows, :width], depth_floor)
    surface = [
        top * own_wet,
        height[:rows, :width] * own_wet,
        zonal[:rows, :width] / thick * own_wet,
        merid[:rows, :width] / thick * own_wet,
        own_wet,
    ]
    nsums = len(surface)
    values[...] = jnp.zeros(values.shape, f32)
    for place in range(nsums):
        values[:, place, :] = surface[place]
    table[...] = jnp.zeros(table.shape, f32)
    links = weights.shape[0]
    blocks = width // LANES
    tile_copy.wait()

    for row in range(rows):
        held = values[row]
        for k in range(links):
            shares = held * weights[k, row : row + 1, :]
            upper = shares.astype(jnp.bfloat16)
            lower = (shares - upper.astype(f32)).astype(jnp.bfloat16)
            both = jnp.concatenate([upper, lower], axis=0)
            stacked = jnp.concatenate(
                [both[:, b * LANES : (b + 1) * LANES] for b in range(blocks)], axis=0
            )
            found = jnp.dot(stacked, hot[k * rows + row], preferred_element_type=f32)
            for b in range(blocks):
                target = tile[k, b, row]
                mine = found[b * 2 * TILE : (b + 1) * 2 * TILE, b * LANES : (b + 1) * LANES]
                table[target] = table[target] + mine
    for place in range(nsums):
        total = table[:, place, :] + table[:, TILE + place, :]
        south, middle, north = total[:TILE], total[TILE : 2 * TILE], total[2 * TILE :]
        sums_mid[place] = middle
        sums_a[place] = jnp.where(even, north, south)
        sums_b[place] = jnp.where(even, south, north)

    run_levels(
        0,
        early_groups(levels),
        temp,
        halo,
        base,
        laps,
        limits_out,
        speeds_out,
        ends_out,
        whole,
    )


def level_step(levels):
    return math.gcd(levels, LEVELS_AT_ONCE)


def early_groups(levels):
    groups = levels // level_step(levels)
    place = lax.axis_index("lat")
    inner = jnp.where(lax.rem(place, 2) == 1, groups // 5, 0)
    return jnp.where(place == 0, groups * 7 // 10, jnp.where(place == 1, groups // 2, inner))


LAST_GROUPS = 2


def run_levels(start, stop, temp, halo, base, laps, limits, speeds, ends, out, done=None):
    step = level_step(temp.shape[0])

    def group(at, carry):
        for inner in range(step):
            level = jnp.int32(at * step + inner)
            out[level] = finish_level(
                level,
                temp[level],
                halo[level],
                base[level],
                laps[level],
                [ends[place] for place in range(3)],
                [limits[place] for place in range(4)],
                [speeds[place] for place in range(4)],
            )
        if done is not None:
            done(at)
        return carry

    lax.fori_loop(start, stop, group, 0)


def tracer_body(
    temp,
    halo,
    base,
    laps,
    limits,
    speeds,
    ends,
    draft,
    height,
    zonal,
    merid,
    out_height,
    out_zonal,
    out_merid,
    out,
    whole,
    sems,
    level_sems,
):
    levels = temp.shape[0]
    step = level_step(levels)
    groups = levels // step
    pairs = [(height, out_height), (zonal, out_zonal), (merid, out_merid)]
    copies = [
        pltpu.make_async_copy(source, target, sems.at[place])
        for place, (source, target) in enumerate(pairs)
    ]
    for copy in copies:
        copy.start()

    def level_copy(at, source=whole):
        part = pl.ds(at * step, step)
        return pltpu.make_async_copy(source.at[part], out.at[part], level_sems.at[at])

    early = early_groups(levels)

    def start(at, carry):
        level_copy(at, draft).start()
        return carry

    lax.fori_loop(0, early, start, 0)
    inside = max(groups - LAST_GROUPS, 0)
    refs = (temp, halo, base, laps, limits, speeds, ends, whole)
    run_levels(early, inside, *refs, lambda at: level_copy(at).start())
    run_levels(inside, groups, *refs)
    for at in range(inside):
        level_copy(at).wait()
    for copy in copies:
        copy.wait()


def merge_body(mid, got_a, got_b, flags, whole, draft, out, out_temp, surface, sems):
    levels = whole.shape[0]
    step = level_step(levels)
    first = step * max(levels // step - LAST_GROUPS, 0)
    part = pl.ds(first, levels - first)
    rest = pltpu.make_async_copy(whole.at[part], out_temp.at[part], sems.at[0])
    rest.start()
    open_sea = (1 - flags[...]).astype(f32)
    nsurf = out.shape[0]
    area = mid[nsurf] + got_a[nsurf] + got_b[nsurf]
    scale = open_sea / jnp.maximum(area, area_floor)
    for place in range(nsurf):
        surface[place] = (mid[place] + got_a[place] + got_b[place]) * scale
    copy = pltpu.make_async_copy(surface, out, sems.at[1])
    copy.start()
    copy.wait()
    rest.wait()


def shards(
    free_elevation,
    zonal_volume_carriage,
    meridional_volume_carriage,
    thermal_field,
    flooded_strata_number,
    aerial_exchanges,
    aerial_terrain_flags,
    donor_tile_number,
    donor_point_number,
    pairing_coefficients,
):
    levels, rows, width = thermal_field.shape
    nflux, band_rows, lanes = aerial_exchanges.shape
    links, _, blocks = donor_tile_number.shape
    assert rows == 2 * TILE and band_rows == TILE and lanes == LANES
    assert 2 * levels <= LANES and lax.axis_size("lon") % 2 == 0
    nsums = 5
    fields = 4 + 2 * links
    flux_at = fields // 2
    flux_tiles = (nflux + 2) // 2
    temp_at = flux_at + flux_tiles
    groups = pl.cdiv(levels, 4)
    tile_lines = jnp.swapaxes(donor_tile_number, 1, 2)
    temp = thermal_field
    edge_a, own, state, points, weights, flags, tile = call(
        load_body,
        [
            shape(temp_at, TILE, width),
            shape(nflux, TILE, LANES),
            shape(4, rows, width),
            shape(links, rows, width, dtype=i32),
            shape(links, rows, width),
            shape(band_rows, lanes, dtype=i32),
            shape(links, blocks, rows, dtype=i32),
        ],
        (
            free_elevation,
            zonal_volume_carriage,
            meridional_volume_carriage,
            flooded_strata_number,
            donor_point_number,
            tile_lines,
            pairing_coefficients,
            aerial_exchanges,
            aerial_terrain_flags,
        ),
        "load",
        1.6,
        scratch=[
            pltpu.VMEM((rows, width), i32),
            pltpu.VMEM((nflux, band_rows, lanes), f32),
            pltpu.SemaphoreType.DMA((9,)),
        ],
        hbm=range(9),
    )
    got_a = swap(edge_a, "lat", 0, False)
    far_tiles = (len(HALO_FLUXES) + 1) // 2
    edge_tiles = temp_at + far_tiles
    draft_b, edges, numbers = call(
        pack_second_body,
        [
            shape(edge_tiles, TILE, width),
            shape(2, rows, LANES),
            shape(2, TILE, LANES),
        ],
        (own, state, points, weights, tile, temp),
        "pack_b",
        0.3,
    )
    (edge_b,) = call(
        functools.partial(pack_flux_body, flux_at),
        [shape(edge_tiles, TILE, width)],
        (draft_b, got_a, edges),
        "pack_flux",
        0.0,
    )
    got_b = swap(edge_b, "lat", 1, False)
    (temp_b,) = call(
        functools.partial(pack_temp_body, 1),
        [shape(groups, TILE, width)],
        (temp, edge_b),
        "pack_temp_b",
        LATE,
    )
    got_temp_b = swap(temp_b, "lat", 1, False)
    (temp_a,) = call(
        functools.partial(pack_temp_body, 0),
        [shape(groups, TILE, width)],
        (temp, temp_b),
        "pack_temp_a",
        0.0,
    )
    got_temp_a = swap(temp_a, "lat", 0, False)
    (edge_c,) = call(
        functools.partial(pack_third_body, flux_at),
        [shape((len(HALO_FLUXES) + 3) // 2, TILE, width)],
        (got_b, edges, numbers),
        "pack_c",
        LATE,
    )
    got_c = swap(edge_c, "lat", 0, False)
    draft_ext, light = call(
        functools.partial(forcing_body, flux_at),
        [shape(7, 3 * TILE, width), shape(2, rows, width)],
        (got_a, got_b, own, numbers, state, points, weights),
        "forcing",
        0.4,
    )
    ext, send_a, send_b, edges_halo = call(
        functools.partial(forcing_halo_body, flux_at),
        [
            shape(7, 3 * TILE, width),
            shape(2, 3 * TILE, LANES),
            shape(2, 3 * TILE, LANES),
            shape(2, TILE, LANES),
        ],
        (draft_ext, got_a, got_b, got_c, own, edges),
        "forcing_halo",
        0.3,
    )
    lon_b = swap(send_b, "lon", 1, True)
    (send_a,) = call(
        pass_body, [shape(2, 3 * TILE, LANES)], (send_a, send_b), "pass_lon", LATE
    )
    lon_a = swap(send_a, "lon", 0, True)
    (hot,) = call(
        hot_body,
        [shape(links * rows, LANES, blocks * LANES, dtype=jnp.bfloat16)],
        (points,),
        "hot",
        0.0,
    )
    base, laps, halo = call(
        before_body,
        [
            shape(levels, rows, width),
            shape(levels, 3 * TILE, width),
            shape(levels, TILE, width),
        ],
        (ext, light, temp, got_temp_a, got_temp_b),
        "before",
        0.0,
    )
    (
        advanced_elevation,
        transport_x_next,
        transport_y_next,
        limits,
        speeds,
        ends,
        sums_a,
        sums_b,
        sums_mid,
        draft,
    ) = call(
        functools.partial(subcycle_body, levels),
        [shape(rows, width)] * 3
        + [shape(4, rows, width), shape(4, rows, width), shape(3, 3 * TILE, LANES)]
        + [shape(nsums, TILE, LANES)] * 3
        + [shape(levels, rows, width)],
        (
            ext,
            edges,
            edges_halo,
            lon_a,
            lon_b,
            temp,
            halo,
            base,
            laps,
            hot,
            weights,
            tile_lines,
        ),
        "subcycles",
        2.6,
        scratch=[
            pltpu.VMEM((rows, TILE, width), f32),
            pltpu.VMEM((3 * TILE, 2 * TILE, LANES), f32),
            pltpu.SMEM((links, blocks, rows), i32),
            pltpu.SemaphoreType.DMA(()),
        ],
        hbm=(11,),
    )
    back_b = swap(sums_b, "lat", 1, False)
    (sums_a,) = call(
        pass_body, [shape(nsums, TILE, LANES)], (sums_a, sums_b), "pass_sums", LATE
    )
    back_a = swap(sums_a, "lat", 0, False)
    advanced_elevation, transport_x_next, transport_y_next, draft_field, draft = call(
        tracer_body,
        [
            pltpu.HBM((rows, width), f32),
            pltpu.HBM((rows, width), f32),
            pltpu.HBM((rows, width), f32),
            pltpu.HBM((levels, rows, width), f32),
            shape(levels, rows, width),
        ],
        (
            temp,
            halo,
            base,
            laps,
            limits,
            speeds,
            ends,
            draft,
            advanced_elevation,
            transport_x_next,
            transport_y_next,
        ),
        "tracer",
        2.5,
        scratch=[
            pltpu.SemaphoreType.DMA((3,)),
            pltpu.SemaphoreType.DMA((levels // level_step(levels),)),
        ],
    )
    marine_skin_condition, advanced_thermal_field = call(
        merge_body,
        [
            pltpu.HBM((nsums - 1, band_rows, lanes), f32),
            pltpu.HBM((levels, rows, width), f32),
        ],
        (sums_mid, back_a, back_b, flags, draft, draft_field),
        "merge",
        0.1,
        aliases={5: 1},
        hbm=(5,),
        scratch=[
            pltpu.VMEM((nsums - 1, band_rows, lanes), f32),
            pltpu.SemaphoreType.DMA((2,)),
        ],
    )
    return (
        advanced_elevation,
        transport_x_next,
        transport_y_next,
        advanced_thermal_field,
        marine_skin_condition,
    )


def solution(mesh):
    flat = P("lat", "lon")
    deep = P(None, "lat", "lon")
    return jax.shard_map(
        shards,
        mesh=mesh,
        in_specs=(flat, flat, flat, deep, flat, deep, flat, deep, deep, deep),
        out_specs=(flat, flat, flat, deep, deep),
        check_vma=False,
    )
```

```python
import functools
import math

import jax
import jax.numpy as jnp
from jax import lax
from jax.experimental import pallas as pl
from jax.experimental.pallas import tpu as pltpu
from jax.sharding import PartitionSpec as P

SUBS = 3

grav_step = 0.6
height_step = 0.6
wind_step = 0.5
fresh_step = 0.5
mixing_fourth = 0.02
advect_coef = 0.1
diapycnal_diffusion = 0.2
heat_gain = 0.3
light_gain = 0.3
light_decay = 8.0
depth_floor = 0.25
area_floor = 1.0

TILE = 8
LANES = 128
HALF = TILE // 2

f32 = jnp.float32
i32 = jnp.int32

LATE = 4.0
FLOPS_PER_US = 1150000000


def swap_pairs(count, first, periodic):
    pairs = []
    for low in range(first, count, 2):
        high = low + 1
        if high == count:
            if not periodic:
                continue
            high = 0
        pairs += [(low, high), (high, low)]
    return pairs


def swap(array, axis, first, periodic):
    return lax.ppermute(array, axis, swap_pairs(lax.axis_size(axis), first, periodic))


def lane_ids(rows, width=LANES):
    return lax.broadcasted_iota(i32, (rows, width), 1)


def row_ids(rows, width=LANES):
    return lax.broadcasted_iota(i32, (rows, width), 0)


def roll_rows(array, by):
    by = by % array.shape[0]
    return pltpu.roll(array, by, 0) if by else array


def roll_lanes(array, by):
    by = by % array.shape[1]
    return pltpu.roll(array, by, 1) if by else array


def call(body, outs, ins, name, took, aliases=None, scratch=(), hbm=()):
    specs = [
        pl.BlockSpec(memory_space=pltpu.HBM if place in hbm else pltpu.VMEM)
        for place in range(len(ins))
    ]
    ins = [
        pltpu.with_memory_space_constraint(leaf, pltpu.HBM) if place in hbm else leaf
        for place, leaf in enumerate(ins)
    ]
    return pl.pallas_call(
        body,
        out_shape=outs,
        in_specs=specs,
        out_specs=[pl.BlockSpec(memory_space=leaf.memory_space) for leaf in outs],
        scratch_shapes=list(scratch),
        input_output_aliases=aliases or {},
        compiler_params=pltpu.CompilerParams(vmem_limit_bytes=12 * 1024 * 1024),
        cost_estimate=pl.CostEstimate(
            flops=int(took * FLOPS_PER_US), bytes_accessed=1024, transcendentals=0
        ),
        name=name,
    )(*ins)


def shape(*dims, dtype=f32):
    return pltpu.VMEM(dims, dtype)


def write_edge(top, fields, out_ref):
    sub = row_ids(TILE, out_ref.shape[2])
    mine = (sub >= HALF) == top
    for place in range(len(fields) // 2):
        first = jnp.where(top, fields[2 * place][TILE:], fields[2 * place][:TILE])
        second = jnp.where(top, fields[2 * place + 1][TILE:], fields[2 * place + 1][:TILE])
        out_ref[place] = jnp.where(mine, first, roll_rows(second, HALF))


def write_planes(planes, out_ref, at):
    planes = planes + [planes[-1]] * (len(planes) % 2)
    for place in range(len(planes) // 2):
        out_ref[at + place] = jnp.concatenate(planes[2 * place : 2 * place + 2], axis=1)


def edge_numbers(top, numbers):
    return jnp.where(top, numbers[1], numbers[0])


def write_temp_edge(top, temp_ref, out_ref, at):
    levels, _, width = temp_ref.shape
    sub = row_ids(TILE, width)
    for group in range(pl.cdiv(levels, 4)):
        packed = jnp.zeros((TILE, width), f32)
        for spot in range(min(4, levels - 4 * group)):
            level = 4 * group + spot
            low = roll_rows(temp_ref[level, :TILE, :], 2 * spot)
            high = roll_rows(temp_ref[level, TILE:, :], 2 * spot + 2)
            packed = jnp.where(sub // 2 == spot, jnp.where(top, high, low), packed)
        out_ref[at + group] = packed


def goes_north(first):
    return (lax.rem(lax.axis_index("lat"), 2) == 0) == (first == 0)


def edge_fields(state, points, weights):
    links = points.shape[0]
    fields = [state[place] for place in range(4)]
    fields += [points[k].astype(f32) for k in range(links)]
    fields += [weights[k] for k in range(links)]
    return fields


def load_body(
    height,
    zonal,
    merid,
    counts,
    points,
    tile,
    weights,
    flux,
    flags,
    edge,
    own,
    state_out,
    points_out,
    weights_out,
    flags_out,
    tile_out,
    counts_in,
    flux_in,
    sems,
):
    pairs = [
        (flux, flux_in),
        (flags, flags_out),
        (tile, tile_out),
        (counts, counts_in),
        (height, state_out.at[0]),
        (zonal, state_out.at[1]),
        (merid, state_out.at[2]),
        (points, points_out),
        (weights, weights_out),
    ]
    copies = [
        pltpu.make_async_copy(source, target, sems.at[place])
        for place, (source, target) in enumerate(pairs)
    ]
    for copy in copies:
        copy.start()
    for copy in copies:
        copy.wait()
    state_out[3] = counts_in[...].astype(f32)
    open_sea = (1 - flags_out[...]).astype(f32)
    masked = [flux_in[plane] * open_sea for plane in range(flux.shape[0])]
    for plane, values in enumerate(masked):
        own[plane] = values
    top = goes_north(0)
    fields = edge_fields(state_out, points_out, weights_out)
    write_edge(top, fields, edge)
    write_planes(masked[:1] + masked, edge, len(fields) // 2)


def pack_second_body(own, state, points, weights, tile, temp, draft, edges, numbers):
    top = goes_north(1)
    fields = edge_fields(state, points, weights)
    write_edge(top, fields, draft)
    links, blocks, rows = tile.shape
    lane = lane_ids(rows)
    diagonal = row_ids(rows, rows) == lane_ids(rows, rows)
    tiles = jnp.zeros((rows, LANES), f32)
    for k in range(links):
        for b in range(blocks):
            line = jnp.broadcast_to(tile[k, b : b + 1, :].astype(f32), (rows, rows))
            upright = jnp.sum(jnp.where(diagonal, line, 0.0), axis=1, keepdims=True)
            tiles = jnp.where(lane == k * blocks + b, upright, tiles)
    numbers[0] = tiles[:TILE]
    numbers[1] = tiles[TILE:]
    masked = [own[plane] for plane in range(own.shape[0])]
    write_planes([edge_numbers(top, numbers)] + masked, draft, len(fields) // 2)
    levels, rows, _ = temp.shape
    for place, columns in enumerate(edge_columns([temp[level] for level in range(levels)], rows)):
        edges[place] = columns


def corner_plane(top, edges):
    west = jnp.where(top, edges[0, TILE:, :], edges[0, :TILE, :])
    east = jnp.where(top, edges[1, TILE:, :], edges[1, :TILE, :])
    return jnp.where((row_ids(TILE) >= HALF) == top, west, roll_rows(east, HALF))


def far_planes(flux_at, received):
    return [spot_of(received, flux_at, 1 + plane) for plane in HALO_FLUXES]


def pack_flux_body(flux_at, draft, received, edges, out):
    planes = far_planes(flux_at, received) + [corner_plane(goes_north(1), edges)]
    at = out.shape[0] - len(planes) // 2
    out[:at] = draft[:at]
    write_planes(planes, out, at)


def edge_columns(fields, rows):
    lane = lane_ids(rows)
    high = jnp.zeros((rows, LANES), f32)
    low = jnp.zeros((rows, LANES), f32)
    for level, field in enumerate(fields):
        ends = jnp.where(lane < HALF, field[:, :LANES], field[:, -LANES:])
        turned = roll_lanes(ends, 2 * level + 2)
        high = jnp.where(lane // 2 == level, turned, high)
        low = jnp.where(lane // 2 == (level + 1) % (LANES // 2), turned, low)
    return roll_lanes(low, -2), high


HALO_FLUXES = (0, 1, 4)


def pass_body(first, second, out):
    out[...] = first[...]


def pack_temp_body(first, temp, other, out):
    write_temp_edge(goes_north(first), temp, out, 0)


def pack_third_body(flux_at, received, edges, numbers, out):
    top = goes_north(0)
    planes = far_planes(flux_at, received)
    write_planes(planes + [corner_plane(top, edges), edge_numbers(top, numbers)], out, 0)


def unpack_rows(top, packed, level):
    spot = level % 4
    return jnp.where(top, roll_rows(packed, -2 * spot), roll_rows(packed, 6 - 2 * spot))


def near_lanes(width):
    return (row_ids(TILE, width) < HALF) == (lax.rem(lax.axis_index("lat"), 2) == 0)


def pick(array, rows):
    return jnp.take_along_axis(array, rows, axis=0, mode="promise_in_bounds")


def pick_lane(array, lanes):
    return jnp.take_along_axis(array, lanes, axis=1, mode="promise_in_bounds")


def spot_of(array, flux_at, place):
    return array[flux_at + place // 2, :, (place % 2) * LANES : (place % 2 + 1) * LANES]


def by_side(even, one, two):
    return jnp.where(even, one, two), jnp.where(even, two, one)


def row_numbers(numbers, column):
    number = jnp.broadcast_to(numbers[:, column : column + 1].astype(i32), (TILE, LANES))
    return number & (TILE - 1), lax.shift_right_logical(number, 3)


FORCING_AT = {0: 4, 1: 5, 4: 6}


def forcing_body(flux_at, got_a, got_b, own, numbers, state, points, weights, ext, light):
    even = lax.rem(lax.axis_index("lat"), 2) == 0
    links, rows, width = points.shape
    blocks = width // LANES
    nflux = own.shape[0]
    ext[:4, :rows, :] = state[...]
    north, south = [], []
    for plane in range(nflux):
        one, two = spot_of(got_a, flux_at, 1 + plane), spot_of(got_b, flux_at, 1 + plane)
        high, low = by_side(even, one, two)
        north.append(high)
        south.append(low)
    mid = [own[plane] for plane in range(nflux)]
    for row_tile in range(rows // TILE):
        here = slice(row_tile * TILE, (row_tile + 1) * TILE)
        for b in range(blocks):
            cols = slice(b * LANES, (b + 1) * LANES)
            totals = [jnp.zeros((TILE, LANES), f32) for _ in range(nflux)]
            for k in range(links):
                within, band = row_numbers(numbers[row_tile], k * blocks + b)
                lanes = points[k, here, cols]
                weight = weights[k, here, cols]
                for plane in range(nflux):
                    value = jnp.where(
                        band == 0,
                        pick(south[plane], within),
                        jnp.where(band == 1, pick(mid[plane], within), pick(north[plane], within)),
                    )
                    totals[plane] = totals[plane] + weight * pick_lane(value, lanes)
            for plane in range(nflux):
                if plane in FORCING_AT:
                    ext[FORCING_AT[plane], here, cols] = totals[plane]
                else:
                    light[plane - 2, here, cols] = totals[plane]


def both_fields(even, near, far):
    north, south = by_side(even, near, far)
    sub = row_ids(*near.shape)
    return [
        jnp.where(sub < HALF, north, south),
        roll_rows(jnp.where(sub < HALF, south, north), HALF),
    ]


def forcing_halo_body(
    flux_at,
    draft,
    got_a,
    got_b,
    got_c,
    own,
    edges,
    ext,
    send_a,
    send_b,
    edges_halo,
):
    even = lax.rem(lax.axis_index("lat"), 2) == 0
    rows, width = 2 * TILE, ext.shape[2]
    blocks = width // LANES
    links = flux_at - 2
    halos = []
    for place in range(flux_at):
        halos += both_fields(even, got_a[place], got_b[place])
    ext[:, :rows, :] = draft[:, :rows, :]
    for place in range(4):
        ext[place, rows:, :] = halos[place]
    tables = {}
    far_at = got_b.shape[0] - (len(HALO_FLUXES) + 1) // 2
    for place, plane in enumerate(HALO_FLUXES):
        one, two = spot_of(got_a, flux_at, 1 + plane), spot_of(got_b, flux_at, 1 + plane)
        north, south = by_side(even, one, two)
        far_north, far_south = by_side(
            even, spot_of(got_c, 0, place), spot_of(got_b, far_at, place)
        )
        tables[plane] = [far_south, south, own[plane], north, far_north]
    sub_one = row_ids(TILE)
    north, south = by_side(
        even, spot_of(got_c, 0, len(HALO_FLUXES) + 1), spot_of(got_b, flux_at, 0)
    )
    numbers = jnp.where(sub_one < HALF, north, south)
    for b in range(blocks):
        cols = slice(b * LANES, (b + 1) * LANES)
        totals = {plane: jnp.zeros((TILE, LANES), f32) for plane in HALO_FLUXES}
        for k in range(links):
            within, band = row_numbers(numbers, k * blocks + b)
            band = band + jnp.where(sub_one < HALF, 2, 0)
            lanes = halos[4 + k][:, cols].astype(i32)
            weight = halos[4 + links + k][:, cols]
            for plane in HALO_FLUXES:
                value = pick(tables[plane][0], within)
                for at in range(1, 5):
                    value = jnp.where(band == at, pick(tables[plane][at], within), value)
                totals[plane] = totals[plane] + weight * pick_lane(value, lanes)
        for plane in HALO_FLUXES:
            ext[FORCING_AT[plane], rows:, cols] = totals[plane]

    lane = lane_ids(3 * TILE)
    to_west = jnp.zeros((3 * TILE, LANES), f32)
    to_east = jnp.zeros((3 * TILE, LANES), f32)
    for place in range(ext.shape[0]):
        low = roll_lanes(ext[place, :, :LANES], 3 * place)
        high = roll_lanes(ext[place, :, width - LANES :], -3 * place)
        to_west = jnp.where((lane >= 3 * place) & (lane < 3 * place + 3), low, to_west)
        edge = LANES - 3 * place
        to_east = jnp.where((lane >= edge - 3) & (lane < edge), high, to_east)
    corner = len(HALO_FLUXES)
    corners = both_fields(even, spot_of(got_c, 0, corner), spot_of(got_b, far_at, corner))
    for place in range(2):
        edges_halo[place] = corners[place]
    lon_even = lax.rem(lax.axis_index("lon"), 2) == 0
    send_a[0] = jnp.where(lon_even, to_east, to_west)
    send_b[0] = jnp.where(lon_even, to_west, to_east)
    for part, columns in ((slice(0, rows), edges), (slice(rows, rows + TILE), edges_halo)):
        send_a[1, part, :] = jnp.where(lon_even, columns[1], columns[0])
        send_b[1, part, :] = jnp.where(lon_even, columns[0], columns[1])


def column_depth(counts, levels):
    scale = 1.0 / (2.0 * levels)
    return counts * scale + counts * (counts - 1.0) * (scale / levels)


def sideways(array, ends):
    rows, width = array.shape
    lane = lane_ids(rows)
    parts = [array[:, at : at + LANES] for at in range(0, width, LANES)]
    right = [roll_lanes(part, -1) for part in parts] + [ends]
    left = [ends] + [roll_lanes(part, 1) for part in parts]
    east = [jnp.where(lane == LANES - 1, b, a) for a, b in zip(right, right[1:])]
    west = [jnp.where(lane == 0, a, b) for a, b in zip(left, left[1:])]
    return jnp.concatenate(east, axis=1), jnp.concatenate(west, axis=1)


def turned(ends, level):
    return pltpu.roll(ends, lax.rem(2 * LANES - 2 * level, LANES), 1)


LEVELS_AT_ONCE = 6
LEVELS_BEFORE = 10


def before_body(ext, light, temp, got_a, got_b, base, laps, halo):
    levels, rows, width = temp.shape
    counts = ext[3]
    own_counts = counts[:rows]
    lane = lane_ids(3 * TILE, width)
    limit_east = jnp.where(lane == width - 1, 0.0, jnp.minimum(counts, roll_lanes(counts, -1)))
    limit_north = jnp.minimum(counts, roll_rows(counts, -1))
    limits = (limit_east, roll_lanes(limit_east, 1), limit_north, roll_rows(limit_north, 1))
    step = math.gcd(levels, LEVELS_BEFORE)
    odd = lax.rem(lax.axis_index("lat"), 2) == 1
    near = near_lanes(width)
    for level in range(levels):
        rows_near = unpack_rows(jnp.logical_not(odd), got_a[level // 4], level)
        rows_far = unpack_rows(odd, got_b[level // 4], level)
        halo[level] = jnp.where(near, rows_near, rows_far)

    def group(at, down_before):
        for inner in range(step):
            level = at * step + inner
            level_f = level.astype(f32)
            own = temp[level]
            whole = jnp.concatenate([own, halo[level]], axis=0)
            east, west = sideways(whole, whole[:, :LANES])
            lap = -4.0 * whole
            for around, limit in zip(
                (east, west, roll_rows(whole, -1), roll_rows(whole, 1)), limits
            ):
                lap = lap + jnp.where(level_f < limit, around, whole)
            laps[level] = lap
            beneath = temp[jnp.minimum(level + 1, levels - 1)]
            down = jnp.where(level_f + 1.0 < own_counts, beneath - own, 0.0)
            absorb = jnp.exp(jnp.full(own.shape, -1.0 / light_decay, f32) * level_f)
            absorb = absorb * (light_gain * (1.0 - math.exp(-1.0 / light_decay)))
            source = absorb * light[1] + jnp.where(level == 0, heat_gain, 0.0) * light[0]
            change = diapycnal_diffusion * (down - down_before) + source
            base[level] = own + jnp.where(level_f < own_counts, change, 0.0)
            down_before = down
        return down_before

    lax.fori_loop(0, levels // step, group, jnp.zeros((rows, width), f32))


def finish_level(level, own, halo_level, base, lap, ends, limits, speeds):
    rows, width = own.shape
    level_f = level.astype(f32)
    lane = lane_ids(3 * TILE)
    side = turned(ends[2], level)
    parts = [lap[:, at : at + LANES] for at in range(0, width, LANES)]
    parts[0] = parts[0] + jnp.where(lane == 0, side, 0.0)
    parts[-1] = parts[-1] + jnp.where(lane == LANES - 1, side, 0.0)
    lap = jnp.concatenate(parts, axis=1)
    whole = jnp.concatenate([own, halo_level], axis=0)
    own_lap = lap[:rows]
    around_temp = sideways(own, turned(ends[0][:rows], level))
    around_temp += (roll_rows(whole, -1)[:rows], roll_rows(whole, 1)[:rows])
    around_lap = sideways(own_lap, turned(ends[1][:rows], level))
    around_lap += (roll_rows(lap, -1)[:rows], roll_rows(lap, 1)[:rows])
    change = jnp.zeros((rows, width), f32)
    for place, limit in enumerate(limits):
        moved = mixing_fourth * (own_lap - around_lap[place])
        moved = moved - speeds[place] * (around_temp[place] + own)
        change = change + jnp.where(level_f < limit, moved, 0.0)
    return base + change


def hot_body(points, hot):
    links, rows, width = points.shape
    blocks = width // LANES
    cells = row_ids(LANES).astype(f32).astype(jnp.bfloat16)
    one, none = jnp.bfloat16(1.0), jnp.bfloat16(0.0)
    for k in range(links):
        for b in range(blocks):
            for row in range(rows):
                line = points[k, row : row + 1, b * LANES : (b + 1) * LANES]
                line = jnp.broadcast_to(line.astype(f32), (2 * TILE, LANES)).astype(jnp.bfloat16)
                line = jnp.concatenate([line] * (LANES // (2 * TILE)), axis=0)
                hot[k * rows + row, :, b * LANES : (b + 1) * LANES] = jnp.transpose(
                    jnp.where(line == cells, one, none)
                )


def subcycle_body(
    levels,
    ext,
    edges_own,
    edges_halo,
    got_a,
    got_b,
    temp,
    halo,
    base,
    laps,
    hot,
    weights,
    tile_hbm,
    out_height,
    out_zonal,
    out_merid,
    limits_out,
    speeds_out,
    ends_out,
    sums_a,
    sums_b,
    sums_mid,
    whole,
    values,
    table,
    tile,
    tile_sem,
):
    tile_copy = pltpu.make_async_copy(tile_hbm, tile, tile_sem)
    tile_copy.start()
    edges = [
        jnp.concatenate([edges_own[place], edges_halo[place]], axis=0) for place in range(2)
    ]
    width = ext.shape[2]
    rows = temp.shape[1]
    lon_even = lax.rem(lax.axis_index("lon"), 2) == 0
    even = lax.rem(lax.axis_index("lat"), 2) == 0
    lane = lane_ids(3 * TILE)
    from_east = [jnp.where(lon_even, got_a[place], got_b[place]) for place in range(2)]
    from_west = [jnp.where(lon_even, got_b[place], got_a[place]) for place in range(2)]
    planes = []
    for place in range(ext.shape[0]):
        third = jnp.where(
            lane < 3,
            roll_lanes(from_east[0], -3 * place),
            jnp.where(lane >= LANES - 3, roll_lanes(from_west[0], 3 * place), 0.0),
        )
        planes.append(jnp.concatenate([ext[place], third], axis=1))
    height, zonal, merid, counts, wind_east, wind_north, fresh = planes

    def east_of(array):
        return roll_lanes(array, -1)

    def west_of(array):
        return roll_lanes(array, 1)

    def north_of(array):
        return roll_rows(array, -1)

    def south_of(array):
        return roll_rows(array, 1)

    depth = column_depth(counts, levels)
    wet = (counts > 0.5).astype(f32)
    east_wet = wet * east_of(wet)
    north_wet = wet * north_of(wet)
    east_depth = jnp.minimum(depth, east_of(depth))
    north_depth = jnp.minimum(depth, north_of(depth))
    east_pull = grav_step * east_depth
    north_pull = grav_step * north_depth
    wind_east = wind_step * wind_east
    wind_north = wind_step * wind_north
    fresh = fresh_step * fresh
    for _ in range(SUBS):
        zonal = east_wet * (zonal - east_pull * (east_of(height) - height) + wind_east)
        merid = north_wet * (merid - north_pull * (north_of(height) - height) + wind_north)
        spread = zonal - west_of(zonal) + merid - south_of(merid)
        height = height + wet * (fresh - height_step * spread)
    out_height[...] = height[:rows, :width]
    out_zonal[...] = zonal[:rows, :width]
    out_merid[...] = merid[:rows, :width]

    limit_east = jnp.minimum(counts, east_of(counts))
    limit_north = jnp.minimum(counts, north_of(counts))
    limit_west, limit_south = west_of(limit_east), south_of(limit_north)
    limits = [
        limit[:rows, :width] for limit in (limit_east, limit_west, limit_north, limit_south)
    ]
    speed_east = 0.5 * advect_coef * zonal / jnp.maximum(east_depth, depth_floor)
    speed_north = 0.5 * advect_coef * merid / jnp.maximum(north_depth, depth_floor)
    speeds = [
        speed[:rows, :width]
        for speed in (speed_east, -west_of(speed_east), speed_north, -south_of(speed_north))
    ]
    for place in range(4):
        limits_out[place] = limits[place]
        speeds_out[place] = speeds[place]

    lane_level = (lane // 2).astype(f32)
    odd_lane = (lane & 1) == 1
    far_east, far_west = from_east[1], from_west[1]

    def column(limit, at):
        return jnp.broadcast_to(limit[:, at : at + 1], (3 * TILE, LANES))

    def edge_lap(center, toward_east, toward_west, at, at_west):
        total = -4.0 * center
        for around, limit in (
            (toward_east, column(limit_east, at)),
            (toward_west, column(limit_east, at_west)),
            (north_of(center), column(limit_north, at)),
            (south_of(center), column(limit_south, at)),
        ):
            total = total + jnp.where(lane_level < limit, around, center)
        return total

    total_lanes = width + LANES
    lap_west = edge_lap(
        far_west,
        roll_lanes(edges[0], 1),
        roll_lanes(far_west, 1),
        total_lanes - 1,
        total_lanes - 2,
    )
    lap_east = edge_lap(
        far_east, roll_lanes(far_east, -1), roll_lanes(edges[1], -1), width, width - 1
    )
    side_west = far_west - roll_lanes(edges[0], 1)
    side_west = jnp.where(lane_level < column(limit_east, total_lanes - 1), side_west, 0.0)
    side_east = far_east - roll_lanes(edges[1], -1)
    side_east = jnp.where(lane_level < column(limit_east, width - 1), side_east, 0.0)
    ends = []
    for west, east in ((far_west, far_east), (lap_west, lap_east), (side_west, side_east)):
        ends.append(roll_lanes(jnp.where(odd_lane, west, east), -1))
    for place in range(3):
        ends_out[place] = ends[place]

    zero = jnp.zeros((), i32)
    top = finish_level(zero, temp[0], halo[0], base[0], laps[0], ends, limits, speeds)
    own_wet = wet[:rows, :width]
    thick = jnp.maximum(depth[:rows, :width], depth_floor)
    surface = [
        top * own_wet,
        height[:rows, :width] * own_wet,
        zonal[:rows, :width] / thick * own_wet,
        merid[:rows, :width] / thick * own_wet,
        own_wet,
    ]
    nsums = len(surface)
    values[...] = jnp.zeros(values.shape, f32)
    for place in range(nsums):
        values[:, place, :] = surface[place]
    table[...] = jnp.zeros(table.shape, f32)
    links = weights.shape[0]
    blocks = width // LANES
    tile_copy.wait()

    for row in range(rows):
        held = values[row]
        for k in range(links):
            shares = held * weights[k, row : row + 1, :]
            upper = shares.astype(jnp.bfloat16)
            lower = (shares - upper.astype(f32)).astype(jnp.bfloat16)
            both = jnp.concatenate([upper, lower], axis=0)
            stacked = jnp.concatenate(
                [both[:, b * LANES : (b + 1) * LANES] for b in range(blocks)], axis=0
            )
            found = jnp.dot(stacked, hot[k * rows + row], preferred_element_type=f32)
            for b in range(blocks):
                target = tile[k, b, row]
                mine = found[b * 2 * TILE : (b + 1) * 2 * TILE, b * LANES : (b + 1) * LANES]
                table[target] = table[target] + mine
    for place in range(nsums):
        total = table[:, place, :] + table[:, TILE + place, :]
        south, middle, north = total[:TILE], total[TILE : 2 * TILE], total[2 * TILE :]
        sums_mid[place] = middle
        sums_a[place] = jnp.where(even, north, south)
        sums_b[place] = jnp.where(even, south, north)

    run_levels(
        0,
        early_groups(levels),
        temp,
        halo,
        base,
        laps,
        limits_out,
        speeds_out,
        ends_out,
        whole,
    )


def level_step(levels):
    return math.gcd(levels, LEVELS_AT_ONCE)


def early_groups(levels):
    groups = levels // level_step(levels)
    place = lax.axis_index("lat")
    inner = jnp.where(lax.rem(place, 2) == 1, groups // 5, 0)
    inner = jnp.where(place == 2, groups // 10, inner)
    return jnp.where(place == 0, groups * 7 // 10, jnp.where(place == 1, groups // 2, inner))


LAST_GROUPS = 2


def run_levels(start, stop, temp, halo, base, laps, limits, speeds, ends, out, done=None):
    step = level_step(temp.shape[0])

    def group(at, carry):
        for inner in range(step):
            level = jnp.int32(at * step + inner)
            out[level] = finish_level(
                level,
                temp[level],
                halo[level],
                base[level],
                laps[level],
                [ends[place] for place in range(3)],
                [limits[place] for place in range(4)],
                [speeds[place] for place in range(4)],
            )
        if done is not None:
            done(at)
        return carry

    lax.fori_loop(start, stop, group, 0)


def tracer_body(
    temp,
    halo,
    base,
    laps,
    limits,
    speeds,
    ends,
    draft,
    height,
    zonal,
    merid,
    out_height,
    out_zonal,
    out_merid,
    out,
    whole,
    sems,
    level_sems,
):
    levels = temp.shape[0]
    step = level_step(levels)
    groups = levels // step
    pairs = [(height, out_height), (zonal, out_zonal), (merid, out_merid)]
    copies = [
        pltpu.make_async_copy(source, target, sems.at[place])
        for place, (source, target) in enumerate(pairs)
    ]
    for copy in copies:
        copy.start()

    def level_copy(at, source=whole):
        part = pl.ds(at * step, step)
        return pltpu.make_async_copy(source.at[part], out.at[part], level_sems.at[at])

    early = early_groups(levels)

    def start(at, carry):
        level_copy(at, draft).start()
        return carry

    lax.fori_loop(0, early, start, 0)
    inside = max(groups - LAST_GROUPS, 0)
    refs = (temp, halo, base, laps, limits, speeds, ends, whole)
    run_levels(early, inside, *refs, lambda at: level_copy(at).start())
    run_levels(inside, groups, *refs)
    for at in range(inside):
        level_copy(at).wait()
    for copy in copies:
        copy.wait()


def merge_body(mid, got_a, got_b, flags, whole, draft, out, out_temp, surface, sems):
    levels = whole.shape[0]
    step = level_step(levels)
    first = step * max(levels // step - LAST_GROUPS, 0)
    part = pl.ds(first, levels - first)
    rest = pltpu.make_async_copy(whole.at[part], out_temp.at[part], sems.at[0])
    rest.start()
    open_sea = (1 - flags[...]).astype(f32)
    nsurf = out.shape[0]
    area = mid[nsurf] + got_a[nsurf] + got_b[nsurf]
    scale = open_sea / jnp.maximum(area, area_floor)
    for place in range(nsurf):
        surface[place] = (mid[place] + got_a[place] + got_b[place]) * scale
    copy = pltpu.make_async_copy(surface, out, sems.at[1])
    copy.start()
    copy.wait()
    rest.wait()


def shards(
    free_elevation,
    zonal_volume_carriage,
    meridional_volume_carriage,
    thermal_field,
    flooded_strata_number,
    aerial_exchanges,
    aerial_terrain_flags,
    donor_tile_number,
    donor_point_number,
    pairing_coefficients,
):
    levels, rows, width = thermal_field.shape
    nflux, band_rows, lanes = aerial_exchanges.shape
    links, _, blocks = donor_tile_number.shape
    assert rows == 2 * TILE and band_rows == TILE and lanes == LANES
    assert 2 * levels <= LANES and lax.axis_size("lon") % 2 == 0
    nsums = 5
    fields = 4 + 2 * links
    flux_at = fields // 2
    flux_tiles = (nflux + 2) // 2
    temp_at = flux_at + flux_tiles
    groups = pl.cdiv(levels, 4)
    tile_lines = jnp.swapaxes(donor_tile_number, 1, 2)
    temp = thermal_field
    edge_a, own, state, points, weights, flags, tile = call(
        load_body,
        [
            shape(temp_at, TILE, width),
            shape(nflux, TILE, LANES),
            shape(4, rows, width),
            shape(links, rows, width, dtype=i32),
            shape(links, rows, width),
            shape(band_rows, lanes, dtype=i32),
            shape(links, blocks, rows, dtype=i32),
        ],
        (
            free_elevation,
            zonal_volume_carriage,
            meridional_volume_carriage,
            flooded_strata_number,
            donor_point_number,
            tile_lines,
            pairing_coefficients,
            aerial_exchanges,
            aerial_terrain_flags,
        ),
        "load",
        1.6,
        scratch=[
            pltpu.VMEM((rows, width), i32),
            pltpu.VMEM((nflux, band_rows, lanes), f32),
            pltpu.SemaphoreType.DMA((9,)),
        ],
        hbm=range(9),
    )
    got_a = swap(edge_a, "lat", 0, False)
    far_tiles = (len(HALO_FLUXES) + 1) // 2
    edge_tiles = temp_at + far_tiles
    draft_b, edges, numbers = call(
        pack_second_body,
        [
            shape(edge_tiles, TILE, width),
            shape(2, rows, LANES),
            shape(2, TILE, LANES),
        ],
        (own, state, points, weights, tile, temp),
        "pack_b",
        0.3,
    )
    (edge_b,) = call(
        functools.partial(pack_flux_body, flux_at),
        [shape(edge_tiles, TILE, width)],
        (draft_b, got_a, edges),
        "pack_flux",
        0.0,
    )
    got_b = swap(edge_b, "lat", 1, False)
    (temp_b,) = call(
        functools.partial(pack_temp_body, 1),
        [shape(groups, TILE, width)],
        (temp, edge_b),
        "pack_temp_b",
        LATE,
    )
    got_temp_b = swap(temp_b, "lat", 1, False)
    (temp_a,) = call(
        functools.partial(pack_temp_body, 0),
        [shape(groups, TILE, width)],
        (temp, temp_b),
        "pack_temp_a",
        0.0,
    )
    got_temp_a = swap(temp_a, "lat", 0, False)
    (edge_c,) = call(
        functools.partial(pack_third_body, flux_at),
        [shape((len(HALO_FLUXES) + 3) // 2, TILE, width)],
        (got_b, edges, numbers),
        "pack_c",
        LATE,
    )
    got_c = swap(edge_c, "lat", 0, False)
    draft_ext, light = call(
        functools.partial(forcing_body, flux_at),
        [shape(7, 3 * TILE, width), shape(2, rows, width)],
        (got_a, got_b, own, numbers, state, points, weights),
        "forcing",
        0.4,
    )
    ext, send_a, send_b, edges_halo = call(
        functools.partial(forcing_halo_body, flux_at),
        [
            shape(7, 3 * TILE, width),
            shape(2, 3 * TILE, LANES),
            shape(2, 3 * TILE, LANES),
            shape(2, TILE, LANES),
        ],
        (draft_ext, got_a, got_b, got_c, own, edges),
        "forcing_halo",
        0.3,
    )
    lon_b = swap(send_b, "lon", 1, True)
    (send_a,) = call(
        pass_body, [shape(2, 3 * TILE, LANES)], (send_a, send_b), "pass_lon", LATE
    )
    lon_a = swap(send_a, "lon", 0, True)
    (hot,) = call(
        hot_body,
        [shape(links * rows, LANES, blocks * LANES, dtype=jnp.bfloat16)],
        (points,),
        "hot",
        0.0,
    )
    base, laps, halo = call(
        before_body,
        [
            shape(levels, rows, width),
            shape(levels, 3 * TILE, width),
            shape(levels, TILE, width),
        ],
        (ext, light, temp, got_temp_a, got_temp_b),
        "before",
        0.0,
    )
    (
        advanced_elevation,
        transport_x_next,
        transport_y_next,
        limits,
        speeds,
        ends,
        sums_a,
        sums_b,
        sums_mid,
        draft,
    ) = call(
        functools.partial(subcycle_body, levels),
        [shape(rows, width)] * 3
        + [shape(4, rows, width), shape(4, rows, width), shape(3, 3 * TILE, LANES)]
        + [shape(nsums, TILE, LANES)] * 3
        + [shape(levels, rows, width)],
        (
            ext,
            edges,
            edges_halo,
            lon_a,
            lon_b,
            temp,
            halo,
            base,
            laps,
            hot,
            weights,
            tile_lines,
        ),
        "subcycles",
        2.6,
        scratch=[
            pltpu.VMEM((rows, TILE, width), f32),
            pltpu.VMEM((3 * TILE, 2 * TILE, LANES), f32),
            pltpu.SMEM((links, blocks, rows), i32),
            pltpu.SemaphoreType.DMA(()),
        ],
        hbm=(11,),
    )
    back_b = swap(sums_b, "lat", 1, False)
    (sums_a,) = call(
        pass_body, [shape(nsums, TILE, LANES)], (sums_a, sums_b), "pass_sums", LATE
    )
    back_a = swap(sums_a, "lat", 0, False)
    advanced_elevation, transport_x_next, transport_y_next, draft_field, draft = call(
        tracer_body,
        [
            pltpu.HBM((rows, width), f32),
            pltpu.HBM((rows, width), f32),
            pltpu.HBM((rows, width), f32),
            pltpu.HBM((levels, rows, width), f32),
            shape(levels, rows, width),
        ],
        (
            temp,
            halo,
            base,
            laps,
            limits,
            speeds,
            ends,
            draft,
            advanced_elevation,
            transport_x_next,
            transport_y_next,
        ),
        "tracer",
        2.5,
        scratch=[
            pltpu.SemaphoreType.DMA((3,)),
            pltpu.SemaphoreType.DMA((levels // level_step(levels),)),
        ],
    )
    marine_skin_condition, advanced_thermal_field = call(
        merge_body,
        [
            pltpu.HBM((nsums - 1, band_rows, lanes), f32),
            pltpu.HBM((levels, rows, width), f32),
        ],
        (sums_mid, back_a, back_b, flags, draft, draft_field),
        "merge",
        0.1,
        aliases={5: 1},
        hbm=(5,),
        scratch=[
            pltpu.VMEM((nsums - 1, band_rows, lanes), f32),
            pltpu.SemaphoreType.DMA((2,)),
        ],
    )
    return (
        advanced_elevation,
        transport_x_next,
        transport_y_next,
        advanced_thermal_field,
        marine_skin_condition,
    )


def solution(mesh):
    flat = P("lat", "lon")
    deep = P(None, "lat", "lon")
    return jax.shard_map(
        shards,
        mesh=mesh,
        in_specs=(flat, flat, flat, deep, flat, deep, flat, deep, deep, deep),
        out_specs=(flat, flat, flat, deep, deep),
        check_vma=False,
    )
```
